256 devices in a mesh: dp: 4 (over y_hi, core), dap: 64 (over z, x, y_lo).
Axes of the slice: x: 4, y: 4 (y_hi: 2, y_lo: 2; y = y_hi * 2 + y_lo), z: 8, core: 2. Of those that a mesh axis runs over, the one named last changes fastest.
Arguments:
- pair_input: bfloat16 [4, 128, 128, 128], P('dp', 'dap'), may hold values from -6 to 6
- cotangent: bfloat16 [4, 128, 128, 128], P('dp', 'dap'), may hold values from -6 to 6
- residue_mask: int32 [4, 128], P('dp'), may hold values from 0 to 1, as said below
- gain_start: float32 [128], replicated, may hold values from 0.5 to 1.5
- proj_start: float32 [128, 512], replicated, may hold values from -0.5 to 0.5
- bias_start: float32 [128, 4], replicated, may hold values from -0.5 to 0.5
- output_start: float32 [128, 128], replicated, may hold values from -0.5 to 0.5
- gain_end: float32 [128], replicated, may hold values from 0.5 to 1.5
- proj_end: float32 [128, 512], replicated, may hold values from -0.5 to 0.5
- bias_end: float32 [128, 4], replicated, may hold values from -0.5 to 0.5
- output_end: float32 [128, 128], replicated, may hold values from -0.5 to 0.5
- gain_transition: float32 [128], replicated, may hold values from 0.5 to 1.5
- transition_up: float32 [128, 512], replicated, may hold values from -0.5 to 0.5
- transition_down: float32 [512, 128], replicated, may hold values from -0.25 to 0.25
Outputs:
- grad_pair: bfloat16 [4, 128, 128, 128], P('dp', 'dap')
- grad_gain_start: float32 [128], replicated
- grad_proj_start: float32 [128, 512], replicated
- grad_bias_start: float32 [128, 4], replicated
- grad_output_start: float32 [128, 128], replicated
- grad_gain_end: float32 [128], replicated
- grad_proj_end: float32 [128, 512], replicated
- grad_bias_end: float32 [128, 4], replicated
- grad_output_end: float32 [128, 128], replicated
- grad_gain_transition: float32 [128], replicated
- grad_transition_up: float32 [128, 512], replicated
- grad_transition_down: float32 [512, 128], replicated
The draws below stay inside these ranges and needn't reach their ends.
Inputs may be any that keep to these rules, and one draw needn't show every extreme that they name: `residue_mask`: row b is 1 on the first L residues of complex b and 0 after them, with L at least half of 128 and less than 128.
All inputs are finite; a program needn't handle non-finite values.
Results may differ from the reference program's by a relative error of at most 0.03.
Values may be sent and summed in bfloat16 or wider, within the bound.
No kernel may reach another device: no remote copies, remote signals or barrier semaphores. Data moves between devices by JAX's collectives and lax.ppermute only.
A program may use at most 64 MiB of HBM per device.

```python
import jax
import jax.numpy as jnp
from jax import lax

C = 128
HEADS = 4
FF = 512
R_DEV = 2
N = 128
B = 4


def draw_residue_mask(key, part):
    key = jax.random.fold_in(key, 7)
    lengths = jax.random.randint(key, (B, 1), N // 2, N)
    positions = jnp.arange(N, dtype=jnp.int32)[None, :]
    return (positions < lengths).astype(jnp.int32)


def levels(key, extent, pieces, low, largest):
    factor_of = 1.0
    for dim, blocks in pieces:
        heights = jax.random.uniform(jax.random.fold_in(jax.random.fold_in(key, 6), dim), (blocks,), jnp.float32, low / len(pieces), largest / len(pieces))
        factor_of = factor_of * jnp.repeat(jnp.exp(heights), extent[dim] // blocks).reshape((-1,) + (1,) * (len(extent) - 1 - dim))
    return factor_of


def centred(stream_key, extent, scale, limit, split=(), held_as=jnp.bfloat16):
    level = levels(stream_key, extent, split, -0.22, 0.18) if split else 1.0
    drawn = jax.random.normal(stream_key, extent, jnp.float32) * scale * level
    return jnp.minimum(jnp.maximum(drawn, -limit), limit).astype(held_as)


def setup_inputs(seed: int = 0) -> dict:
    seeds = jax.random.split(jax.random.key(seed), 15)
    pair_input = centred(seeds[0], (B, N, N, C), 1.0, 6.0, ((0, 4), (1, 64)))
    cotangent = centred(seeds[1], (B, N, N, C), 1.0, 6.0, ((0, 4), (1, 64)))
    residue_mask = draw_residue_mask(jax.random.fold_in(seeds[14], 71), 0)
    gain_start = jnp.clip(1.0 + 0.1 * jax.random.normal(seeds[3], (C,), jnp.float32), 0.5, 1.5)
    proj_start = centred(seeds[4], (C, 4 * C), C ** -0.5, 0.5, (), jnp.float32)
    bias_start = centred(seeds[5], (C, HEADS), C ** -0.5, 0.5, (), jnp.float32)
    output_start = centred(seeds[6], (C, C), C ** -0.5, 0.5, (), jnp.float32)
    gain_end = jnp.clip(1.0 + 0.1 * jax.random.normal(seeds[7], (C,), jnp.float32), 0.5, 1.5)
    proj_end = centred(seeds[8], (C, 4 * C), C ** -0.5, 0.5, (), jnp.float32)
    bias_end = centred(seeds[9], (C, HEADS), C ** -0.5, 0.5, (), jnp.float32)
    output_end = centred(seeds[10], (C, C), C ** -0.5, 0.5, (), jnp.float32)
    gain_transition = jnp.clip(1.0 + 0.1 * jax.random.normal(seeds[11], (C,), jnp.float32), 0.5, 1.5)
    transition_up = centred(seeds[12], (C, FF), C ** -0.5, 0.5, (), jnp.float32)
    transition_down = centred(seeds[13], (FF, C), FF ** -0.5, 0.25, (), jnp.float32)
    return {"pair_input": pair_input, "cotangent": cotangent, "residue_mask": residue_mask, "gain_start": gain_start, "proj_start": proj_start, "bias_start": bias_start, "output_start": output_start, "gain_end": gain_end, "proj_end": proj_end, "bias_end": bias_end, "output_end": output_end, "gain_transition": gain_transition, "transition_up": transition_up, "transition_down": transition_down}


EPS = 1e-05
FULL_PRECISION = lax.Precision.HIGHEST

def normalize(pair_rows, scaling):
    widened = pair_rows.astype(jnp.float32)
    centre = widened - lax.optimization_barrier(jnp.mean(widened, -1, keepdims=True))
    spread = lax.optimization_barrier(jnp.mean(centre * centre, -1, keepdims=True))
    return (centre * lax.rsqrt(spread + EPS) * scaling).astype(jnp.bfloat16)

def plane_rows(pair_rows, scaling, w_bias):
    normed = normalize(pair_rows, scaling).astype(jnp.float32)
    return jnp.einsum('rkc,ch->hrk', normed, w_bias, precision=FULL_PRECISION).astype(jnp.bfloat16)

def attend(pair_rows, bias_plane, kept_keys, scaling, w_proj, w_out):
    row_count, col_count, channels = pair_rows.shape
    head_size = channels // HEADS
    head_shape = (row_count, col_count, HEADS, head_size)
    normed = normalize(pair_rows, scaling).reshape(row_count * col_count, channels)
    projected = jnp.dot(normed, w_proj.astype(jnp.bfloat16), preferred_element_type=jnp.float32)
    queries = (projected[:, :channels] * head_size ** (-0.5)).astype(jnp.bfloat16).reshape(head_shape)
    key_vectors = projected[:, channels:2 * channels].astype(jnp.bfloat16).reshape(head_shape)
    values = projected[:, 2 * channels:3 * channels].astype(jnp.bfloat16).reshape(head_shape)
    gating = jax.nn.sigmoid(projected[:, 3 * channels:])
    scores = jnp.einsum('rjhd,rkhd->rhjk', queries.astype(jnp.float32), key_vectors.astype(jnp.float32), precision=FULL_PRECISION) + bias_plane
    weights = jnp.exp(scores) * kept_keys
    attention = (weights / lax.optimization_barrier(jnp.sum(weights, -1, keepdims=True))).astype(jnp.bfloat16)
    mixture = jnp.einsum('rhjk,rkhd->rjhd', attention.astype(jnp.float32), values.astype(jnp.float32), precision=FULL_PRECISION)
    gated_mix = (gating * mixture.reshape(row_count * col_count, channels)).astype(jnp.bfloat16)
    update = jnp.dot(gated_mix, w_out.astype(jnp.bfloat16), preferred_element_type=jnp.float32)
    return update.reshape(row_count, col_count, channels)

def transition(pair_rows, scaling, w_up, w_down):
    row_count, col_count, channels = pair_rows.shape
    normed = normalize(pair_rows, scaling).reshape(row_count * col_count, channels)
    widened = jnp.dot(normed, w_up.astype(jnp.bfloat16), preferred_element_type=jnp.float32)
    hidden = jax.nn.gelu(widened, approximate=False).astype(jnp.bfloat16)
    update = jnp.dot(hidden, w_down.astype(jnp.bfloat16), preferred_element_type=jnp.float32)
    return update.reshape(row_count, col_count, channels)

def split_rows(pair_full):
    return pair_full.reshape((N // R_DEV, R_DEV) + pair_full.shape[1:])

def triangle(pair_full, kept_keys, scaling, w_proj, w_bias, w_out):
    bias_plane = plane_rows(pair_full, scaling, w_bias).astype(jnp.float32)

    def per_block(pair_block):
        return attend(pair_block, bias_plane, kept_keys, scaling, w_proj, w_out)
    update = lax.map(jax.checkpoint(per_block), split_rows(pair_full)).reshape(pair_full.shape)
    return (pair_full.astype(jnp.float32) + update).astype(jnp.bfloat16)

def forward(pair_full, kept_keys, weight_set):
    gain_start, proj_start, bias_start, output_start, gain_end, proj_end, bias_end, output_end, gain_transition, transition_up, transition_down = weight_set
    first_pair = triangle(pair_full, kept_keys, gain_start, proj_start, bias_start, output_start)
    second = triangle(jnp.transpose(first_pair, (1, 0, 2)), kept_keys, gain_end, proj_end, bias_end, output_end)

    def per_block(pair_block):
        return transition(pair_block, gain_transition, transition_up, transition_down)
    update = lax.map(jax.checkpoint(per_block), split_rows(second)).reshape(second.shape)
    final_pair = second.astype(jnp.float32) + update
    return jnp.transpose(final_pair, (1, 0, 2))

def reference(pair_input, cotangent, residue_mask, gain_start, proj_start, bias_start, output_start, gain_end, proj_end, bias_end, output_end, gain_transition, transition_up, transition_down):
    weight_set = (gain_start, proj_start, bias_start, output_start, gain_end, proj_end, bias_end, output_end, gain_transition, transition_up, transition_down)

    def one_complex(members):
        pair_one, cotangent_one, mask_one = members
        kept_keys = mask_one.astype(jnp.float32)

        def local_forward(pair_full, weights_in):
            return forward(pair_full, kept_keys, weights_in)
        result, pullback = jax.vjp(local_forward, pair_one, weight_set)
        return pullback(cotangent_one.astype(jnp.float32))
    grad_pair, grad_weights = lax.map(one_complex, (pair_input, cotangent, residue_mask))
    factor = 1.0 / (B * N)
    summed = [lax.optimization_barrier(jnp.sum(gradient, 0)) * factor for gradient in grad_weights]
    return (grad_pair, summed[0], summed[1], summed[2], summed[3], summed[4], summed[5], summed[6], summed[7], summed[8], summed[9], summed[10])
```

```python
import functools

import jax
import jax.numpy as jnp
from jax import lax
from jax.experimental import pallas as pl
from jax.experimental.pallas import tpu as pltpu
from jax.sharding import PartitionSpec as P

HEADS = 4
EPS = 1e-05
F32 = jnp.float32
BF16 = jnp.bfloat16
C = 128
FULL = lax.Precision.HIGHEST
VMEM_LIMIT = 48 * 1024 * 1024


def dot(a, b, contract=((1,), (0,)), precision=None):
    return lax.dot_general(a, b, (contract, ((), ())), precision=precision, preferred_element_type=F32)


NN = ((1,), (0,))
NT = ((1,), (1,))
TN = ((0,), (0,))


def ln_stats(x):
    centre = x - jnp.mean(x, -1, keepdims=True)
    spread = jnp.mean(centre * centre, -1, keepdims=True)
    rstd = lax.rsqrt(spread + EPS)
    return centre * rstd, rstd


def ln_back(dn, xhat, rstd, gain):
    t = dn * gain
    m1 = jnp.mean(t, -1, keepdims=True)
    m2 = jnp.mean(t * xhat, -1, keepdims=True)
    dx = rstd * (t - m1 - xhat * m2)
    return dx.astype(BF16).astype(F32), jnp.sum(dn * xhat, 0, keepdims=True)


def head_masks(dtype):
    lane = lax.broadcasted_iota(jnp.int32, (1, C), 1)
    size = C // HEADS
    return [((lane >= h * size) & (lane < (h + 1) * size)).astype(dtype) for h in range(HEADS)]


def stack_heads(a, masks):
    return jnp.concatenate([a * m for m in masks], 0)


def unstack_heads(a, masks):
    n = a.shape[0] // HEADS
    total = a[:n] * masks[0]
    for h in range(1, HEADS):
        total = total + a[h * n : (h + 1) * n] * masks[h]
    return total


def project(n, w_ref):
    proj = dot(n, w_ref[...].astype(BF16))
    scale = (C // HEADS) ** (-0.5)
    q = (proj[:, :C] * scale).astype(BF16)
    k = proj[:, C : 2 * C].astype(BF16)
    v = proj[:, 2 * C : 3 * C].astype(BF16)
    return q, k, v, jax.nn.sigmoid(proj[:, 3 * C :])


def plane_of(n, wt_ref):
    return dot(wt_ref[...], n.astype(F32), NT, FULL)


def rows_of(ref, start, count, stride):
    return ref[pl.ds(start, count, stride=stride), :]


def plane_local_kernel(x_ref, g_ref, wt_ref, out_ref, small):
    n_dst, rows, _ = out_ref.shape
    xhat, _ = ln_stats(x_ref[...].astype(F32))
    n = (xhat * g_ref[...]).astype(BF16)
    plane = plane_of(n, wt_ref)
    small[0:HEADS, :] = plane[:, :C]
    small[HEADS : 2 * HEADS, :] = plane[:, C:]
    out_ref[...] = jnp.broadcast_to(small[...].astype(BF16)[None], (n_dst, rows, C))


def start_forward_kernel(
    recv_ref, x_ref, cot_ref, mask_ref, g_ref, w_ref, wo_ref, ge_ref, wte_ref,
    send_ref, qkv_ref, gating_ref, mix_ref, prob_ref, first_ref,
    fscr, plane, sscr, small,
):
    n_dst = recv_ref.shape[0]
    N = 2 * n_dst
    rows = send_ref.shape[1]
    fscr[...] = recv_ref[...].astype(F32).reshape(n_dst * 8, C)
    for r in range(2):
        for h in range(HEADS):
            plane[pl.ds(h * N + r, n_dst, stride=2), :] = rows_of(fscr, r * 4 + h, n_dst, 8)
    masks = head_masks(BF16)
    kept = mask_ref[...].astype(F32)
    x = x_ref[...].astype(F32)
    xhat, _ = ln_stats(x)
    n = (xhat * g_ref[...]).astype(BF16)
    q, k, v, gating = project(n, w_ref)
    qkv_ref[:, :C] = q
    qkv_ref[:, C : 2 * C] = k
    qkv_ref[:, 2 * C :] = v
    gating_ref[...] = gating
    mixes = []
    for r in range(2):
        part = slice(r * N, (r + 1) * N)
        s = dot(q[part], stack_heads(k[part], masks), NT)
        probs = []
        for h in range(HEADS):
            w = jnp.exp(s[:, h * N : (h + 1) * N] + plane[h * N : (h + 1) * N, :]) * kept
            probs.append(w / jnp.sum(w, -1, keepdims=True))
        prob = jnp.concatenate(probs, 1)
        prob_ref[part, :] = prob
        mixes.append(dot(prob.astype(BF16), stack_heads(v[part], masks)))
    mix = jnp.concatenate(mixes, 0)
    mix_ref[...] = mix
    update = dot((gating * mix).astype(BF16), wo_ref[...].astype(BF16))
    first = (x + update).astype(BF16)
    first_ref[...] = first
    first = first.astype(F32)
    xhat_e, _ = ln_stats(first)
    plane_e = plane_of((xhat_e * ge_ref[...]).astype(BF16), wte_ref)
    small[0:HEADS, :] = plane_e[:, :N]
    small[HEADS : 2 * HEADS, :] = plane_e[:, N:]
    fscr[0 : 2 * N, :] = first
    for r in range(2):
        for a in range(2):
            sscr[pl.ds(r * 2 + a, n_dst, stride=rows), :] = rows_of(fscr, r * N + a, n_dst, 2)
    fscr[0 : 2 * N, :] = cot_ref[...].astype(F32)
    for r in range(2):
        for a in range(2):
            sscr[pl.ds(4 + r * 2 + a, n_dst, stride=rows), :] = rows_of(fscr, r * N + a, n_dst, 2)
    for i in range(8):
        sscr[pl.ds(8 + i, n_dst, stride=rows), :] = jnp.broadcast_to(small[i : i + 1, :], (n_dst, C))
    send_ref[...] = sscr[...].reshape(n_dst, rows, C).astype(BF16)


def put_wide(scr, src, value, row, n_dst, rows):
    for t in range(4):
        src[...] = value[:, t * C : (t + 1) * C]
        for i in range(2):
            scr[pl.ds(row + i * 4 + t, n_dst, stride=rows), :] = rows_of(src, i, n_dst, 2)


def put_narrow(scr, src, row, n_dst, rows, each):
    for i in range(each):
        scr[pl.ds(row + i, n_dst, stride=rows), :] = rows_of(src, i, n_dst, each)


def put_small(scr, row, values, n_dst, rows):
    scr[pl.ds(row, n_dst, stride=rows), :] = jnp.zeros((n_dst, C), F32)
    for e, value in enumerate(values):
        scr[e * rows + row : e * rows + row + 1, :] = value


def end_kernel(
    recv_ref, mask_ref, g_ref, w_ref, wo_ref, gt_ref, wu_ref, wd_ref,
    send_ref,
    fscr, zscr, cscr, plane, down, narrow, sscr,
):
    n_dst, in_rows, _ = recv_ref.shape
    N = 2 * n_dst
    rows = send_ref.shape[1]
    fscr[...] = recv_ref[...].astype(F32).reshape(n_dst * in_rows, C)
    for r in range(2):
        for a in range(2):
            zscr[pl.ds(a * N + r, n_dst, stride=2), :] = rows_of(fscr, r * 2 + a, n_dst, in_rows)
            cscr[pl.ds(a * N + r, n_dst, stride=2), :] = rows_of(fscr, 4 + r * 2 + a, n_dst, in_rows)
        for h in range(HEADS):
            plane[pl.ds(h * N + r, n_dst, stride=2), :] = rows_of(fscr, 8 + r * 4 + h, n_dst, in_rows)
    masks = head_masks(BF16)
    masks_f = head_masks(F32)
    length = jnp.sum(mask_ref[...].astype(F32), -1, keepdims=True)
    kept = (lax.broadcasted_iota(jnp.int32, (N, 1), 0).astype(F32) < length).astype(F32)
    x = zscr[...]
    cot = cscr[...]
    xhat, rstd = ln_stats(x)
    n = (xhat * g_ref[...]).astype(BF16)
    q, k, v, gating = project(n, w_ref)
    saved = []
    mixes = []
    for a in range(2):
        part = slice(a * N, (a + 1) * N)
        ks = stack_heads(k[part], masks)
        vs = stack_heads(v[part], masks)
        s = dot(ks, q[part], NT) + plane[...]
        probs = []
        for h in range(HEADS):
            w = jnp.exp(s[h * N : (h + 1) * N]) * kept
            probs.append(w / jnp.sum(w, 0, keepdims=True))
        prob = jnp.concatenate(probs, 0)
        prob_b = prob.astype(BF16)
        mixes.append(dot(prob_b, vs, TN))
        saved.append((ks, vs, prob, prob_b))
    mix = jnp.concatenate(mixes, 0)
    gated = (gating * mix).astype(BF16)
    wo = wo_ref[...].astype(BF16)
    second = (x + dot(gated, wo)).astype(BF16).astype(F32)
    xhat2, rstd2 = ln_stats(second)
    n2 = (xhat2 * gt_ref[...]).astype(BF16)
    wu = wu_ref[...].astype(BF16)
    wd = wd_ref[...].astype(BF16)
    cot_b = cot.astype(BF16)
    up = dot(n2, wu)
    cdf = 0.5 * (1.0 + lax.erf(up * (0.5**0.5)))
    hidden = (up * cdf).astype(BF16)
    dhidden = dot(cot_b, wd, NT).astype(BF16).astype(F32)
    slope = cdf + up * (jnp.exp(-0.5 * up * up) * 0.3989422804014327)
    dup = (dhidden * slope).astype(BF16)
    down[...] = dot(hidden, cot_b, TN)
    put_narrow(sscr, down, 28, n_dst, rows, 8)
    put_wide(sscr, narrow, dot(n2, dup, TN), 20, n_dst, rows)
    dn2 = dot(dup, wu, NT).astype(BF16).astype(F32)
    dx2, dgain_t = ln_back(dn2, xhat2, rstd2, gt_ref[...])
    dsecond = (cot + dx2).astype(BF16)
    narrow[...] = dot(gated, dsecond, TN)
    put_narrow(sscr, narrow, 36, n_dst, rows, 2)
    dgated = dot(dsecond, wo, NT).astype(BF16).astype(F32)
    dgating = dgated * mix
    dmix = (dgated * gating).astype(BF16)
    dq, dk, dv = [], [], []
    for a in range(2):
        part = slice(a * N, (a + 1) * N)
        ks, vs, prob, prob_b = saved[a]
        dprob = dot(vs, dmix[part], NT).astype(BF16).astype(F32)
        dv.append(unstack_heads(dot(prob_b, dmix[part]), masks_f))
        ds = []
        for h in range(HEADS):
            p = prob[h * N : (h + 1) * N]
            d = dprob[h * N : (h + 1) * N]
            ds.append(p * (d - jnp.sum(p * d, 0, keepdims=True)))
        ds = jnp.concatenate(ds, 0)
        if a == 0:
            plane[...] = ds
        else:
            plane[...] += ds
        ds = ds.astype(BF16)
        dq.append(dot(ds, ks, TN))
        dk.append(unstack_heads(dot(ds, q[part]), masks_f))
    for r in range(2):
        for h in range(HEADS):
            sscr[pl.ds(r * 4 + h, n_dst, stride=rows), :] = rows_of(plane, h * N + r, n_dst, 2)
    dproj = project_cotangent(dq, dk, dv, gating, dgating)
    put_wide(sscr, narrow, dot(n, dproj, TN), 12, n_dst, rows)
    dn = dot(dproj, w_ref[...].astype(BF16), NT).astype(BF16).astype(F32)
    dx, dgain = ln_back(dn, xhat, rstd, g_ref[...])
    zscr[...] = dsecond.astype(F32) + dx
    for r in range(2):
        for a in range(2):
            sscr[pl.ds(8 + r * 2 + a, n_dst, stride=rows), :] = rows_of(zscr, a * N + r, n_dst, 2)
    put_small(sscr, 38, [dgain_t, dgain], n_dst, rows)
    sscr[pl.ds(39, n_dst, stride=rows), :] = jnp.zeros((n_dst, C), F32)
    send_ref[...] = sscr[...].reshape(n_dst, rows, C).astype(BF16)


def project_cotangent(dq, dk, dv, gating, dgating):
    scale = (C // HEADS) ** (-0.5)
    dq = jnp.concatenate(dq, 0).astype(BF16).astype(F32) * scale
    dk = jnp.concatenate(dk, 0)
    dv = jnp.concatenate(dv, 0)
    dg = dgating * gating * (1.0 - gating)
    return jnp.concatenate([dq.astype(BF16), dk.astype(BF16), dv.astype(BF16), dg.astype(BF16)], 1)


def plane_back(planes, n, xhat, rstd, gain, wt8_ref, p8_ref, wt_ref):
    N = planes.shape[1]
    planes = planes.astype(BF16)
    wt8_ref[...] = jnp.zeros_like(wt8_ref)
    wt8_ref[0:HEADS, :] = wt_ref[...]
    p8_ref[...] = jnp.zeros_like(p8_ref)
    wide = planes.astype(F32)
    dns = []
    dbias = 0.0
    for r in range(2):
        p8_ref[0:HEADS, :] = wide[r * HEADS : (r + 1) * HEADS, :]
        p = p8_ref[...]
        dns.append(dot(p, wt8_ref[...], TN, FULL))
        dbias = dbias + dot(p.astype(BF16), n[r * N : (r + 1) * N])
    dn = jnp.concatenate(dns, 0).astype(BF16).astype(F32)
    dx, dgain = ln_back(dn, xhat, rstd, gain)
    return dx, dgain, dbias[0:HEADS]


def start_backward_kernel(
    recv_ref, x_ref, first_ref, qkv_ref, gating_ref, mix_ref, prob_ref, g_ref, w_ref, wo_ref, ge_ref, wte_ref,
    send_ref, sum_ref, gsum_ref,
    fscr, gscr, plane, narrow, sscr, wt8, p8,
):
    n_dst, in_rows, _ = recv_ref.shape
    N = 2 * n_dst
    rows = send_ref.shape[1]
    recv = recv_ref[...].astype(F32)
    total = jnp.sum(recv, 0)
    sum_ref[...] = total
    fscr[...] = recv.reshape(n_dst * in_rows, C)
    for r in range(2):
        for a in range(2):
            gscr[pl.ds(r * N + a, n_dst, stride=2), :] = rows_of(fscr, 8 + r * 2 + a, n_dst, in_rows)
    first = first_ref[...].astype(F32)
    xhat_e, rstd_e = ln_stats(first)
    n_e = (xhat_e * ge_ref[...]).astype(BF16)
    dxe, dgain_e, dbias_e = plane_back(total[0:8], n_e, xhat_e, rstd_e, ge_ref[...], wt8, p8, wte_ref)
    dfirst = (gscr[...] + dxe).astype(BF16)
    masks = head_masks(BF16)
    masks_f = head_masks(F32)
    xhat, rstd = ln_stats(x_ref[...].astype(F32))
    n = (xhat * g_ref[...]).astype(BF16)
    q = qkv_ref[:, :C]
    k = qkv_ref[:, C : 2 * C]
    v = qkv_ref[:, 2 * C :]
    gating = gating_ref[...]
    mix = mix_ref[...]
    gated = (gating * mix).astype(BF16)
    wo = wo_ref[...].astype(BF16)
    narrow[...] = dot(gated, dfirst, TN)
    put_narrow(sscr, narrow, 16, n_dst, rows, 2)
    dgated = dot(dfirst, wo, NT).astype(BF16).astype(F32)
    dgating = dgated * mix
    dmix = (dgated * gating).astype(BF16)
    dq, dk, dv = [], [], []
    for r in range(2):
        part = slice(r * N, (r + 1) * N)
        ks = stack_heads(k[part], masks)
        vs = stack_heads(v[part], masks)
        prob = prob_ref[part, :]
        dprob = dot(dmix[part], vs, NT).astype(BF16).astype(F32)
        dv.append(unstack_heads(dot(prob.astype(BF16), dmix[part], TN), masks_f))
        ds = []
        for h in range(HEADS):
            p = prob[:, h * N : (h + 1) * N]
            d = dprob[:, h * N : (h + 1) * N]
            ds.append(p * (d - jnp.sum(p * d, -1, keepdims=True)))
            if r == 0:
                plane[h * N : (h + 1) * N, :] = ds[h]
            else:
                plane[h * N : (h + 1) * N, :] += ds[h]
        ds = jnp.concatenate(ds, 1).astype(BF16)
        dq.append(dot(ds, ks))
        dk.append(unstack_heads(dot(ds, q[part], TN), masks_f))
    for r in range(2):
        for h in range(HEADS):
            sscr[pl.ds(r * 4 + h, n_dst, stride=rows), :] = rows_of(plane, h * N + r, n_dst, 2)
    dproj = project_cotangent(dq, dk, dv, gating, dgating)
    put_wide(sscr, narrow, dot(n, dproj, TN), 8, n_dst, rows)
    dn = dot(dproj, w_ref[...].astype(BF16), NT).astype(BF16).astype(F32)
    dx, dgain = ln_back(dn, xhat, rstd, g_ref[...])
    gsum_ref[...] = dfirst.astype(F32) + dx
    put_small(sscr, 18, [dbias_e[h : h + 1] for h in range(HEADS)] + [dgain_e, dgain], n_dst, rows)
    for i in range(19, rows):
        sscr[pl.ds(i, n_dst, stride=rows), :] = jnp.zeros((n_dst, C), F32)
    send_ref[...] = sscr[...].reshape(n_dst, rows, C).astype(BF16)


def start_plane_kernel(
    recv_ref, sum_ref, gsum_ref, x_ref, g_ref, wt_ref, grad_ref, part_ref, wt8, p8
):
    total = jnp.sum(recv_ref[...].astype(F32), 0)
    xhat, rstd = ln_stats(x_ref[...].astype(F32))
    n = (xhat * g_ref[...]).astype(BF16)
    dx, dgain, dbias = plane_back(total[0:8], n, xhat, rstd, g_ref[...], wt8, p8, wt_ref)
    grad_ref[...] = (gsum_ref[...] + dx).astype(BF16)
    part_ref[0:28, :] = sum_ref[12:40, :]
    part_ref[28:40, :] = total[8:20]
    part_ref[40:44, :] = dbias
    part_ref[44:45, :] = dgain
    part_ref[45:48, :] = jnp.zeros((3, C), F32)


def spread_kernel(a_ref, b_ref, c_ref, d_ref, out_ref):
    total = (a_ref[...] + b_ref[...]) + (c_ref[...] + d_ref[...])
    out_ref[...] = jnp.broadcast_to(total.astype(BF16)[None], out_ref.shape)


def finish_kernel(
    factor, recv_ref,
    gs_ref, ps_ref, bs_ref, os_ref, ge_ref, pe_ref, be_ref, oe_ref, gt_ref, up_ref, down_ref,
    fscr, block,
):
    n_dst, rows, _ = recv_ref.shape
    recv = recv_ref[...].astype(F32) * factor
    fscr[...] = recv.reshape(n_dst * rows, C)

    def wide(ref, row):
        for t in range(4):
            for i in range(2):
                block[pl.ds(i, n_dst, stride=2), :] = rows_of(fscr, row + i * 4 + t, n_dst, rows)
            ref[:, t * C : (t + 1) * C] = block[...]

    def narrow(ref, row, each):
        for i in range(each):
            ref[pl.ds(i, n_dst, stride=each), :] = rows_of(fscr, row + i, n_dst, rows)

    wide(pe_ref, 0)
    wide(up_ref, 8)
    narrow(down_ref, 16, 8)
    narrow(oe_ref, 24, 2)
    wide(ps_ref, 28)
    narrow(os_ref, 36, 2)
    tail = jnp.sum(recv[:, 40:48, :], 0)
    bs_ref[...] = tail[0:HEADS]

    def one(e, row):
        return fscr[e * rows + row : e * rows + row + 1, :]

    gt_ref[...] = one(0, 26)
    for h in range(HEADS):
        be_ref[h : h + 1, :] = one(h, 38)
    ge_ref[...] = one(1, 26) + one(4, 38)
    gs_ref[...] = tail[HEADS : HEADS + 1] + one(5, 38)


def shape(dims, dtype=F32):
    return jax.ShapeDtypeStruct(dims, dtype)


def call(body, out_shape, scratch, *operands):
    whole = pl.BlockSpec(memory_space=pltpu.VMEM)
    many = isinstance(out_shape, (list, tuple))
    return pl.pallas_call(
        body,
        out_shape=out_shape,
        in_specs=[whole] * len(operands),
        out_specs=[whole] * len(out_shape) if many else whole,
        scratch_shapes=[pltpu.VMEM(s, F32) for s in scratch],
        compiler_params=pltpu.CompilerParams(vmem_limit_bytes=VMEM_LIMIT),
    )(*operands)


def swap(buffer):
    return lax.all_to_all(buffer, "dap", split_axis=0, concat_axis=0, tiled=True)


def local(
    pair_input, cotangent, residue_mask, gain_start, proj_start, bias_start, output_start,
    gain_end, proj_end, bias_end, output_end, gain_transition, transition_up, transition_down,
):
    _, _, N, _ = pair_input.shape
    n_dst = N // 2
    x = pair_input.reshape(2 * N, C)
    cot = cotangent.reshape(2 * N, C)
    g_s, g_e, g_t = (g.reshape(1, C) for g in (gain_start, gain_end, gain_transition))
    wt_s, wt_e = bias_start.T, bias_end.T
    tokens = (2 * N, C)
    wide = (C, 4 * C)

    send = call(plane_local_kernel, shape((n_dst, 8, C), BF16), [(8, C)], x, g_s, wt_s)
    recv = swap(send)
    send, qkv, gating, mix, prob, first = call(
        start_forward_kernel,
        [shape((n_dst, 16, C), BF16), shape((2 * N, 3 * C), BF16), shape(tokens), shape(tokens),
         shape((2 * N, HEADS * N)), shape(tokens, BF16)],
        [(n_dst * 8, C), (HEADS * N, N), (n_dst * 16, C), (8, C)],
        recv, x, cot, residue_mask, g_s, proj_start, output_start, g_e, wt_e,
    )
    recv = swap(send)
    send = call(
        end_kernel,
        shape((n_dst, 40, C), BF16),
        [(n_dst * 16, C), tokens, tokens, (HEADS * N, N), (4 * C, C), (C, C), (n_dst * 40, C)],
        recv, residue_mask, g_e, proj_end, output_end, g_t, transition_up, transition_down,
    )
    recv = swap(send)
    send, summed, gsum = call(
        start_backward_kernel,
        [shape((n_dst, 24, C), BF16), shape((40, C)), shape(tokens)],
        [(n_dst * 40, C), tokens, (HEADS * N, N), (C, C), (n_dst * 24, C), (8, C), (8, C)],
        recv, x, first, qkv, gating, mix, prob, g_s, proj_start, output_start, g_e, wt_e,
    )
    recv = swap(send)
    grad, part = call(
        start_plane_kernel,
        [shape(tokens, BF16), shape((48, C))],
        [(8, C), (8, C)],
        recv, summed, gsum, x, g_s, wt_s,
    )
    n_dp = lax.axis_size("dp")
    others = [lax.ppermute(part, "dp", [(i, i ^ d) for i in range(n_dp)]) for d in range(1, n_dp)]
    send = call(spread_kernel, shape((n_dst, 48, C), BF16), [], part, *others)
    recv = swap(send)
    factor = 1.0 / (n_dp * N)
    gs, ps, bs, os, ge, pe, be, oe, gt, up, down = call(
        functools.partial(finish_kernel, factor),
        [shape((1, C)), shape(wide), shape((HEADS, C)), shape((C, C)),
         shape((1, C)), shape(wide), shape((HEADS, C)), shape((C, C)),
         shape((1, C)), shape(wide), shape((4 * C, C))],
        [(n_dst * 48, C), (C, C)],
        recv,
    )
    return (
        grad.reshape(1, 2, N, C), gs.reshape(C), ps, bs.T, os, ge.reshape(C), pe, be.T, oe, gt.reshape(C), up, down,
    )


def solution(mesh):
    rows = P("dp", "dap", None, None)
    in_specs = (rows, rows, P("dp", None)) + (P(),) * 11
    out_specs = (rows,) + (P(),) * 11
    return jax.shard_map(local, mesh=mesh, in_specs=in_specs, out_specs=out_specs, check_vma=False)
```

```python
import functools

import jax
import jax.numpy as jnp
from jax import lax
from jax.experimental import pallas as pl
from jax.experimental.pallas import tpu as pltpu
from jax.sharding import PartitionSpec as P

HEADS = 4
EPS = 1e-05
F32 = jnp.float32
BF16 = jnp.bfloat16
C = 128
HALF = 13
FULL = lax.Precision.HIGHEST
VMEM_LIMIT = 48 * 1024 * 1024


def dot(a, b, contract=((1,), (0,)), precision=None):
    return lax.dot_general(a, b, (contract, ((), ())), precision=precision, preferred_element_type=F32)


NN = ((1,), (0,))
NT = ((1,), (1,))
TN = ((0,), (0,))


def ln_stats(x):
    centre = x - jnp.mean(x, -1, keepdims=True)
    spread = jnp.mean(centre * centre, -1, keepdims=True)
    rstd = lax.rsqrt(spread + EPS)
    return centre * rstd, rstd


def ln_back(dn, xhat, rstd, gain):
    t = dn * gain
    m1 = jnp.mean(t, -1, keepdims=True)
    m2 = jnp.mean(t * xhat, -1, keepdims=True)
    dx = rstd * (t - m1 - xhat * m2)
    return dx.astype(BF16).astype(F32), jnp.sum(dn * xhat, 0, keepdims=True)


def head_masks(dtype):
    lane = lax.broadcasted_iota(jnp.int32, (1, C), 1)
    size = C // HEADS
    return [((lane >= h * size) & (lane < (h + 1) * size)).astype(dtype) for h in range(HEADS)]


def stack_heads(a, masks):
    return jnp.concatenate([a * m for m in masks], 0)


def unstack_heads(a, masks):
    n = a.shape[0] // HEADS
    total = a[:n] * masks[0]
    for h in range(1, HEADS):
        total = total + a[h * n : (h + 1) * n] * masks[h]
    return total


def project(n, w_ref):
    proj = dot(n, w_ref[...].astype(BF16))
    scale = (C // HEADS) ** (-0.5)
    q = (proj[:, :C] * scale).astype(BF16)
    k = proj[:, C : 2 * C].astype(BF16)
    v = proj[:, 2 * C : 3 * C].astype(BF16)
    return q, k, v, jax.nn.sigmoid(proj[:, 3 * C :])


def plane_of(n, wt):
    return dot(wt, n.astype(F32), NT, FULL)


def core_index():
    return lax.rem(lax.axis_index("dp"), 2)


def rows_of(ref, start, count, stride):
    return ref[pl.ds(start, count, stride=stride), :]


WT_S, WT_E = slice(0, 4), slice(4, 8)
G_S, G_E, G_T, KEPT = slice(8, 9), slice(9, 10), slice(10, 11), slice(11, 12)


def plane_local_kernel(
    x_hbm, gs_hbm, wts_hbm, ge_hbm, wte_hbm, gt_hbm, mask_hbm,
    out_ref, args_ref,
    x_ref, gs, wts, ge, wte, gt, mask, small, sems,
):
    n_dst, rows, _ = out_ref.shape
    moves = [(gs_hbm, gs), (wts_hbm, wts), (x_hbm, x_ref), (ge_hbm, ge), (wte_hbm, wte), (gt_hbm, gt), (mask_hbm, mask)]
    copies = [pltpu.make_async_copy(src, dst, sems.at[i]) for i, (src, dst) in enumerate(moves)]
    for copy in copies:
        copy.start()
    for copy in copies:
        copy.wait()
    args_ref[WT_S, :] = wts[...]
    args_ref[WT_E, :] = wte[...]
    args_ref[G_S, :] = gs[...]
    args_ref[G_E, :] = ge[...]
    args_ref[G_T, :] = gt[...]
    args_ref[KEPT, :] = mask[...].astype(F32)
    args_ref[12:16, :] = jnp.zeros((4, C), F32)
    xhat, _ = ln_stats(x_ref[...].astype(F32))
    n = (xhat * gs[...]).astype(BF16)
    plane = plane_of(n, wts[...])
    small[0:HEADS, :] = plane[:, :C]
    small[HEADS : 2 * HEADS, :] = plane[:, C:]
    out_ref[...] = jnp.broadcast_to(small[...].astype(BF16)[None], (n_dst, rows, C))


def start_scores_kernel(
    x_ref, cot_hbm, args_ref, w_ref, wo_hbm,
    qkv_ref, gating_ref, score_ref, n_ref, cot_ref, wo_ref,
    sems,
):
    copies = [pltpu.make_async_copy(cot_hbm, cot_ref, sems.at[0]), pltpu.make_async_copy(wo_hbm, wo_ref, sems.at[1])]
    for copy in copies:
        copy.start()
    N = score_ref.shape[1] // HEADS
    masks = head_masks(BF16)
    xhat, _ = ln_stats(x_ref[...].astype(F32))
    n = (xhat * args_ref[G_S, :]).astype(BF16)
    n_ref[...] = n
    q, k, v, gating = project(n, w_ref)
    qkv_ref[:, :C] = q
    qkv_ref[:, C : 2 * C] = k
    qkv_ref[:, 2 * C :] = v
    gating_ref[...] = gating
    for r in range(2):
        part = slice(r * N, (r + 1) * N)
        score_ref[part, :] = dot(q[part], stack_heads(k[part], masks), NT)
    for copy in copies:
        copy.wait()


def start_forward_kernel(
    recv_ref, x_ref, cot_ref, args_ref, qkv_ref, gating_ref, score_ref, wo_ref,
    send_ref, mix_ref, prob_ref, first_ref,
    fscr, plane, sscr, small,
):
    n_dst = recv_ref.shape[0]
    N = 2 * n_dst
    rows = send_ref.shape[1]
    fscr[...] = recv_ref[...].astype(F32).reshape(n_dst * 8, C)
    for r in range(2):
        for h in range(HEADS):
            plane[pl.ds(h * N + r, n_dst, stride=2), :] = rows_of(fscr, r * 4 + h, n_dst, 8)
    masks = head_masks(BF16)
    kept = args_ref[KEPT, :]
    x = x_ref[...].astype(F32)
    v = qkv_ref[:, 2 * C :]
    gating = gating_ref[...]
    mixes = []
    for r in range(2):
        part = slice(r * N, (r + 1) * N)
        probs = []
        for h in range(HEADS):
            w = jnp.exp(score_ref[part, h * N : (h + 1) * N] + plane[h * N : (h + 1) * N, :]) * kept
            probs.append(w / jnp.sum(w, -1, keepdims=True))
        prob = jnp.concatenate(probs, 1)
        prob_ref[part, :] = prob
        mixes.append(dot(prob.astype(BF16), stack_heads(v[part], masks)))
    mix = jnp.concatenate(mixes, 0)
    mix_ref[...] = mix
    update = dot((gating * mix).astype(BF16), wo_ref[...].astype(BF16))
    first = (x + update).astype(BF16)
    first_ref[...] = first
    first = first.astype(F32)
    xhat_e, _ = ln_stats(first)
    plane_e = plane_of((xhat_e * args_ref[G_E, :]).astype(BF16), args_ref[WT_E, :])
    small[0:HEADS, :] = plane_e[:, :N]
    small[HEADS : 2 * HEADS, :] = plane_e[:, N:]
    fscr[0 : 2 * N, :] = first
    for r in range(2):
        for a in range(2):
            sscr[pl.ds(r * 2 + a, n_dst, stride=rows), :] = rows_of(fscr, r * N + a, n_dst, 2)
    fscr[0 : 2 * N, :] = cot_ref[...].astype(F32)
    for r in range(2):
        for a in range(2):
            sscr[pl.ds(4 + r * 2 + a, n_dst, stride=rows), :] = rows_of(fscr, r * N + a, n_dst, 2)
    for i in range(8):
        sscr[pl.ds(8 + i, n_dst, stride=rows), :] = jnp.broadcast_to(small[i : i + 1, :], (n_dst, C))
    send_ref[...] = sscr[...].reshape(n_dst, rows, C).astype(BF16)


def put_wide(scr, src, value, starts, n_dst, rows):
    for t in range(4):
        src[...] = value[:, t * C : (t + 1) * C]
        for i in range(2):
            scr[pl.ds(starts[i] + t, n_dst, stride=rows), :] = rows_of(src, i, n_dst, 2)


def put_narrow(scr, src, row, n_dst, rows, each):
    for i in range(each):
        scr[pl.ds(row + i, n_dst, stride=rows), :] = rows_of(src, i, n_dst, each)


def put_small(scr, row, values, n_dst, rows):
    scr[pl.ds(row, n_dst, stride=rows), :] = jnp.zeros((n_dst, C), F32)
    for e, value in enumerate(values):
        scr[e * rows + row : e * rows + row + 1, :] = value


def end_kernel(
    recv_ref, args_ref, w_ref, wo_ref, wu_ref, wd_ref,
    send_ref, small_ref, hidden_ref, dup_ref, n_ref, n2_ref, cot_ref, dproj_ref, gated_ref, dsecond_ref,
    fscr, zscr, cscr, plane, sscr,
):
    n_dst, in_rows, _ = recv_ref.shape
    N = 2 * n_dst
    rows = send_ref.shape[1]
    fscr[...] = recv_ref[...].astype(F32).reshape(n_dst * in_rows, C)
    for r in range(2):
        for a in range(2):
            zscr[pl.ds(a * N + r, n_dst, stride=2), :] = rows_of(fscr, r * 2 + a, n_dst, in_rows)
            cscr[pl.ds(a * N + r, n_dst, stride=2), :] = rows_of(fscr, 4 + r * 2 + a, n_dst, in_rows)
        for h in range(HEADS):
            plane[pl.ds(h * N + r, n_dst, stride=2), :] = rows_of(fscr, 8 + r * 4 + h, n_dst, in_rows)
    masks = head_masks(BF16)
    masks_f = head_masks(F32)
    gain, gain_t = args_ref[G_E, :], args_ref[G_T, :]
    length = jnp.sum(args_ref[KEPT, :], -1, keepdims=True)
    kept = (lax.broadcasted_iota(jnp.int32, (N, 1), 0).astype(F32) < length).astype(F32)
    x = zscr[...]
    cot = cscr[...]
    xhat, rstd = ln_stats(x)
    n = (xhat * gain).astype(BF16)
    q, k, v, gating = project(n, w_ref)
    saved = []
    mixes = []
    for a in range(2):
        part = slice(a * N, (a + 1) * N)
        ks = stack_heads(k[part], masks)
        vs = stack_heads(v[part], masks)
        s = dot(ks, q[part], NT) + plane[...]
        probs = []
        for h in range(HEADS):
            w = jnp.exp(s[h * N : (h + 1) * N]) * kept
            probs.append(w / jnp.sum(w, 0, keepdims=True))
        prob = jnp.concatenate(probs, 0)
        prob_b = prob.astype(BF16)
        mixes.append(dot(prob_b, vs, TN))
        saved.append((ks, vs, prob, prob_b))
    mix = jnp.concatenate(mixes, 0)
    gated = (gating * mix).astype(BF16)
    wo = wo_ref[...].astype(BF16)
    second = (x + dot(gated, wo)).astype(BF16).astype(F32)
    xhat2, rstd2 = ln_stats(second)
    n2 = (xhat2 * gain_t).astype(BF16)
    wu = wu_ref[...].astype(BF16)
    wd = wd_ref[...].astype(BF16)
    cot_b = cot.astype(BF16)
    up = dot(n2, wu)
    cdf = 0.5 * (1.0 + lax.erf(up * (0.5**0.5)))
    hidden = (up * cdf).astype(BF16)
    dhidden = dot(cot_b, wd, NT).astype(BF16).astype(F32)
    slope = cdf + up * (jnp.exp(-0.5 * up * up) * 0.3989422804014327)
    dup = (dhidden * slope).astype(BF16)
    hidden_ref[...] = hidden
    dup_ref[...] = dup
    n_ref[...] = n
    n2_ref[...] = n2
    cot_ref[...] = cot_b
    gated_ref[...] = gated
    dn2 = dot(dup, wu, NT).astype(BF16).astype(F32)
    dx2, dgain_t = ln_back(dn2, xhat2, rstd2, gain_t)
    dsecond = (cot + dx2).astype(BF16)
    dsecond_ref[...] = dsecond
    dgated = dot(dsecond, wo, NT).astype(BF16).astype(F32)
    dgating = dgated * mix
    dmix = (dgated * gating).astype(BF16)
    dq, dk, dv = [], [], []
    for a in range(2):
        part = slice(a * N, (a + 1) * N)
        ks, vs, prob, prob_b = saved[a]
        dprob = dot(vs, dmix[part], NT).astype(BF16).astype(F32)
        dv.append(unstack_heads(dot(prob_b, dmix[part]), masks_f))
        ds = []
        for h in range(HEADS):
            p = prob[h * N : (h + 1) * N]
            d = dprob[h * N : (h + 1) * N]
            ds.append(p * (d - jnp.sum(p * d, 0, keepdims=True)))
        ds = jnp.concatenate(ds, 0)
        if a == 0:
            plane[...] = ds
        else:
            plane[...] += ds
        ds = ds.astype(BF16)
        dq.append(dot(ds, ks, TN))
        dk.append(unstack_heads(dot(ds, q[part]), masks_f))
    for r in range(2):
        for h in range(HEADS):
            sscr[pl.ds(r * 4 + h, n_dst, stride=rows), :] = rows_of(plane, h * N + r, n_dst, 2)
    dproj = project_cotangent(dq, dk, dv, gating, dgating)
    dproj_ref[...] = dproj
    dn = dot(dproj, w_ref[...].astype(BF16), NT).astype(BF16).astype(F32)
    dx, dgain = ln_back(dn, xhat, rstd, gain)
    zscr[...] = dsecond.astype(F32) + dx
    for r in range(2):
        for a in range(2):
            sscr[pl.ds(8 + r * 2 + a, n_dst, stride=rows), :] = rows_of(zscr, a * N + r, n_dst, 2)
    for i in range(12, rows):
        sscr[pl.ds(i, n_dst, stride=rows), :] = jnp.zeros((n_dst, C), F32)
    send_ref[...] = sscr[...].reshape(n_dst, rows, C).astype(BF16)
    small_ref[0:1, :] = dgain_t
    small_ref[1:2, :] = dgain
    small_ref[2:8, :] = jnp.zeros((6, C), F32)


def end_weights_kernel(
    hidden_ref, dup_ref, n_ref, n2_ref, cot_ref, dproj_ref, gated_ref, dsecond_ref,
    keep_ref, give_ref,
    down, narrow, wscr,
):
    half = keep_ref.shape[0]
    n_dst = half // HALF
    down[...] = dot(hidden_ref[...], cot_ref[...], TN)
    put_narrow(wscr, down, half + 4, n_dst, HALF, 8)
    put_wide(wscr, narrow, dot(n2_ref[...], dup_ref[...], TN), (8, half), n_dst, HALF)
    put_wide(wscr, narrow, dot(n_ref[...], dproj_ref[...], TN), (0, 4), n_dst, HALF)
    narrow[...] = dot(gated_ref[...], dsecond_ref[...], TN)
    for i in range(2):
        wscr[pl.ds(i * half + 12, n_dst, stride=HALF), :] = rows_of(narrow, i, n_dst, 2)
    core = core_index()
    keep_ref[...] = wscr[pl.ds(pl.multiple_of(core * half, 8), half), :]
    give_ref[...] = wscr[pl.ds(pl.multiple_of((1 - core) * half, 8), half), :].astype(BF16)


def project_cotangent(dq, dk, dv, gating, dgating):
    scale = (C // HEADS) ** (-0.5)
    dq = jnp.concatenate(dq, 0).astype(BF16).astype(F32) * scale
    dk = jnp.concatenate(dk, 0)
    dv = jnp.concatenate(dv, 0)
    dg = dgating * gating * (1.0 - gating)
    return jnp.concatenate([dq.astype(BF16), dk.astype(BF16), dv.astype(BF16), dg.astype(BF16)], 1)


def plane_back(planes, n, wt8_ref, p8_ref, wt):
    N = planes.shape[1]
    planes = planes.astype(BF16)
    wt8_ref[...] = jnp.zeros_like(wt8_ref)
    wt8_ref[0:HEADS, :] = wt
    p8_ref[...] = jnp.zeros_like(p8_ref)
    wide = planes.astype(F32)
    dns = []
    dbias = 0.0
    for r in range(2):
        p8_ref[0:HEADS, :] = wide[r * HEADS : (r + 1) * HEADS, :]
        p = p8_ref[...]
        dns.append(dot(p, wt8_ref[...], TN, FULL))
        dbias = dbias + dot(p.astype(BF16), n[r * N : (r + 1) * N])
    dn = jnp.concatenate(dns, 0).astype(BF16).astype(F32)
    return dn, dbias[0:HEADS]


def start_backward_kernel(
    recv_ref, keep_ref, got_ref, small_ref, n_ref, first_ref, qkv_ref, gating_ref, mix_ref, prob_ref, args_ref, wo_ref,
    send_ref, dfirst_ref, dproj_ref,
    fscr, gscr, plane, narrow, sscr, wscr, wt8, p8,
):
    n_dst, in_rows, _ = recv_ref.shape
    N = 2 * n_dst
    rows = send_ref.shape[1]
    recv = recv_ref[...].astype(F32)
    total = jnp.sum(recv, 0)
    fscr[...] = recv.reshape(n_dst * in_rows, C)
    for r in range(2):
        for a in range(2):
            gscr[pl.ds(r * N + a, n_dst, stride=2), :] = rows_of(fscr, 8 + r * 2 + a, n_dst, in_rows)
    first = first_ref[...].astype(F32)
    xhat_e, rstd_e = ln_stats(first)
    n_e = (xhat_e * args_ref[G_E, :]).astype(BF16)
    dn_e, dbias_e = plane_back(total[0:8], n_e, wt8, p8, args_ref[WT_E, :])
    dxe, dgain_e = ln_back(dn_e, xhat_e, rstd_e, args_ref[G_E, :])
    dfirst = (gscr[...] + dxe).astype(BF16)
    dfirst_ref[...] = dfirst
    masks = head_masks(BF16)
    masks_f = head_masks(F32)
    n = n_ref[...]
    q = qkv_ref[:, :C]
    k = qkv_ref[:, C : 2 * C]
    v = qkv_ref[:, 2 * C :]
    gating = gating_ref[...]
    mix = mix_ref[...]
    gated = (gating * mix).astype(BF16)
    wo = wo_ref[...].astype(BF16)
    narrow[...] = dot(gated, dfirst, TN)
    put_narrow(sscr, narrow, 16, n_dst, rows, 2)
    dgated = dot(dfirst, wo, NT).astype(BF16).astype(F32)
    dgating = dgated * mix
    dmix = (dgated * gating).astype(BF16)
    dq, dk, dv = [], [], []
    for r in range(2):
        part = slice(r * N, (r + 1) * N)
        ks = stack_heads(k[part], masks)
        vs = stack_heads(v[part], masks)
        prob = prob_ref[part, :]
        dprob = dot(dmix[part], vs, NT).astype(BF16).astype(F32)
        dv.append(unstack_heads(dot(prob.astype(BF16), dmix[part], TN), masks_f))
        ds = []
        for h in range(HEADS):
            p = prob[:, h * N : (h + 1) * N]
            d = dprob[:, h * N : (h + 1) * N]
            ds.append(p * (d - jnp.sum(p * d, -1, keepdims=True)))
            if r == 0:
                plane[h * N : (h + 1) * N, :] = ds[h]
            else:
                plane[h * N : (h + 1) * N, :] += ds[h]
        ds = jnp.concatenate(ds, 1).astype(BF16)
        dq.append(dot(ds, ks))
        dk.append(unstack_heads(dot(ds, q[part], TN), masks_f))
    for r in range(2):
        for h in range(HEADS):
            sscr[pl.ds(r * 4 + h, n_dst, stride=rows), :] = rows_of(plane, h * N + r, n_dst, 2)
    dproj = project_cotangent(dq, dk, dv, gating, dgating)
    put_wide(sscr, narrow, dot(n, dproj, TN), (8, 12), n_dst, rows)
    dproj_ref[...] = dproj
    smalls = [small_ref[0:1, :], small_ref[1:2, :], dgain_e] + [dbias_e[h : h + 1] for h in range(HEADS)]
    put_small(sscr, 18, smalls, n_dst, rows)
    wscr[...] = keep_ref[...] + got_ref[...].astype(F32)
    for i in range(HALF):
        sscr[pl.ds(19 + i, n_dst, stride=rows), :] = rows_of(wscr, i, n_dst, HALF)
    send_ref[...] = sscr[...].reshape(n_dst, rows, C).astype(BF16)


def start_plane_kernel(recv_ref, dproj_ref, x_ref, w_ref, args_ref, dn_ref, dn_plane_ref, part_ref, wt8, p8):
    total = jnp.sum(recv_ref[...].astype(F32), 0)
    xhat, _ = ln_stats(x_ref[...].astype(F32))
    n = (xhat * args_ref[G_S, :]).astype(BF16)
    dn = dot(dproj_ref[...], w_ref[...].astype(BF16), NT).astype(BF16)
    dn_ref[...] = dn
    dn_plane, dbias = plane_back(total[0:8], n, wt8, p8, args_ref[WT_S, :])
    dn_plane_ref[...] = dn_plane.astype(BF16)
    part_ref[0:11, :] = total[8:19]
    part_ref[11:15, :] = dbias
    part_ref[15:16, :] = jnp.sum((dn_plane + dn.astype(F32)) * xhat, 0, keepdims=True)
    part_ref[16 : 16 + HALF, :] = total[19 : 19 + HALF]
    part_ref[16 + HALF : 32, :] = jnp.zeros((16 - HALF, C), F32)


def grad_kernel(dn_ref, dn_plane_ref, dfirst_ref, x_ref, args_ref, grad_ref):
    xhat, rstd = ln_stats(x_ref[...].astype(F32))
    dx, _ = ln_back(dn_ref[...].astype(F32), xhat, rstd, args_ref[G_S, :])
    dx_plane, _ = ln_back(dn_plane_ref[...].astype(F32), xhat, rstd, args_ref[G_S, :])
    grad_ref[...] = (dfirst_ref[...].astype(F32) + dx + dx_plane).astype(BF16)


def spread_kernel(a_ref, b_ref, c_ref, d_ref, out_ref, scr):
    near = a_ref[...] + c_ref[...]
    total = near + (b_ref[...] + d_ref[...])
    scr[0:8, :] = jnp.where(core_index() == 0, total[0:8], total[8:16])
    scr[8:24, :] = near[16:32]
    out_ref[...] = jnp.broadcast_to(scr[...].astype(BF16)[None], out_ref.shape)


def finish_kernel(
    factor, recv_ref, other_ref,
    gs_ref, ps_ref, bs_ref, os_ref, ge_ref, pe_ref, be_ref, oe_ref, gt_ref, up_ref, down_ref,
    fscr, block,
):
    n_dst, half, _ = recv_ref.shape
    size = n_dst * half
    core = core_index()
    for index, ref in ((core, recv_ref), (1 - core, other_ref)):
        fscr[pl.ds(pl.multiple_of(index * size, 8), size), :] = ref[...].astype(F32).reshape(size, C) * factor

    def rows(row):
        return rows_of(fscr, row, n_dst, half)

    def wide(ref, starts):
        for t in range(4):
            for i in range(2):
                block[pl.ds(i, n_dst, stride=2), :] = rows(starts[i] + t)
            ref[:, t * C : (t + 1) * C] = block[...]

    def narrow(ref, starts):
        for i, start in enumerate(starts):
            ref[pl.ds(i, n_dst, stride=len(starts)), :] = rows(start)

    def one(e, row):
        start = e * half + row
        return fscr[start : start + 1, :]

    wide(ps_ref, (0, 4))
    wide(pe_ref, (8, 12))
    wide(up_ref, (16, size + 8))
    narrow(down_ref, range(size + 12, size + 20))
    narrow(os_ref, (size, size + 1))
    narrow(oe_ref, (20, size + 20))
    for h in range(HEADS):
        bs_ref[h : h + 1, :] = jnp.sum(rows(size + 3 + h), 0, keepdims=True)
        be_ref[h : h + 1, :] = one(3 + h, size + 2)
    gt_ref[...] = one(0, size + 2)
    ge_ref[...] = one(1, size + 2) + one(2, size + 2)
    gs_ref[...] = jnp.sum(rows(size + 7), 0, keepdims=True)


def shape(dims, dtype=F32):
    return jax.ShapeDtypeStruct(dims, dtype)


def call(body, out_shape, scratch, *operands, in_hbm=()):
    many = isinstance(out_shape, (list, tuple))
    whole = pl.BlockSpec(memory_space=pltpu.VMEM)
    spaces = [pltpu.HBM if i in in_hbm else pltpu.VMEM for i in range(len(operands))]
    operands = [pltpu.with_memory_space_constraint(a, m) if m is pltpu.HBM else a for a, m in zip(operands, spaces)]
    return pl.pallas_call(
        body,
        out_shape=out_shape,
        in_specs=[pl.BlockSpec(memory_space=m) for m in spaces],
        out_specs=[whole] * len(out_shape) if many else whole,
        scratch_shapes=[pltpu.VMEM(s, F32) if isinstance(s, tuple) else s for s in scratch],
        compiler_params=pltpu.CompilerParams(vmem_limit_bytes=VMEM_LIMIT),
    )(*operands)


def swap(buffer):
    return lax.all_to_all(buffer, "dap", split_axis=0, concat_axis=0, tiled=True)


def local(
    pair_input, cotangent, residue_mask, gain_start, proj_start, bias_start, output_start,
    gain_end, proj_end, bias_end, output_end, gain_transition, transition_up, transition_down,
):
    _, _, N, _ = pair_input.shape
    n_dst = N // 2
    x = pair_input.reshape(2 * N, C)
    cot = cotangent.reshape(2 * N, C)
    g_s, g_e, g_t = (g.reshape(1, C) for g in (gain_start, gain_end, gain_transition))
    wt_s, wt_e = bias_start.T, bias_end.T
    tokens = (2 * N, C)
    wide = (C, 4 * C)

    send, args = call(
        plane_local_kernel,
        [shape((n_dst, 8, C), BF16), shape((16, C))],
        [pltpu.VMEM(tokens, BF16), (1, C), (HEADS, C), (1, C), (HEADS, C), (1, C),
         pltpu.VMEM((1, C), jnp.int32), (8, C), pltpu.SemaphoreType.DMA((7,))],
        x, g_s, wt_s, g_e, wt_e, g_t, residue_mask,
        in_hbm=range(7),
    )
    recv = swap(send)
    qkv, gating, score, n, cot, wo = call(
        start_scores_kernel,
        [shape((2 * N, 3 * C), BF16), shape(tokens), shape((2 * N, HEADS * N)), shape(tokens, BF16),
         shape(tokens, BF16), shape((C, C))],
        [pltpu.SemaphoreType.DMA((2,))],
        x, cot, args, proj_start, output_start,
        in_hbm=(1, 4),
    )
    send, mix, prob, first = call(
        start_forward_kernel,
        [shape((n_dst, 16, C), BF16), shape(tokens), shape((2 * N, HEADS * N)), shape(tokens, BF16)],
        [(n_dst * 8, C), (HEADS * N, N), (n_dst * 16, C), (8, C)],
        recv, x, cot, args, qkv, gating, score, wo,
    )
    recv = swap(send)
    n_dp = lax.axis_size("dp")
    to_core = [(i, i ^ 1) for i in range(n_dp)]
    half = (n_dst * HALF, C)
    hidden = (2 * N, 4 * C)
    send, small, *saved = call(
        end_kernel,
        [shape((n_dst, 16, C), BF16), shape((8, C)), shape(hidden, BF16), shape(hidden, BF16), shape(tokens, BF16),
         shape(tokens, BF16), shape(tokens, BF16), shape(hidden, BF16), shape(tokens, BF16), shape(tokens, BF16)],
        [(n_dst * 16, C), tokens, tokens, (HEADS * N, N), (n_dst * 16, C)],
        recv, args, proj_end, output_end, transition_up, transition_down,
    )
    recv = swap(send)
    keep, give = call(
        end_weights_kernel,
        [shape(half), shape(half, BF16)],
        [(4 * C, C), (C, C), (n_dst * 2 * HALF, C)],
        *saved,
    )
    got = lax.ppermute(give, "dp", to_core)
    send, dfirst, dproj = call(
        start_backward_kernel,
        [shape((n_dst, 32, C), BF16), shape(tokens, BF16), shape(hidden, BF16)],
        [(n_dst * 16, C), tokens, (HEADS * N, N), (C, C), (n_dst * 32, C), half, (8, C), (8, C)],
        recv, keep, got, small, n, first, qkv, gating, mix, prob, args, wo,
    )
    recv = swap(send)
    dn, dn_plane, part = call(
        start_plane_kernel,
        [shape(tokens, BF16), shape(tokens, BF16), shape((32, C))],
        [(8, C), (8, C)],
        recv, dproj, x, proj_start, args,
    )
    others = [lax.ppermute(part, "dp", [(i, i ^ d) for i in range(n_dp)]) for d in range(1, n_dp)]
    grad = call(grad_kernel, shape(tokens, BF16), [], dn, dn_plane, dfirst, x, args)
    send = call(spread_kernel, shape((n_dst, 24, C), BF16), [(24, C)], part, *others)
    recv = swap(send)
    other = lax.ppermute(recv, "dp", to_core)
    factor = 1.0 / (n_dp * N)
    gs, ps, bs, os, ge, pe, be, oe, gt, up, down = call(
        functools.partial(finish_kernel, factor),
        [shape((1, C)), shape(wide), shape((HEADS, C)), shape((C, C)),
         shape((1, C)), shape(wide), shape((HEADS, C)), shape((C, C)),
         shape((1, C)), shape(wide), shape((4 * C, C))],
        [(n_dst * 48, C), (C, C)],
        recv, other,
    )
    return (
        grad.reshape(1, 2, N, C), gs.reshape(C), ps, bs.T, os, ge.reshape(C), pe, be.T, oe, gt.reshape(C), up, down,
    )


def solution(mesh):
    rows = P("dp", "dap", None, None)
    in_specs = (rows, rows, P("dp", None)) + (P(),) * 11
    out_specs = (rows,) + (P(),) * 11
    return jax.shard_map(local, mesh=mesh, in_specs=in_specs, out_specs=out_specs, check_vma=False)
```

```python
import functools

import jax
import jax.numpy as jnp
from jax import lax
from jax.experimental import pallas as pl
from jax.experimental.pallas import tpu as pltpu
from jax.sharding import PartitionSpec as P

HEADS = 4
EPS = 1e-05
F32 = jnp.float32
BF16 = jnp.bfloat16
C = 128
HALF = 13
VMEM_LIMIT = 48 * 1024 * 1024


def dot(a, b, contract=((1,), (0,))):
    return lax.dot_general(a, b, (contract, ((), ())), preferred_element_type=F32)


NN = ((1,), (0,))
NT = ((1,), (1,))
TN = ((0,), (0,))


def ln_stats(x):
    centre = x - jnp.mean(x, -1, keepdims=True)
    spread = jnp.mean(centre * centre, -1, keepdims=True)
    rstd = lax.rsqrt(spread + EPS)
    return centre * rstd, rstd


def ln_back(dn, xhat, rstd, gain):
    t = dn * gain
    m1 = jnp.mean(t, -1, keepdims=True)
    m2 = jnp.mean(t * xhat, -1, keepdims=True)
    dx = rstd * (t - m1 - xhat * m2)
    return dx.astype(BF16).astype(F32), jnp.sum(dn * xhat, 0, keepdims=True)


def head_masks(dtype):
    lane = lax.broadcasted_iota(jnp.int32, (1, C), 1)
    size = C // HEADS
    return [((lane >= h * size) & (lane < (h + 1) * size)).astype(dtype) for h in range(HEADS)]


def stack_heads(a, masks):
    return jnp.concatenate([a * m for m in masks], 0)


def unstack_heads(a, masks):
    n = a.shape[0] // HEADS
    total = a[:n] * masks[0]
    for h in range(1, HEADS):
        total = total + a[h * n : (h + 1) * n] * masks[h]
    return total


def project(n, w_ref):
    proj = dot(n, w_ref[...].astype(BF16))
    scale = (C // HEADS) ** (-0.5)
    q = (proj[:, :C] * scale).astype(BF16)
    k = proj[:, C : 2 * C].astype(BF16)
    v = proj[:, 2 * C : 3 * C].astype(BF16)
    return q, k, v, jax.nn.sigmoid(proj[:, 3 * C :])


def split(scr, wt):
    for i in range(3):
        part = wt.astype(BF16).astype(F32)
        scr[i * HEADS : (i + 1) * HEADS, :] = part
        wt = wt - part
    scr[3 * HEADS : 16, :] = jnp.zeros((16 - 3 * HEADS, C), F32)
    return scr[...].astype(BF16)


def plane_of(n, parts):
    out = dot(parts, n, NT)
    return out[0:4] + out[4:8] + out[8:12]


def core_index():
    return lax.rem(lax.axis_index("dp"), 2)


def rows_of(ref, start, count, stride):
    return ref[pl.ds(start, count, stride=stride), :]


WT_S, WT_E = slice(0, 16), slice(16, 32)
G_S, G_E, G_T, KEPT = slice(0, 1), slice(1, 2), slice(2, 3), slice(3, 4)


def plane_local_kernel(
    x_hbm, gs_hbm, wts_hbm, ge_hbm, wte_hbm, gt_hbm, mask_hbm,
    out_ref, args_ref, parts_ref,
    x_ref, gs, wts, ge, wte, gt, mask, small, scr, sems,
):
    n_dst, rows, _ = out_ref.shape
    moves = [(gs_hbm, gs), (wts_hbm, wts), (x_hbm, x_ref), (ge_hbm, ge), (wte_hbm, wte), (gt_hbm, gt), (mask_hbm, mask)]
    copies = [pltpu.make_async_copy(src, dst, sems.at[i]) for i, (src, dst) in enumerate(moves)]
    for copy in copies:
        copy.start()
    for copy in copies:
        copy.wait()
    parts_ref[WT_S, :] = split(scr, wts[...])
    parts_ref[WT_E, :] = split(scr, wte[...])
    args_ref[G_S, :] = gs[...]
    args_ref[G_E, :] = ge[...]
    args_ref[G_T, :] = gt[...]
    args_ref[KEPT, :] = mask[...].astype(F32)
    args_ref[4:8, :] = jnp.zeros((4, C), F32)
    xhat, _ = ln_stats(x_ref[...].astype(F32))
    n = (xhat * gs[...]).astype(BF16)
    plane = plane_of(n, parts_ref[WT_S, :])
    small[0:HEADS, :] = plane[:, :C]
    small[HEADS : 2 * HEADS, :] = plane[:, C:]
    out_ref[...] = jnp.broadcast_to(small[...].astype(BF16)[None], (n_dst, rows, C))


def start_scores_kernel(
    x_ref, cot_hbm, args_ref, w_ref, wo_hbm,
    qkv_ref, gating_ref, score_ref, n_ref, cot_ref, wo_ref,
    sems,
):
    copies = [pltpu.make_async_copy(cot_hbm, cot_ref, sems.at[0]), pltpu.make_async_copy(wo_hbm, wo_ref, sems.at[1])]
    for copy in copies:
        copy.start()
    N = score_ref.shape[1] // HEADS
    masks = head_masks(BF16)
    xhat, _ = ln_stats(x_ref[...].astype(F32))
    n = (xhat * args_ref[G_S, :]).astype(BF16)
    n_ref[...] = n
    q, k, v, gating = project(n, w_ref)
    qkv_ref[:, :C] = q
    qkv_ref[:, C : 2 * C] = k
    qkv_ref[:, 2 * C :] = v
    gating_ref[...] = gating
    for r in range(2):
        part = slice(r * N, (r + 1) * N)
        score_ref[part, :] = dot(q[part], stack_heads(k[part], masks), NT)
    for copy in copies:
        copy.wait()


def start_forward_kernel(
    recv_ref, x_ref, cot_ref, args_ref, parts_ref, qkv_ref, gating_ref, score_ref, wo_ref,
    send_ref, mix_ref, prob_ref, first_ref,
    fscr, plane, sscr, small,
):
    n_dst = recv_ref.shape[0]
    N = 2 * n_dst
    rows = send_ref.shape[1]
    fscr[...] = recv_ref[...].astype(F32).reshape(n_dst * 8, C)
    for r in range(2):
        for h in range(HEADS):
            plane[pl.ds(h * N + r, n_dst, stride=2), :] = rows_of(fscr, r * 4 + h, n_dst, 8)
    masks = head_masks(BF16)
    kept = args_ref[KEPT, :]
    x = x_ref[...].astype(F32)
    v = qkv_ref[:, 2 * C :]
    gating = gating_ref[...]
    mixes = []
    for r in range(2):
        part = slice(r * N, (r + 1) * N)
        probs = []
        for h in range(HEADS):
            w = jnp.exp(score_ref[part, h * N : (h + 1) * N] + plane[h * N : (h + 1) * N, :]) * kept
            probs.append(w / jnp.sum(w, -1, keepdims=True))
        prob = jnp.concatenate(probs, 1)
        prob_ref[part, :] = prob
        mixes.append(dot(prob.astype(BF16), stack_heads(v[part], masks)))
    mix = jnp.concatenate(mixes, 0)
    mix_ref[...] = mix
    update = dot((gating * mix).astype(BF16), wo_ref[...].astype(BF16))
    first = (x + update).astype(BF16)
    first_ref[...] = first
    first = first.astype(F32)
    xhat_e, _ = ln_stats(first)
    plane_e = plane_of((xhat_e * args_ref[G_E, :]).astype(BF16), parts_ref[WT_E, :])
    small[0:HEADS, :] = plane_e[:, :N]
    small[HEADS : 2 * HEADS, :] = plane_e[:, N:]
    fscr[0 : 2 * N, :] = first
    for r in range(2):
        for a in range(2):
            sscr[pl.ds(r * 2 + a, n_dst, stride=rows), :] = rows_of(fscr, r * N + a, n_dst, 2)
    fscr[0 : 2 * N, :] = cot_ref[...].astype(F32)
    for r in range(2):
        for a in range(2):
            sscr[pl.ds(4 + r * 2 + a, n_dst, stride=rows), :] = rows_of(fscr, r * N + a, n_dst, 2)
    for i in range(8):
        sscr[pl.ds(8 + i, n_dst, stride=rows), :] = jnp.broadcast_to(small[i : i + 1, :], (n_dst, C))
    send_ref[...] = sscr[...].reshape(n_dst, rows, C).astype(BF16)


def put_wide(scr, src, value, starts, n_dst, rows):
    for t in range(4):
        src[...] = value[:, t * C : (t + 1) * C]
        for i in range(2):
            scr[pl.ds(starts[i] + t, n_dst, stride=rows), :] = rows_of(src, i, n_dst, 2)


def put_narrow(scr, src, row, n_dst, rows, each):
    for i in range(each):
        scr[pl.ds(row + i, n_dst, stride=rows), :] = rows_of(src, i, n_dst, each)


def put_small(scr, row, values, n_dst, rows):
    scr[pl.ds(row, n_dst, stride=rows), :] = jnp.zeros((n_dst, C), F32)
    for e, value in enumerate(values):
        scr[e * rows + row : e * rows + row + 1, :] = value


def end_kernel(
    recv_ref, args_ref, w_ref, wo_ref, wu_ref, wd_ref,
    send_ref, small_ref, hidden_ref, dup_ref, n_ref, n2_ref, cot_ref, dproj_ref, gated_ref, dsecond_ref,
    fscr, zscr, cscr, plane, sscr,
):
    n_dst, in_rows, _ = recv_ref.shape
    N = 2 * n_dst
    rows = send_ref.shape[1]
    fscr[...] = recv_ref[...].astype(F32).reshape(n_dst * in_rows, C)
    for r in range(2):
        for a in range(2):
            zscr[pl.ds(a * N + r, n_dst, stride=2), :] = rows_of(fscr, r * 2 + a, n_dst, in_rows)
            cscr[pl.ds(a * N + r, n_dst, stride=2), :] = rows_of(fscr, 4 + r * 2 + a, n_dst, in_rows)
        for h in range(HEADS):
            plane[pl.ds(h * N + r, n_dst, stride=2), :] = rows_of(fscr, 8 + r * 4 + h, n_dst, in_rows)
    masks = head_masks(BF16)
    masks_f = head_masks(F32)
    gain, gain_t = args_ref[G_E, :], args_ref[G_T, :]
    length = jnp.sum(args_ref[KEPT, :], -1, keepdims=True)
    kept = (lax.broadcasted_iota(jnp.int32, (N, 1), 0).astype(F32) < length).astype(F32)
    x = zscr[...]
    cot = cscr[...]
    xhat, rstd = ln_stats(x)
    n = (xhat * gain).astype(BF16)
    q, k, v, gating = project(n, w_ref)
    saved = []
    mixes = []
    for a in range(2):
        part = slice(a * N, (a + 1) * N)
        ks = stack_heads(k[part], masks)
        vs = stack_heads(v[part], masks)
        s = dot(ks, q[part], NT) + plane[...]
        probs = []
        for h in range(HEADS):
            w = jnp.exp(s[h * N : (h + 1) * N]) * kept
            probs.append(w / jnp.sum(w, 0, keepdims=True))
        prob = jnp.concatenate(probs, 0)
        prob_b = prob.astype(BF16)
        mixes.append(dot(prob_b, vs, TN))
        saved.append((ks, vs, prob, prob_b))
    mix = jnp.concatenate(mixes, 0)
    gated = (gating * mix).astype(BF16)
    wo = wo_ref[...].astype(BF16)
    second = (x + dot(gated, wo)).astype(BF16).astype(F32)
    xhat2, rstd2 = ln_stats(second)
    n2 = (xhat2 * gain_t).astype(BF16)
    wu = wu_ref[...].astype(BF16)
    wd = wd_ref[...].astype(BF16)
    cot_b = cot.astype(BF16)
    up = dot(n2, wu)
    cdf = 0.5 * (1.0 + lax.erf(up * (0.5**0.5)))
    hidden = (up * cdf).astype(BF16)
    dhidden = dot(cot_b, wd, NT).astype(BF16).astype(F32)
    slope = cdf + up * (jnp.exp(-0.5 * up * up) * 0.3989422804014327)
    dup = (dhidden * slope).astype(BF16)
    hidden_ref[...] = hidden
    dup_ref[...] = dup
    n_ref[...] = n
    n2_ref[...] = n2
    cot_ref[...] = cot_b
    gated_ref[...] = gated
    dn2 = dot(dup, wu, NT).astype(BF16).astype(F32)
    dx2, dgain_t = ln_back(dn2, xhat2, rstd2, gain_t)
    dsecond = (cot + dx2).astype(BF16)
    dsecond_ref[...] = dsecond
    dgated = dot(dsecond, wo, NT).astype(BF16).astype(F32)
    dgating = dgated * mix
    dmix = (dgated * gating).astype(BF16)
    dq, dk, dv = [], [], []
    for a in range(2):
        part = slice(a * N, (a + 1) * N)
        ks, vs, prob, prob_b = saved[a]
        dprob = dot(vs, dmix[part], NT).astype(BF16).astype(F32)
        dv.append(unstack_heads(dot(prob_b, dmix[part]), masks_f))
        ds = []
        for h in range(HEADS):
            p = prob[h * N : (h + 1) * N]
            d = dprob[h * N : (h + 1) * N]
            ds.append(p * (d - jnp.sum(p * d, 0, keepdims=True)))
        ds = jnp.concatenate(ds, 0)
        if a == 0:
            plane[...] = ds
        else:
            plane[...] += ds
        ds = ds.astype(BF16)
        dq.append(dot(ds, ks, TN))
        dk.append(unstack_heads(dot(ds, q[part]), masks_f))
    for r in range(2):
        for h in range(HEADS):
            sscr[pl.ds(r * 4 + h, n_dst, stride=rows), :] = rows_of(plane, h * N + r, n_dst, 2)
    dproj = project_cotangent(dq, dk, dv, gating, dgating)
    dproj_ref[...] = dproj
    dn = dot(dproj, w_ref[...].astype(BF16), NT).astype(BF16).astype(F32)
    dx, dgain = ln_back(dn, xhat, rstd, gain)
    zscr[...] = dsecond.astype(F32) + dx
    for r in range(2):
        for a in range(2):
            sscr[pl.ds(8 + r * 2 + a, n_dst, stride=rows), :] = rows_of(zscr, a * N + r, n_dst, 2)
    for i in range(12, rows):
        sscr[pl.ds(i, n_dst, stride=rows), :] = jnp.zeros((n_dst, C), F32)
    send_ref[...] = sscr[...].reshape(n_dst, rows, C).astype(BF16)
    small_ref[0:1, :] = dgain_t
    small_ref[1:2, :] = dgain
    small_ref[2:8, :] = jnp.zeros((6, C), F32)


def end_weights_kernel(
    hidden_ref, dup_ref, n_ref, n2_ref, cot_ref, dproj_ref, gated_ref, dsecond_ref,
    keep_ref, give_ref,
    down, narrow, wscr,
):
    half = keep_ref.shape[0]
    n_dst = half // HALF
    down[...] = dot(hidden_ref[...], cot_ref[...], TN)
    put_narrow(wscr, down, half + 4, n_dst, HALF, 8)
    put_wide(wscr, narrow, dot(n2_ref[...], dup_ref[...], TN), (8, half), n_dst, HALF)
    put_wide(wscr, narrow, dot(n_ref[...], dproj_ref[...], TN), (0, 4), n_dst, HALF)
    narrow[...] = dot(gated_ref[...], dsecond_ref[...], TN)
    for i in range(2):
        wscr[pl.ds(i * half + 12, n_dst, stride=HALF), :] = rows_of(narrow, i, n_dst, 2)
    core = core_index()
    keep_ref[...] = wscr[pl.ds(pl.multiple_of(core * half, 8), half), :]
    give_ref[...] = wscr[pl.ds(pl.multiple_of((1 - core) * half, 8), half), :].astype(BF16)


def project_cotangent(dq, dk, dv, gating, dgating):
    scale = (C // HEADS) ** (-0.5)
    dq = jnp.concatenate(dq, 0).astype(BF16).astype(F32) * scale
    dk = jnp.concatenate(dk, 0)
    dv = jnp.concatenate(dv, 0)
    dg = dgating * gating * (1.0 - gating)
    return jnp.concatenate([dq.astype(BF16), dk.astype(BF16), dv.astype(BF16), dg.astype(BF16)], 1)


def plane_back(planes, n, p_ref, parts):
    N = planes.shape[1]
    p_ref[...] = jnp.zeros_like(p_ref)
    dns = []
    dbias = 0.0
    for r in range(2):
        for i in range(3):
            p_ref[i * HEADS : (i + 1) * HEADS, :] = planes[r * HEADS : (r + 1) * HEADS]
        p = p_ref[...].astype(BF16)
        dns.append(dot(p, parts, TN))
        dbias = dbias + dot(p, n[r * N : (r + 1) * N])
    return jnp.concatenate(dns, 0).astype(BF16).astype(F32), dbias[0:HEADS]


def start_backward_kernel(
    recv_ref, keep_ref, got_ref, small_ref, n_ref, first_ref, qkv_ref, gating_ref, mix_ref, prob_ref, args_ref, parts_ref, wo_ref,
    send_ref, dfirst_ref, dproj_ref,
    fscr, gscr, plane, narrow, sscr, wscr, p_ref,
):
    n_dst, in_rows, _ = recv_ref.shape
    N = 2 * n_dst
    rows = send_ref.shape[1]
    recv = recv_ref[...].astype(F32)
    total = jnp.sum(recv, 0)
    fscr[...] = recv.reshape(n_dst * in_rows, C)
    for r in range(2):
        for a in range(2):
            gscr[pl.ds(r * N + a, n_dst, stride=2), :] = rows_of(fscr, 8 + r * 2 + a, n_dst, in_rows)
    first = first_ref[...].astype(F32)
    xhat_e, rstd_e = ln_stats(first)
    n_e = (xhat_e * args_ref[G_E, :]).astype(BF16)
    dn_e, dbias_e = plane_back(total[0:8], n_e, p_ref, parts_ref[WT_E, :])
    dxe, dgain_e = ln_back(dn_e, xhat_e, rstd_e, args_ref[G_E, :])
    dfirst = (gscr[...] + dxe).astype(BF16)
    dfirst_ref[...] = dfirst
    masks = head_masks(BF16)
    masks_f = head_masks(F32)
    n = n_ref[...]
    q = qkv_ref[:, :C]
    k = qkv_ref[:, C : 2 * C]
    v = qkv_ref[:, 2 * C :]
    gating = gating_ref[...]
    mix = mix_ref[...]
    gated = (gating * mix).astype(BF16)
    wo = wo_ref[...].astype(BF16)
    narrow[...] = dot(gated, dfirst, TN)
    put_narrow(sscr, narrow, 16, n_dst, rows, 2)
    dgated = dot(dfirst, wo, NT).astype(BF16).astype(F32)
    dgating = dgated * mix
    dmix = (dgated * gating).astype(BF16)
    dq, dk, dv = [], [], []
    for r in range(2):
        part = slice(r * N, (r + 1) * N)
        ks = stack_heads(k[part], masks)
        vs = stack_heads(v[part], masks)
        prob = prob_ref[part, :]
        dprob = dot(dmix[part], vs, NT).astype(BF16).astype(F32)
        dv.append(unstack_heads(dot(prob.astype(BF16), dmix[part], TN), masks_f))
        ds = []
        for h in range(HEADS):
            p = prob[:, h * N : (h + 1) * N]
            d = dprob[:, h * N : (h + 1) * N]
            ds.append(p * (d - jnp.sum(p * d, -1, keepdims=True)))
            if r == 0:
                plane[h * N : (h + 1) * N, :] = ds[h]
            else:
                plane[h * N : (h + 1) * N, :] += ds[h]
        ds = jnp.concatenate(ds, 1).astype(BF16)
        dq.append(dot(ds, ks))
        dk.append(unstack_heads(dot(ds, q[part], TN), masks_f))
    for r in range(2):
        for h in range(HEADS):
            sscr[pl.ds(r * 4 + h, n_dst, stride=rows), :] = rows_of(plane, h * N + r, n_dst, 2)
    dproj = project_cotangent(dq, dk, dv, gating, dgating)
    put_wide(sscr, narrow, dot(n, dproj, TN), (8, 12), n_dst, rows)
    dproj_ref[...] = dproj
    smalls = [small_ref[0:1, :], small_ref[1:2, :], dgain_e] + [dbias_e[h : h + 1] for h in range(HEADS)]
    put_small(sscr, 18, smalls, n_dst, rows)
    wscr[...] = keep_ref[...] + got_ref[...].astype(F32)
    for i in range(HALF):
        sscr[pl.ds(19 + i, n_dst, stride=rows), :] = rows_of(wscr, i, n_dst, HALF)
    send_ref[...] = sscr[...].reshape(n_dst, rows, C).astype(BF16)


def start_plane_kernel(recv_ref, dproj_ref, x_ref, w_ref, args_ref, parts_ref, dn_ref, dn_plane_ref, part_ref, p_ref):
    total = jnp.sum(recv_ref[...].astype(F32), 0)
    xhat, _ = ln_stats(x_ref[...].astype(F32))
    n = (xhat * args_ref[G_S, :]).astype(BF16)
    dn = dot(dproj_ref[...], w_ref[...].astype(BF16), NT).astype(BF16)
    dn_ref[...] = dn
    dn_plane, dbias = plane_back(total[0:8], n, p_ref, parts_ref[WT_S, :])
    dn_plane_ref[...] = dn_plane.astype(BF16)
    part_ref[0:11, :] = total[8:19]
    part_ref[11:15, :] = dbias
    part_ref[15:16, :] = jnp.sum((dn_plane + dn.astype(F32)) * xhat, 0, keepdims=True)
    part_ref[16 : 16 + HALF, :] = total[19 : 19 + HALF]
    part_ref[16 + HALF : 32, :] = jnp.zeros((16 - HALF, C), F32)


def grad_kernel(dn_ref, dn_plane_ref, dfirst_ref, x_ref, args_ref, grad_ref):
    xhat, rstd = ln_stats(x_ref[...].astype(F32))
    dx, _ = ln_back(dn_ref[...].astype(F32), xhat, rstd, args_ref[G_S, :])
    dx_plane, _ = ln_back(dn_plane_ref[...].astype(F32), xhat, rstd, args_ref[G_S, :])
    grad_ref[...] = (dfirst_ref[...].astype(F32) + dx + dx_plane).astype(BF16)


def spread_kernel(a_ref, b_ref, c_ref, d_ref, out_ref, scr):
    near = a_ref[...] + c_ref[...]
    total = near + (b_ref[...] + d_ref[...])
    scr[0:8, :] = jnp.where(core_index() == 0, total[0:8], total[8:16])
    scr[8:24, :] = near[16:32]
    out_ref[...] = jnp.broadcast_to(scr[...].astype(BF16)[None], out_ref.shape)


def finish_kernel(
    factor, recv_ref, other_ref,
    gs_out, ps_out, bs_out, os_out, ge_out, pe_out, be_out, oe_out, gt_out, up_out, down_out,
    gs_ref, ps_ref, bs_ref, os_ref, ge_ref, pe_ref, be_ref, oe_ref, gt_ref, up_ref, down_ref,
    fscr, block, sems,
):
    copies = []

    def leave(ref, out):
        copies.append(pltpu.make_async_copy(ref, out, sems.at[len(copies)]))
        copies[-1].start()

    n_dst, half, _ = recv_ref.shape
    size = n_dst * half
    core = core_index()
    for index, ref in ((core, recv_ref), (1 - core, other_ref)):
        fscr[pl.ds(pl.multiple_of(index * size, 8), size), :] = ref[...].astype(F32).reshape(size, C) * factor

    def rows(row):
        return rows_of(fscr, row, n_dst, half)

    def wide(ref, starts):
        for t in range(4):
            for i in range(2):
                block[pl.ds(i, n_dst, stride=2), :] = rows(starts[i] + t)
            ref[:, t * C : (t + 1) * C] = block[...]

    def narrow(ref, starts):
        for i, start in enumerate(starts):
            ref[pl.ds(i, n_dst, stride=len(starts)), :] = rows(start)

    def one(e, row):
        start = e * half + row
        return fscr[start : start + 1, :]

    wide(ps_ref, (0, 4))
    leave(ps_ref, ps_out)
    wide(pe_ref, (8, 12))
    leave(pe_ref, pe_out)
    wide(up_ref, (16, size + 8))
    leave(up_ref, up_out)
    narrow(down_ref, range(size + 12, size + 20))
    leave(down_ref, down_out)
    narrow(os_ref, (size, size + 1))
    leave(os_ref, os_out)
    narrow(oe_ref, (20, size + 20))
    leave(oe_ref, oe_out)
    for h in range(HEADS):
        bs_ref[h : h + 1, :] = jnp.sum(rows(size + 3 + h), 0, keepdims=True)
        be_ref[h : h + 1, :] = one(3 + h, size + 2)
    gt_ref[...] = one(0, size + 2)
    ge_ref[...] = one(1, size + 2) + one(2, size + 2)
    gs_ref[...] = jnp.sum(rows(size + 7), 0, keepdims=True)
    for ref, out in ((bs_ref, bs_out), (be_ref, be_out), (gt_ref, gt_out), (ge_ref, ge_out), (gs_ref, gs_out)):
        leave(ref, out)
    for copy in copies:
        copy.wait()


def shape(dims, dtype=F32):
    return jax.ShapeDtypeStruct(dims, dtype)


def call(body, out_shape, scratch, *operands, in_hbm=(), out=pltpu.VMEM):
    many = isinstance(out_shape, (list, tuple))
    whole = pl.BlockSpec(memory_space=out)
    spaces = [pltpu.HBM if i in in_hbm else pltpu.VMEM for i in range(len(operands))]
    operands = [pltpu.with_memory_space_constraint(a, m) if m is pltpu.HBM else a for a, m in zip(operands, spaces)]
    return pl.pallas_call(
        body,
        out_shape=out_shape,
        in_specs=[pl.BlockSpec(memory_space=m) for m in spaces],
        out_specs=[whole] * len(out_shape) if many else whole,
        scratch_shapes=[pltpu.VMEM(s, F32) if isinstance(s, tuple) else s for s in scratch],
        compiler_params=pltpu.CompilerParams(vmem_limit_bytes=VMEM_LIMIT),
    )(*operands)


def swap(buffer):
    return lax.all_to_all(buffer, "dap", split_axis=0, concat_axis=0, tiled=True)


def local(
    pair_input, cotangent, residue_mask, gain_start, proj_start, bias_start, output_start,
    gain_end, proj_end, bias_end, output_end, gain_transition, transition_up, transition_down,
):
    _, _, N, _ = pair_input.shape
    n_dst = N // 2
    x = pair_input.reshape(2 * N, C)
    cot = cotangent.reshape(2 * N, C)
    g_s, g_e, g_t = (g.reshape(1, C) for g in (gain_start, gain_end, gain_transition))
    wt_s, wt_e = bias_start.T, bias_end.T
    tokens = (2 * N, C)
    wide = (C, 4 * C)

    send, args, parts = call(
        plane_local_kernel,
        [shape((n_dst, 8, C), BF16), shape((8, C)), shape((32, C), BF16)],
        [pltpu.VMEM(tokens, BF16), (1, C), (HEADS, C), (1, C), (HEADS, C), (1, C),
         pltpu.VMEM((1, C), jnp.int32), (8, C), (16, C), pltpu.SemaphoreType.DMA((7,))],
        x, g_s, wt_s, g_e, wt_e, g_t, residue_mask,
        in_hbm=range(7),
    )
    recv = swap(send)
    qkv, gating, score, n, cot, wo = call(
        start_scores_kernel,
        [shape((2 * N, 3 * C), BF16), shape(tokens), shape((2 * N, HEADS * N)), shape(tokens, BF16),
         shape(tokens, BF16), shape((C, C))],
        [pltpu.SemaphoreType.DMA((2,))],
        x, cot, args, proj_start, output_start,
        in_hbm=(1, 4),
    )
    send, mix, prob, first = call(
        start_forward_kernel,
        [shape((n_dst, 16, C), BF16), shape(tokens), shape((2 * N, HEADS * N)), shape(tokens, BF16)],
        [(n_dst * 8, C), (HEADS * N, N), (n_dst * 16, C), (8, C)],
        recv, x, cot, args, parts, qkv, gating, score, wo,
    )
    recv = swap(send)
    n_dp = lax.axis_size("dp")
    to_core = [(i, i ^ 1) for i in range(n_dp)]
    half = (n_dst * HALF, C)
    hidden = (2 * N, 4 * C)
    send, small, *saved = call(
        end_kernel,
        [shape((n_dst, 16, C), BF16), shape((8, C)), shape(hidden, BF16), shape(hidden, BF16), shape(tokens, BF16),
         shape(tokens, BF16), shape(tokens, BF16), shape(hidden, BF16), shape(tokens, BF16), shape(tokens, BF16)],
        [(n_dst * 16, C), tokens, tokens, (HEADS * N, N), (n_dst * 16, C)],
        recv, args, proj_end, output_end, transition_up, transition_down,
    )
    recv = swap(send)
    keep, give = call(
        end_weights_kernel,
        [shape(half), shape(half, BF16)],
        [(4 * C, C), (C, C), (n_dst * 2 * HALF, C)],
        *saved,
    )
    got = lax.ppermute(give, "dp", to_core)
    send, dfirst, dproj = call(
        start_backward_kernel,
        [shape((n_dst, 32, C), BF16), shape(tokens, BF16), shape(hidden, BF16)],
        [(n_dst * 16, C), tokens, (HEADS * N, N), (C, C), (n_dst * 32, C), half, (16, C)],
        recv, keep, got, small, n, first, qkv, gating, mix, prob, args, parts, wo,
    )
    recv = swap(send)
    dn, dn_plane, part = call(
        start_plane_kernel,
        [shape(tokens, BF16), shape(tokens, BF16), shape((32, C))],
        [(16, C)],
        recv, dproj, x, proj_start, args, parts,
    )
    others = [lax.ppermute(part, "dp", [(i, i ^ d) for i in range(n_dp)]) for d in range(1, n_dp)]
    grad = call(grad_kernel, shape(tokens, BF16), [], dn, dn_plane, dfirst, x, args)
    grad, *others = lax.optimization_barrier((grad, *others))
    send = call(spread_kernel, shape((n_dst, 24, C), BF16), [(24, C)], part, *others)
    recv = swap(send)
    other = lax.ppermute(recv, "dp", to_core)
    factor = 1.0 / (n_dp * N)
    vector, bias, square, tall = (1, C), (HEADS, C), (C, C), (4 * C, C)
    sizes = [vector, wide, bias, square, vector, wide, bias, square, vector, wide, tall]
    gs, ps, bs, os, ge, pe, be, oe, gt, up, down = call(
        functools.partial(finish_kernel, factor),
        [shape(size) for size in sizes],
        [*sizes, (n_dst * 48, C), square, pltpu.SemaphoreType.DMA((len(sizes),))],
        recv, other,
        out=pltpu.HBM,
    )
    return (
        grad.reshape(1, 2, N, C), gs.reshape(C), ps, bs.T, os, ge.reshape(C), pe, be.T, oe, gt.reshape(C), up, down,
    )


def solution(mesh):
    rows = P("dp", "dap", None, None)
    in_specs = (rows, rows, P("dp", None)) + (P(),) * 11
    out_specs = (rows,) + (P(),) * 11
    return jax.shard_map(local, mesh=mesh, in_specs=in_specs, out_specs=out_specs, check_vma=False)
```

```python
import functools

import jax
import jax.numpy as jnp
from jax import lax
from jax.experimental import pallas as pl
from jax.experimental.pallas import tpu as pltpu
from jax.sharding import PartitionSpec as P

HEADS = 4
EPS = 1e-05
F32 = jnp.float32
BF16 = jnp.bfloat16
C = 128
HALF = 13
VMEM_LIMIT = 48 * 1024 * 1024


def dot(a, b, contract=((1,), (0,))):
    return lax.dot_general(a, b, (contract, ((), ())), preferred_element_type=F32)


NN = ((1,), (0,))
NT = ((1,), (1,))
TN = ((0,), (0,))


def ln_stats(x):
    centre = x - jnp.mean(x, -1, keepdims=True)
    spread = jnp.mean(centre * centre, -1, keepdims=True)
    rstd = lax.rsqrt(spread + EPS)
    return centre * rstd, rstd


def ln_back(dn, xhat, rstd, gain):
    t = dn * gain
    m1 = jnp.mean(t, -1, keepdims=True)
    m2 = jnp.mean(t * xhat, -1, keepdims=True)
    dx = rstd * (t - m1 - xhat * m2)
    return dx.astype(BF16).astype(F32), jnp.sum(dn * xhat, 0, keepdims=True)


def head_masks(dtype):
    lane = lax.broadcasted_iota(jnp.int32, (1, C), 1)
    size = C // HEADS
    return [((lane >= h * size) & (lane < (h + 1) * size)).astype(dtype) for h in range(HEADS)]


def stack_heads(a, masks):
    return jnp.concatenate([a * m for m in masks], 0)


def unstack_heads(a, masks):
    n = a.shape[0] // HEADS
    total = a[:n] * masks[0]
    for h in range(1, HEADS):
        total = total + a[h * n : (h + 1) * n] * masks[h]
    return total


def interleave(chains):
    done = object()
    while chains:
        chains = [chain for chain in chains if next(chain, done) is not done]


def project(n, w):
    proj = dot(n, w)
    scale = (C // HEADS) ** (-0.5)
    q = (proj[:, :C] * scale).astype(BF16)
    k = proj[:, C : 2 * C].astype(BF16)
    v = proj[:, 2 * C : 3 * C].astype(BF16)
    return q, k, v, jax.nn.sigmoid(proj[:, 3 * C :])


def split(scr, wt):
    for i in range(3):
        part = wt.astype(BF16).astype(F32)
        scr[i * HEADS : (i + 1) * HEADS, :] = part
        wt = wt - part
    scr[3 * HEADS : 16, :] = jnp.zeros((16 - 3 * HEADS, C), F32)
    return scr[...].astype(BF16)


def plane_of(n, parts):
    out = dot(parts, n, NT)
    return out[0:4] + out[4:8] + out[8:12]


def core_index():
    return lax.rem(lax.axis_index("dp"), 2)


def rows_of(ref, start, count, stride):
    return ref[pl.ds(start, count, stride=stride), :]


WT_S, WT_E = slice(0, 16), slice(16, 32)
G_S, G_E, G_T, KEPT = slice(0, 1), slice(1, 2), slice(2, 3), slice(3, 4)


def plane_local_kernel(
    x_hbm, gs_hbm, wts_hbm, ge_hbm, wte_hbm, gt_hbm, mask_hbm,
    out_ref, args_ref, parts_ref,
    x_ref, gs, wts, ge, wte, gt, mask, small, scr, sems,
):
    n_dst, rows, _ = out_ref.shape
    moves = [(gs_hbm, gs), (wts_hbm, wts), (x_hbm, x_ref), (ge_hbm, ge), (wte_hbm, wte), (gt_hbm, gt), (mask_hbm, mask)]
    copies = [pltpu.make_async_copy(src, dst, sems.at[i]) for i, (src, dst) in enumerate(moves)]
    for copy in copies:
        copy.start()
    for copy in copies:
        copy.wait()
    parts_ref[WT_S, :] = split(scr, wts[...])
    parts_ref[WT_E, :] = split(scr, wte[...])
    args_ref[G_S, :] = gs[...]
    args_ref[G_E, :] = ge[...]
    args_ref[G_T, :] = gt[...]
    args_ref[KEPT, :] = mask[...].astype(F32)
    args_ref[4:8, :] = jnp.zeros((4, C), F32)
    xhat, _ = ln_stats(x_ref[...].astype(F32))
    n = (xhat * gs[...]).astype(BF16)
    plane = plane_of(n, parts_ref[WT_S, :])
    small[0:HEADS, :] = plane[:, :C]
    small[HEADS : 2 * HEADS, :] = plane[:, C:]
    out_ref[...] = jnp.broadcast_to(small[...].astype(BF16)[None], (n_dst, rows, C))


def start_scores_kernel(
    x_ref, cot_hbm, args_ref, w_ref, wo_hbm,
    qkv_ref, gating_ref, score_ref, n_ref, cot_ref, wo_ref,
    sems,
):
    copies = [pltpu.make_async_copy(cot_hbm, cot_ref, sems.at[0]), pltpu.make_async_copy(wo_hbm, wo_ref, sems.at[1])]
    for copy in copies:
        copy.start()
    N = score_ref.shape[1] // HEADS
    masks = head_masks(BF16)
    xhat, _ = ln_stats(x_ref[...].astype(F32))
    n = (xhat * args_ref[G_S, :]).astype(BF16)
    n_ref[...] = n
    q, k, v, gating = project(n, w_ref[...].astype(BF16))
    qkv_ref[:, :C] = q
    qkv_ref[:, C : 2 * C] = k
    qkv_ref[:, 2 * C :] = v
    gating_ref[...] = gating
    for r in range(2):
        part = slice(r * N, (r + 1) * N)
        score_ref[part, :] = dot(q[part], stack_heads(k[part], masks), NT)
    for copy in copies:
        copy.wait()


def start_forward_kernel(
    recv_ref, x_ref, cot_ref, args_ref, parts_ref, qkv_ref, gating_ref, score_ref, wo_ref,
    send_ref, mix_ref, prob_ref, first_ref,
    fscr, plane, sscr, small,
):
    n_dst = recv_ref.shape[0]
    N = 2 * n_dst
    rows = send_ref.shape[1]
    fscr[...] = recv_ref[...].astype(F32).reshape(n_dst * 8, C)
    for r in range(2):
        for h in range(HEADS):
            plane[pl.ds(h * N + r, n_dst, stride=2), :] = rows_of(fscr, r * 4 + h, n_dst, 8)
    masks = head_masks(BF16)
    kept = args_ref[KEPT, :]
    x = x_ref[...].astype(F32)
    v = qkv_ref[:, 2 * C :]
    gating = gating_ref[...]
    wo = wo_ref[...].astype(BF16)
    parts = parts_ref[WT_E, :]

    def chain(r):
        part = slice(r * N, (r + 1) * N)
        probs = []
        for h in range(HEADS):
            w = jnp.exp(score_ref[part, h * N : (h + 1) * N] + plane[h * N : (h + 1) * N, :]) * kept
            probs.append(w * (1.0 / jnp.sum(w, -1, keepdims=True)))
        prob = jnp.concatenate(probs, 1)
        prob_ref[part, :] = prob
        yield
        mix = dot(prob.astype(BF16), stack_heads(v[part], masks))
        mix_ref[part, :] = mix
        yield
        first = (x[part] + dot((gating[part] * mix).astype(BF16), wo)).astype(BF16)
        first_ref[part, :] = first
        yield
        first = first.astype(F32)
        fscr[part, :] = first
        xhat, _ = ln_stats(first)
        yield
        small[r * HEADS : (r + 1) * HEADS, :] = plane_of((xhat * args_ref[G_E, :]).astype(BF16), parts)
        yield
        for a in range(2):
            sscr[pl.ds(r * 2 + a, n_dst, stride=rows), :] = rows_of(fscr, r * N + a, n_dst, 2)

    interleave([chain(r) for r in range(2)])
    fscr[0 : 2 * N, :] = cot_ref[...].astype(F32)
    for r in range(2):
        for a in range(2):
            sscr[pl.ds(4 + r * 2 + a, n_dst, stride=rows), :] = rows_of(fscr, r * N + a, n_dst, 2)
    for i in range(8):
        sscr[pl.ds(8 + i, n_dst, stride=rows), :] = jnp.broadcast_to(small[i : i + 1, :], (n_dst, C))
    send_ref[...] = sscr[...].reshape(n_dst, rows, C).astype(BF16)


def put_wide(scr, src, value, starts, n_dst, rows):
    for t in range(4):
        src[t * C : (t + 1) * C, :] = value[:, t * C : (t + 1) * C]
        for i in range(2):
            scr[pl.ds(starts[i] + t, n_dst, stride=rows), :] = rows_of(src, t * C + i, n_dst, 2)


def put_narrow(scr, src, row, n_dst, rows, each):
    for i in range(each):
        scr[pl.ds(row + i, n_dst, stride=rows), :] = rows_of(src, i, n_dst, each)


def put_small(scr, row, values, n_dst, rows):
    scr[pl.ds(row, n_dst, stride=rows), :] = jnp.zeros((n_dst, C), F32)
    for e, value in enumerate(values):
        scr[e * rows + row : e * rows + row + 1, :] = value


def end_kernel(
    recv_ref, args_ref, w_ref, wo_ref, wu_ref, wd_ref,
    send_ref, small_ref, hidden_ref, dup_ref, n_ref, n2_ref, cot_ref, dproj_ref, gated_ref, dsecond_ref,
    fscr, zscr, cscr, plane, sscr,
):
    n_dst, in_rows, _ = recv_ref.shape
    N = 2 * n_dst
    rows = send_ref.shape[1]
    fscr[...] = recv_ref[...].astype(F32).reshape(n_dst * in_rows, C)
    for r in range(2):
        for a in range(2):
            zscr[pl.ds(a * N + r, n_dst, stride=2), :] = rows_of(fscr, r * 2 + a, n_dst, in_rows)
            cscr[pl.ds(a * N + r, n_dst, stride=2), :] = rows_of(fscr, 4 + r * 2 + a, n_dst, in_rows)
        for h in range(HEADS):
            plane[pl.ds(h * N + r, n_dst, stride=2), :] = rows_of(fscr, 8 + r * 4 + h, n_dst, in_rows)
    masks = head_masks(BF16)
    masks_f = head_masks(F32)
    gain, gain_t = args_ref[G_E, :], args_ref[G_T, :]
    length = jnp.sum(args_ref[KEPT, :], -1, keepdims=True)
    kept = (lax.broadcasted_iota(jnp.int32, (N, 1), 0).astype(F32) < length).astype(F32)
    w = w_ref[...].astype(BF16)
    wo = wo_ref[...].astype(BF16)
    wu = wu_ref[...].astype(BF16)
    wd = wd_ref[...].astype(BF16)
    results = {}

    def chain(a):
        part = slice(a * N, (a + 1) * N)
        x = zscr[part, :]
        cot = cscr[part, :]
        cot_b = cot.astype(BF16)
        cot_ref[part, :] = cot_b
        xhat, rstd = ln_stats(x)
        n = (xhat * gain).astype(BF16)
        n_ref[part, :] = n
        yield
        q, k, v, gating = project(n, w)
        yield
        ks = stack_heads(k, masks)
        vs = stack_heads(v, masks)
        s = dot(ks, q, NT) + plane[...]
        yield
        probs = []
        for h in range(HEADS):
            e = jnp.exp(s[h * N : (h + 1) * N]) * kept
            probs.append(e * (1.0 / jnp.sum(e, 0, keepdims=True)))
        prob = jnp.concatenate(probs, 0)
        prob_b = prob.astype(BF16)
        yield
        mix = dot(prob_b, vs, TN)
        yield
        gated = (gating * mix).astype(BF16)
        gated_ref[part, :] = gated
        second = (x + dot(gated, wo)).astype(BF16).astype(F32)
        yield
        xhat2, rstd2 = ln_stats(second)
        n2 = (xhat2 * gain_t).astype(BF16)
        n2_ref[part, :] = n2
        dhidden = dot(cot_b, wd, NT).astype(BF16).astype(F32)
        yield
        up = dot(n2, wu)
        yield
        cdf = 0.5 * (1.0 + lax.erf(up * (0.5**0.5)))
        slope = cdf + up * (jnp.exp(-0.5 * up * up) * 0.3989422804014327)
        dup = (dhidden * slope).astype(BF16)
        hidden_ref[part, :] = (up * cdf).astype(BF16)
        dup_ref[part, :] = dup
        yield
        dn2 = dot(dup, wu, NT).astype(BF16).astype(F32)
        yield
        dx2, dgain_t = ln_back(dn2, xhat2, rstd2, gain_t)
        dsecond = (cot + dx2).astype(BF16)
        dsecond_ref[part, :] = dsecond
        yield
        dgated = dot(dsecond, wo, NT).astype(BF16).astype(F32)
        yield
        dmix = (dgated * gating).astype(BF16)
        dprob = dot(vs, dmix, NT).astype(BF16).astype(F32)
        yield
        ds = []
        for h in range(HEADS):
            p = prob[h * N : (h + 1) * N]
            d = dprob[h * N : (h + 1) * N]
            ds.append(p * (d - jnp.sum(p * d, 0, keepdims=True)))
        ds = jnp.concatenate(ds, 0)
        dv = unstack_heads(dot(prob_b, dmix), masks_f)
        yield
        ds_b = ds.astype(BF16)
        dq = dot(ds_b, ks, TN)
        dk = unstack_heads(dot(ds_b, q), masks_f)
        yield
        dproj = project_cotangent(dq, dk, dv, gating, dgated * mix)
        dproj_ref[part, :] = dproj
        dn = dot(dproj, w, NT).astype(BF16).astype(F32)
        yield
        dx, dgain = ln_back(dn, xhat, rstd, gain)
        zscr[part, :] = dsecond.astype(F32) + dx
        results[a] = ds, dgain_t, dgain

    interleave([chain(a) for a in range(2)])
    (ds, dgain_t, dgain), (ds_b, dgain_t_b, dgain_b) = results[0], results[1]
    plane[...] = ds + ds_b
    for r in range(2):
        for h in range(HEADS):
            sscr[pl.ds(r * 4 + h, n_dst, stride=rows), :] = rows_of(plane, h * N + r, n_dst, 2)
        for a in range(2):
            sscr[pl.ds(8 + r * 2 + a, n_dst, stride=rows), :] = rows_of(zscr, a * N + r, n_dst, 2)
    for i in range(12, rows):
        sscr[pl.ds(i, n_dst, stride=rows), :] = jnp.zeros((n_dst, C), F32)
    send_ref[...] = sscr[...].reshape(n_dst, rows, C).astype(BF16)
    small_ref[0:1, :] = dgain_t + dgain_t_b
    small_ref[1:2, :] = dgain + dgain_b
    small_ref[2:8, :] = jnp.zeros((6, C), F32)


def end_weights_kernel(
    hidden_ref, dup_ref, n_ref, n2_ref, cot_ref, dproj_ref, gated_ref, dsecond_ref,
    keep_ref, give_ref,
    down, up, proj, narrow, wscr,
):
    half = keep_ref.shape[0]
    n_dst = half // HALF
    down[...] = dot(hidden_ref[...], cot_ref[...], TN)
    put_narrow(wscr, down, half + 4, n_dst, HALF, 8)
    put_wide(wscr, up, dot(n2_ref[...], dup_ref[...], TN), (8, half), n_dst, HALF)
    put_wide(wscr, proj, dot(n_ref[...], dproj_ref[...], TN), (0, 4), n_dst, HALF)
    narrow[...] = dot(gated_ref[...], dsecond_ref[...], TN)
    for i in range(2):
        wscr[pl.ds(i * half + 12, n_dst, stride=HALF), :] = rows_of(narrow, i, n_dst, 2)
    core = core_index()
    keep_ref[...] = wscr[pl.ds(pl.multiple_of(core * half, 8), half), :]
    give_ref[...] = wscr[pl.ds(pl.multiple_of((1 - core) * half, 8), half), :].astype(BF16)


def project_cotangent(dq, dk, dv, gating, dgating):
    dq = dq.astype(BF16).astype(F32) * (C // HEADS) ** (-0.5)
    dg = dgating * gating * (1.0 - gating)
    return jnp.concatenate([dq.astype(BF16), dk.astype(BF16), dv.astype(BF16), dg.astype(BF16)], 1)


def plane_back(plane, n, p_ref, parts):
    p_ref[...] = jnp.zeros_like(p_ref)
    for i in range(3):
        p_ref[i * HEADS : (i + 1) * HEADS, :] = plane
    p = p_ref[...].astype(BF16)
    return dot(p, parts, TN).astype(BF16).astype(F32), dot(p, n)[0:HEADS]


def start_backward_kernel(
    recv_ref, keep_ref, got_ref, small_ref, n_ref, first_ref, qkv_ref, gating_ref, mix_ref, prob_ref, args_ref, parts_ref, wo_ref,
    send_ref, dfirst_ref, dproj_ref,
    fscr, gscr, plane, narrow, wide, sscr, wscr, p_ref,
):
    n_dst, in_rows, _ = recv_ref.shape
    N = 2 * n_dst
    rows = send_ref.shape[1]
    recv = recv_ref[...].astype(F32)
    total = jnp.sum(recv, 0)
    fscr[...] = recv.reshape(n_dst * in_rows, C)
    for r in range(2):
        for a in range(2):
            gscr[pl.ds(r * N + a, n_dst, stride=2), :] = rows_of(fscr, 8 + r * 2 + a, n_dst, in_rows)
    masks = head_masks(BF16)
    masks_f = head_masks(F32)
    gain_e = args_ref[G_E, :]
    parts = parts_ref[WT_E, :]
    wo = wo_ref[...].astype(BF16)
    results = {}

    def chain(r):
        part = slice(r * N, (r + 1) * N)
        xhat, rstd = ln_stats(first_ref[part, :].astype(F32))
        n_e = (xhat * gain_e).astype(BF16)
        yield
        dn_e, dbias_e = plane_back(total[r * HEADS : (r + 1) * HEADS], n_e, p_ref.at[r], parts)
        yield
        dxe, dgain_e = ln_back(dn_e, xhat, rstd, gain_e)
        dfirst = (gscr[part, :] + dxe).astype(BF16)
        dfirst_ref[part, :] = dfirst
        yield
        q = qkv_ref[part, :C]
        ks = stack_heads(qkv_ref[part, C : 2 * C], masks)
        vs = stack_heads(qkv_ref[part, 2 * C :], masks)
        gating = gating_ref[part, :]
        mix = mix_ref[part, :]
        prob = prob_ref[part, :]
        dgated = dot(dfirst, wo, NT).astype(BF16).astype(F32)
        yield
        dmix = (dgated * gating).astype(BF16)
        dprob = dot(dmix, vs, NT).astype(BF16).astype(F32)
        yield
        ds = []
        for h in range(HEADS):
            p = prob[:, h * N : (h + 1) * N]
            d = dprob[:, h * N : (h + 1) * N]
            ds.append(p * (d - jnp.sum(p * d, -1, keepdims=True)))
        dv = unstack_heads(dot(prob.astype(BF16), dmix, TN), masks_f)
        yield
        ds_b = jnp.concatenate(ds, 1).astype(BF16)
        dq = dot(ds_b, ks)
        dk = unstack_heads(dot(ds_b, q, TN), masks_f)
        yield
        dproj_ref[part, :] = project_cotangent(dq, dk, dv, gating, dgated * mix)
        results[r] = ds, dgain_e, dbias_e

    interleave([chain(r) for r in range(2)])
    (ds, dgain_e, dbias_e), (ds_b, dgain_b, dbias_b) = results[0], results[1]
    dgain_e, dbias_e = dgain_e + dgain_b, dbias_e + dbias_b
    for h in range(HEADS):
        plane[h * N : (h + 1) * N, :] = ds[h] + ds_b[h]
    for r in range(2):
        for h in range(HEADS):
            sscr[pl.ds(r * 4 + h, n_dst, stride=rows), :] = rows_of(plane, h * N + r, n_dst, 2)
    gated = (gating_ref[...] * mix_ref[...]).astype(BF16)
    narrow[0:C, :] = dot(gated, dfirst_ref[...], TN)
    put_narrow(sscr, narrow, 16, n_dst, rows, 2)
    put_wide(sscr, wide, dot(n_ref[...], dproj_ref[...], TN), (8, 12), n_dst, rows)
    smalls = [small_ref[0:1, :], small_ref[1:2, :], dgain_e] + [dbias_e[h : h + 1] for h in range(HEADS)]
    put_small(sscr, 18, smalls, n_dst, rows)
    wscr[...] = keep_ref[...] + got_ref[...].astype(F32)
    for i in range(HALF):
        sscr[pl.ds(19 + i, n_dst, stride=rows), :] = rows_of(wscr, i, n_dst, HALF)
    send_ref[...] = sscr[...].reshape(n_dst, rows, C).astype(BF16)


def start_plane_kernel(recv_ref, dproj_ref, x_ref, w_ref, args_ref, parts_ref, dn_ref, dn_plane_ref, part_ref, p_ref):
    total = jnp.sum(recv_ref[...].astype(F32), 0)
    xhat, _ = ln_stats(x_ref[...].astype(F32))
    n = (xhat * args_ref[G_S, :]).astype(BF16)
    dn = dot(dproj_ref[...], w_ref[...].astype(BF16), NT).astype(BF16)
    dn_ref[...] = dn
    N = n.shape[0] // 2
    backs = [
        plane_back(total[r * HEADS : (r + 1) * HEADS], n[r * N : (r + 1) * N], p_ref.at[r], parts_ref[WT_S, :])
        for r in range(2)
    ]
    dn_plane = jnp.concatenate([back[0] for back in backs], 0)
    dbias = backs[0][1] + backs[1][1]
    dn_plane_ref[...] = dn_plane.astype(BF16)
    part_ref[0:11, :] = total[8:19]
    part_ref[11:15, :] = dbias
    part_ref[15:16, :] = jnp.sum((dn_plane + dn.astype(F32)) * xhat, 0, keepdims=True)
    part_ref[16 : 16 + HALF, :] = total[19 : 19 + HALF]
    part_ref[16 + HALF : 32, :] = jnp.zeros((16 - HALF, C), F32)


def grad_kernel(dn_ref, dn_plane_ref, dfirst_ref, x_ref, args_ref, grad_ref):
    xhat, rstd = ln_stats(x_ref[...].astype(F32))
    dx, _ = ln_back(dn_ref[...].astype(F32), xhat, rstd, args_ref[G_S, :])
    dx_plane, _ = ln_back(dn_plane_ref[...].astype(F32), xhat, rstd, args_ref[G_S, :])
    grad_ref[...] = (dfirst_ref[...].astype(F32) + dx + dx_plane).astype(BF16)


def spread_kernel(a_ref, b_ref, c_ref, d_ref, out_ref, scr):
    near = a_ref[...] + c_ref[...]
    total = near + (b_ref[...] + d_ref[...])
    scr[0:8, :] = jnp.where(core_index() == 0, total[0:8], total[8:16])
    scr[8:24, :] = near[16:32]
    out_ref[...] = jnp.broadcast_to(scr[...].astype(BF16)[None], out_ref.shape)


def finish_kernel(
    factor, recv_ref, other_ref,
    gs_out, ps_out, bs_out, os_out, ge_out, pe_out, be_out, oe_out, gt_out, up_out, down_out,
    gs_ref, ps_ref, bs_ref, os_ref, ge_ref, pe_ref, be_ref, oe_ref, gt_ref, up_ref, down_ref,
    fscr, block, sems,
):
    copies = []

    def leave(ref, out):
        copies.append(pltpu.make_async_copy(ref, out, sems.at[len(copies)]))
        copies[-1].start()

    n_dst, half, _ = recv_ref.shape
    size = n_dst * half
    core = core_index()
    for index, ref in ((core, recv_ref), (1 - core, other_ref)):
        fscr[pl.ds(pl.multiple_of(index * size, 8), size), :] = ref[...].astype(F32).reshape(size, C) * factor

    def rows(row):
        return rows_of(fscr, row, n_dst, half)

    def wide(ref, starts):
        for t in range(4):
            for i in range(2):
                block[pl.ds(i, n_dst, stride=2), :] = rows(starts[i] + t)
            ref[:, t * C : (t + 1) * C] = block[...]

    def narrow(ref, starts):
        for i, start in enumerate(starts):
            ref[pl.ds(i, n_dst, stride=len(starts)), :] = rows(start)

    def one(e, row):
        start = e * half + row
        return fscr[start : start + 1, :]

    wide(ps_ref, (0, 4))
    leave(ps_ref, ps_out)
    wide(pe_ref, (8, 12))
    leave(pe_ref, pe_out)
    wide(up_ref, (16, size + 8))
    leave(up_ref, up_out)
    narrow(down_ref, range(size + 12, size + 20))
    leave(down_ref, down_out)
    narrow(os_ref, (size, size + 1))
    leave(os_ref, os_out)
    narrow(oe_ref, (20, size + 20))
    leave(oe_ref, oe_out)
    for h in range(HEADS):
        bs_ref[h : h + 1, :] = jnp.sum(rows(size + 3 + h), 0, keepdims=True)
        be_ref[h : h + 1, :] = one(3 + h, size + 2)
    gt_ref[...] = one(0, size + 2)
    ge_ref[...] = one(1, size + 2) + one(2, size + 2)
    gs_ref[...] = jnp.sum(rows(size + 7), 0, keepdims=True)
    for ref, out in ((bs_ref, bs_out), (be_ref, be_out), (gt_ref, gt_out), (ge_ref, ge_out), (gs_ref, gs_out)):
        leave(ref, out)
    for copy in copies:
        copy.wait()


def shape(dims, dtype=F32):
    return jax.ShapeDtypeStruct(dims, dtype)


def call(body, out_shape, scratch, *operands, in_hbm=(), out=pltpu.VMEM):
    many = isinstance(out_shape, (list, tuple))
    whole = pl.BlockSpec(memory_space=out)
    spaces = [pltpu.HBM if i in in_hbm else pltpu.VMEM for i in range(len(operands))]
    operands = [pltpu.with_memory_space_constraint(a, m) if m is pltpu.HBM else a for a, m in zip(operands, spaces)]
    return pl.pallas_call(
        body,
        out_shape=out_shape,
        in_specs=[pl.BlockSpec(memory_space=m) for m in spaces],
        out_specs=[whole] * len(out_shape) if many else whole,
        scratch_shapes=[pltpu.VMEM(s, F32) if isinstance(s, tuple) else s for s in scratch],
        compiler_params=pltpu.CompilerParams(vmem_limit_bytes=VMEM_LIMIT),
    )(*operands)


def swap(buffer):
    return lax.all_to_all(buffer, "dap", split_axis=0, concat_axis=0, tiled=True)


def local(
    pair_input, cotangent, residue_mask, gain_start, proj_start, bias_start, output_start,
    gain_end, proj_end, bias_end, output_end, gain_transition, transition_up, transition_down,
):
    _, _, N, _ = pair_input.shape
    n_dst = N // 2
    x = pair_input.reshape(2 * N, C)
    cot = cotangent.reshape(2 * N, C)
    g_s, g_e, g_t = (g.reshape(1, C) for g in (gain_start, gain_end, gain_transition))
    wt_s, wt_e = bias_start.T, bias_end.T
    tokens = (2 * N, C)
    wide = (C, 4 * C)

    send, args, parts = call(
        plane_local_kernel,
        [shape((n_dst, 8, C), BF16), shape((8, C)), shape((32, C), BF16)],
        [pltpu.VMEM(tokens, BF16), (1, C), (HEADS, C), (1, C), (HEADS, C), (1, C),
         pltpu.VMEM((1, C), jnp.int32), (8, C), (16, C), pltpu.SemaphoreType.DMA((7,))],
        x, g_s, wt_s, g_e, wt_e, g_t, residue_mask,
        in_hbm=range(7),
    )
    recv = swap(send)
    qkv, gating, score, n, cot, wo = call(
        start_scores_kernel,
        [shape((2 * N, 3 * C), BF16), shape(tokens), shape((2 * N, HEADS * N)), shape(tokens, BF16),
         shape(tokens, BF16), shape((C, C))],
        [pltpu.SemaphoreType.DMA((2,))],
        x, cot, args, proj_start, output_start,
        in_hbm=(1, 4),
    )
    send, mix, prob, first = call(
        start_forward_kernel,
        [shape((n_dst, 16, C), BF16), shape(tokens), shape((2 * N, HEADS * N)), shape(tokens, BF16)],
        [(n_dst * 8, C), (HEADS * N, N), (n_dst * 16, C), (8, C)],
        recv, x, cot, args, parts, qkv, gating, score, wo,
    )
    recv = swap(send)
    n_dp = lax.axis_size("dp")
    to_core = [(i, i ^ 1) for i in range(n_dp)]
    half = (n_dst * HALF, C)
    hidden = (2 * N, 4 * C)
    send, small, *saved = call(
        end_kernel,
        [shape((n_dst, 16, C), BF16), shape((8, C)), shape(hidden, BF16), shape(hidden, BF16), shape(tokens, BF16),
         shape(tokens, BF16), shape(tokens, BF16), shape(hidden, BF16), shape(tokens, BF16), shape(tokens, BF16)],
        [(n_dst * 16, C), tokens, tokens, (HEADS * N, N), (n_dst * 16, C)],
        recv, args, proj_end, output_end, transition_up, transition_down,
    )
    recv = swap(send)
    keep, give = call(
        end_weights_kernel,
        [shape(half), shape(half, BF16)],
        [(4 * C, C), (4 * C, C), (4 * C, C), (C, C), (n_dst * 2 * HALF, C)],
        *saved,
    )
    got = lax.ppermute(give, "dp", to_core)
    send, dfirst, dproj = call(
        start_backward_kernel,
        [shape((n_dst, 32, C), BF16), shape(tokens, BF16), shape(hidden, BF16)],
        [(n_dst * 16, C), tokens, (HEADS * N, N), (C, C), (4 * C, C), (n_dst * 32, C), half, (2, 16, C)],
        recv, keep, got, small, n, first, qkv, gating, mix, prob, args, parts, wo,
    )
    recv = swap(send)
    dn, dn_plane, part = call(
        start_plane_kernel,
        [shape(tokens, BF16), shape(tokens, BF16), shape((32, C))],
        [(2, 16, C)],
        recv, dproj, x, proj_start, args, parts,
    )
    others = [lax.ppermute(part, "dp", [(i, i ^ d) for i in range(n_dp)]) for d in range(1, n_dp)]
    grad = call(grad_kernel, shape(tokens, BF16), [], dn, dn_plane, dfirst, x, args)
    grad, *others = lax.optimization_barrier((grad, *others))
    send = call(spread_kernel, shape((n_dst, 24, C), BF16), [(24, C)], part, *others)
    recv = swap(send)
    other = lax.ppermute(recv, "dp", to_core)
    factor = 1.0 / (n_dp * N)
    vector, bias, square, tall = (1, C), (HEADS, C), (C, C), (4 * C, C)
    sizes = [vector, wide, bias, square, vector, wide, bias, square, vector, wide, tall]
    gs, ps, bs, os, ge, pe, be, oe, gt, up, down = call(
        functools.partial(finish_kernel, factor),
        [shape(size) for size in sizes],
        [*sizes, (n_dst * 48, C), square, pltpu.SemaphoreType.DMA((len(sizes),))],
        recv, other,
        out=pltpu.HBM,
    )
    return (
        grad.reshape(1, 2, N, C), gs.reshape(C), ps, bs.T, os, ge.reshape(C), pe, be.T, oe, gt.reshape(C), up, down,
    )


def solution(mesh):
    rows = P("dp", "dap", None, None)
    in_specs = (rows, rows, P("dp", None)) + (P(),) * 11
    out_specs = (rows,) + (P(),) * 11
    return jax.shard_map(local, mesh=mesh, in_specs=in_specs, out_specs=out_specs, check_vma=False)
```

```python
import functools

import jax
import jax.numpy as jnp
from jax import lax
from jax.experimental import pallas as pl
from jax.experimental.pallas import tpu as pltpu
from jax.sharding import PartitionSpec as P

HEADS = 4
EPS = 1e-05
F32 = jnp.float32
BF16 = jnp.bfloat16
C = 128
HALF = 13
VMEM_LIMIT = 48 * 1024 * 1024


def dot(a, b, contract=((1,), (0,))):
    return lax.dot_general(a, b, (contract, ((), ())), preferred_element_type=F32)


NN = ((1,), (0,))
NT = ((1,), (1,))
TN = ((0,), (0,))


def ln_stats(x):
    centre = x - jnp.mean(x, -1, keepdims=True)
    spread = jnp.mean(centre * centre, -1, keepdims=True)
    rstd = lax.rsqrt(spread + EPS)
    return centre * rstd, rstd


def ln_back(dn, xhat, rstd, gain):
    t = dn * gain
    m1 = jnp.mean(t, -1, keepdims=True)
    m2 = jnp.mean(t * xhat, -1, keepdims=True)
    dx = rstd * (t - m1 - xhat * m2)
    return dx.astype(BF16).astype(F32), jnp.sum(dn * xhat, 0, keepdims=True)


def head_masks(dtype):
    lane = lax.broadcasted_iota(jnp.int32, (1, C), 1)
    size = C // HEADS
    return [((lane >= h * size) & (lane < (h + 1) * size)).astype(dtype) for h in range(HEADS)]


def stack_heads(a, masks):
    return jnp.concatenate([a * m for m in masks], 0)


def unstack_heads(a, masks):
    n = a.shape[0] // HEADS
    total = a[:n] * masks[0]
    for h in range(1, HEADS):
        total = total + a[h * n : (h + 1) * n] * masks[h]
    return total


def interleave(chains):
    done = object()
    while chains:
        chains = [chain for chain in chains if next(chain, done) is not done]


def project(n, w):
    proj = dot(n, w)
    scale = (C // HEADS) ** (-0.5)
    q = (proj[:, :C] * scale).astype(BF16)
    k = proj[:, C : 2 * C].astype(BF16)
    v = proj[:, 2 * C : 3 * C].astype(BF16)
    return q, k, v, jax.nn.sigmoid(proj[:, 3 * C :])


def split(scr, wt):
    for i in range(3):
        part = wt.astype(BF16).astype(F32)
        scr[i * HEADS : (i + 1) * HEADS, :] = part
        wt = wt - part
    scr[3 * HEADS : 16, :] = jnp.zeros((16 - 3 * HEADS, C), F32)
    return scr[...].astype(BF16)


def plane_of(n, parts):
    out = dot(parts, n, NT)
    return out[0:4] + out[4:8] + out[8:12]


def core_index():
    return lax.rem(lax.axis_index("dp"), 2)


def rows_of(ref, start, count, stride):
    return ref[pl.ds(start, count, stride=stride), :]


WT_S, WT_E = slice(0, 16), slice(16, 32)
G_S, G_E, G_T, KEPT = slice(0, 1), slice(1, 2), slice(2, 3), slice(3, 4)


def plane_local_kernel(
    x_hbm, gs_hbm, wts_hbm, ge_hbm, wte_hbm, gt_hbm, mask_hbm,
    out_ref, args_ref, parts_ref,
    x_ref, gs, wts, ge, wte, gt, mask, small, scr, sems,
):
    n_dst, rows, _ = out_ref.shape
    moves = [(gs_hbm, gs), (wts_hbm, wts), (x_hbm, x_ref), (ge_hbm, ge), (wte_hbm, wte), (gt_hbm, gt), (mask_hbm, mask)]
    copies = [pltpu.make_async_copy(src, dst, sems.at[i]) for i, (src, dst) in enumerate(moves)]
    for copy in copies:
        copy.start()
    for copy in copies:
        copy.wait()
    parts_ref[WT_S, :] = split(scr, wts[...])
    parts_ref[WT_E, :] = split(scr, wte[...])
    args_ref[G_S, :] = gs[...]
    args_ref[G_E, :] = ge[...]
    args_ref[G_T, :] = gt[...]
    args_ref[KEPT, :] = mask[...].astype(F32)
    args_ref[4:8, :] = jnp.zeros((4, C), F32)
    xhat, _ = ln_stats(x_ref[...].astype(F32))
    n = (xhat * gs[...]).astype(BF16)
    plane = plane_of(n, parts_ref[WT_S, :])
    small[0:HEADS, :] = plane[:, :C]
    small[HEADS : 2 * HEADS, :] = plane[:, C:]
    out_ref[...] = jnp.broadcast_to(small[...].astype(BF16)[None], (n_dst, rows, C))


def start_scores_kernel(
    x_ref, cot_hbm, args_ref, w_ref, wo_hbm,
    qkv_ref, gating_ref, score_ref, n_ref, cot_ref, wo_ref,
    sems,
):
    copies = [pltpu.make_async_copy(cot_hbm, cot_ref, sems.at[0]), pltpu.make_async_copy(wo_hbm, wo_ref, sems.at[1])]
    for copy in copies:
        copy.start()
    N = score_ref.shape[1] // HEADS
    masks = head_masks(BF16)
    xhat, _ = ln_stats(x_ref[...].astype(F32))
    n = (xhat * args_ref[G_S, :]).astype(BF16)
    n_ref[...] = n
    q, k, v, gating = project(n, w_ref[...].astype(BF16))
    qkv_ref[:, :C] = q
    qkv_ref[:, C : 2 * C] = k
    qkv_ref[:, 2 * C :] = v
    gating_ref[...] = gating
    for r in range(2):
        part = slice(r * N, (r + 1) * N)
        score_ref[part, :] = dot(q[part], stack_heads(k[part], masks), NT)
    for copy in copies:
        copy.wait()


def start_forward_kernel(
    recv_ref, x_ref, cot_ref, args_ref, parts_ref, qkv_ref, gating_ref, score_ref, wo_ref,
    send_ref, mix_ref, prob_ref, first_ref,
    fscr, plane, sscr, small,
):
    n_dst = recv_ref.shape[0]
    N = 2 * n_dst
    rows = send_ref.shape[1]
    fscr[...] = recv_ref[...].astype(F32).reshape(n_dst * 8, C)
    for r in range(2):
        for h in range(HEADS):
            plane[pl.ds(h * N + r, n_dst, stride=2), :] = rows_of(fscr, r * 4 + h, n_dst, 8)
    masks = head_masks(BF16)
    kept = args_ref[KEPT, :]
    x = x_ref[...].astype(F32)
    v = qkv_ref[:, 2 * C :]
    gating = gating_ref[...]
    wo = wo_ref[...].astype(BF16)
    parts = parts_ref[WT_E, :]

    def chain(r):
        part = slice(r * N, (r + 1) * N)
        probs = []
        for h in range(HEADS):
            w = jnp.exp(score_ref[part, h * N : (h + 1) * N] + plane[h * N : (h + 1) * N, :]) * kept
            probs.append(w * (1.0 / jnp.sum(w, -1, keepdims=True)))
        prob = jnp.concatenate(probs, 1)
        prob_ref[part, :] = prob
        yield
        mix = dot(prob.astype(BF16), stack_heads(v[part], masks))
        mix_ref[part, :] = mix
        yield
        first = (x[part] + dot((gating[part] * mix).astype(BF16), wo)).astype(BF16)
        first_ref[part, :] = first
        yield
        first = first.astype(F32)
        fscr[part, :] = first
        xhat, _ = ln_stats(first)
        yield
        small[r * HEADS : (r + 1) * HEADS, :] = plane_of((xhat * args_ref[G_E, :]).astype(BF16), parts)
        yield
        for a in range(2):
            sscr[pl.ds(r * 2 + a, n_dst, stride=rows), :] = rows_of(fscr, r * N + a, n_dst, 2)

    interleave([chain(r) for r in range(2)])
    fscr[0 : 2 * N, :] = cot_ref[...].astype(F32)
    for r in range(2):
        for a in range(2):
            sscr[pl.ds(4 + r * 2 + a, n_dst, stride=rows), :] = rows_of(fscr, r * N + a, n_dst, 2)
    for i in range(8):
        sscr[pl.ds(8 + i, n_dst, stride=rows), :] = jnp.broadcast_to(small[i : i + 1, :], (n_dst, C))
    send_ref[...] = sscr[...].reshape(n_dst, rows, C).astype(BF16)


def put_wide(scr, src, value, starts, n_dst, rows):
    for t in range(4):
        src[t * C : (t + 1) * C, :] = value[:, t * C : (t + 1) * C]
        for i in range(2):
            scr[pl.ds(starts[i] + t, n_dst, stride=rows), :] = rows_of(src, t * C + i, n_dst, 2)


def put_narrow(scr, src, row, n_dst, rows, each):
    for i in range(each):
        scr[pl.ds(row + i, n_dst, stride=rows), :] = rows_of(src, i, n_dst, each)


def put_small(scr, row, values, n_dst, rows):
    scr[pl.ds(row, n_dst, stride=rows), :] = jnp.zeros((n_dst, C), F32)
    for e, value in enumerate(values):
        scr[e * rows + row : e * rows + row + 1, :] = value


def end_kernel(
    recv_ref, args_ref, w_ref, wo_ref, wu_ref, wd_ref,
    send_ref, small_ref, hidden_ref, dup_ref, n_ref, n2_ref, cot_ref, dproj_ref, gated_ref, dsecond_ref,
    fscr, zscr, cscr, plane, sscr,
):
    n_dst, in_rows, _ = recv_ref.shape
    N = 2 * n_dst
    rows = send_ref.shape[1]
    fscr[...] = recv_ref[...].astype(F32).reshape(n_dst * in_rows, C)
    for r in range(2):
        for a in range(2):
            zscr[pl.ds(a * N + r, n_dst, stride=2), :] = rows_of(fscr, r * 2 + a, n_dst, in_rows)
            cscr[pl.ds(a * N + r, n_dst, stride=2), :] = rows_of(fscr, 4 + r * 2 + a, n_dst, in_rows)
        for h in range(HEADS):
            plane[pl.ds(h * N + r, n_dst, stride=2), :] = rows_of(fscr, 8 + r * 4 + h, n_dst, in_rows)
    masks = head_masks(BF16)
    masks_f = head_masks(F32)
    gain, gain_t = args_ref[G_E, :], args_ref[G_T, :]
    length = jnp.sum(args_ref[KEPT, :], -1, keepdims=True)
    kept = (lax.broadcasted_iota(jnp.int32, (N, 1), 0).astype(F32) < length).astype(F32)
    w = w_ref[...].astype(BF16)
    wo = wo_ref[...].astype(BF16)
    wu = wu_ref[...].astype(BF16)
    wd = wd_ref[...].astype(BF16)
    results = {}

    def chain(a):
        part = slice(a * N, (a + 1) * N)
        x = zscr[part, :]
        cot = cscr[part, :]
        cot_b = cot.astype(BF16)
        cot_ref[part, :] = cot_b
        xhat, rstd = ln_stats(x)
        n = (xhat * gain).astype(BF16)
        n_ref[part, :] = n
        yield
        q, k, v, gating = project(n, w)
        yield
        ks = stack_heads(k, masks)
        vs = stack_heads(v, masks)
        s = dot(ks, q, NT) + plane[...]
        yield
        probs = []
        for h in range(HEADS):
            e = jnp.exp(s[h * N : (h + 1) * N]) * kept
            probs.append(e * (1.0 / jnp.sum(e, 0, keepdims=True)))
        prob = jnp.concatenate(probs, 0)
        prob_b = prob.astype(BF16)
        yield
        mix = dot(prob_b, vs, TN)
        yield
        gated = (gating * mix).astype(BF16)
        gated_ref[part, :] = gated
        second = (x + dot(gated, wo)).astype(BF16).astype(F32)
        yield
        xhat2, rstd2 = ln_stats(second)
        n2 = (xhat2 * gain_t).astype(BF16)
        n2_ref[part, :] = n2
        dhidden = dot(cot_b, wd, NT).astype(BF16).astype(F32)
        yield
        up = dot(n2, wu)
        yield
        cdf = 0.5 * (1.0 + lax.erf(up * (0.5**0.5)))
        slope = cdf + up * (jnp.exp(-0.5 * up * up) * 0.3989422804014327)
        dup = (dhidden * slope).astype(BF16)
        hidden_ref[part, :] = (up * cdf).astype(BF16)
        dup_ref[part, :] = dup
        yield
        dn2 = dot(dup, wu, NT).astype(BF16).astype(F32)
        yield
        dx2, dgain_t = ln_back(dn2, xhat2, rstd2, gain_t)
        dsecond = (cot + dx2).astype(BF16)
        dsecond_ref[part, :] = dsecond
        yield
        dgated = dot(dsecond, wo, NT).astype(BF16).astype(F32)
        yield
        dmix = (dgated * gating).astype(BF16)
        dprob = dot(vs, dmix, NT).astype(BF16).astype(F32)
        yield
        ds = []
        for h in range(HEADS):
            p = prob[h * N : (h + 1) * N]
            d = dprob[h * N : (h + 1) * N]
            ds.append(p * (d - jnp.sum(p * d, 0, keepdims=True)))
        ds = jnp.concatenate(ds, 0)
        dv = unstack_heads(dot(prob_b, dmix), masks_f)
        yield
        ds_b = ds.astype(BF16)
        dq = dot(ds_b, ks, TN)
        dk = unstack_heads(dot(ds_b, q), masks_f)
        yield
        dproj = project_cotangent(dq, dk, dv, gating, dgated * mix)
        dproj_ref[part, :] = dproj
        dn = dot(dproj, w, NT).astype(BF16).astype(F32)
        yield
        dx, dgain = ln_back(dn, xhat, rstd, gain)
        zscr[part, :] = dsecond.astype(F32) + dx
        results[a] = ds, dgain_t, dgain

    interleave([chain(a) for a in range(2)])
    (ds, dgain_t, dgain), (ds_b, dgain_t_b, dgain_b) = results[0], results[1]
    plane[...] = ds + ds_b
    for r in range(2):
        for h in range(HEADS):
            sscr[pl.ds(r * 4 + h, n_dst, stride=rows), :] = rows_of(plane, h * N + r, n_dst, 2)
        for a in range(2):
            sscr[pl.ds(8 + r * 2 + a, n_dst, stride=rows), :] = rows_of(zscr, a * N + r, n_dst, 2)
    for i in range(12, rows):
        sscr[pl.ds(i, n_dst, stride=rows), :] = jnp.zeros((n_dst, C), F32)
    send_ref[...] = sscr[...].reshape(n_dst, rows, C).astype(BF16)
    small_ref[0:1, :] = dgain_t + dgain_t_b
    small_ref[1:2, :] = dgain + dgain_b
    small_ref[2:8, :] = jnp.zeros((6, C), F32)


def end_weights_kernel(
    hidden_ref, dup_ref, n_ref, n2_ref, cot_ref, dproj_ref, gated_ref, dsecond_ref,
    keep_ref, give_ref,
    down, up, proj, narrow, wscr,
):
    half = keep_ref.shape[0]
    n_dst = half // HALF
    down[...] = dot(hidden_ref[...], cot_ref[...], TN)
    put_narrow(wscr, down, half + 4, n_dst, HALF, 8)
    put_wide(wscr, up, dot(n2_ref[...], dup_ref[...], TN), (8, half), n_dst, HALF)
    put_wide(wscr, proj, dot(n_ref[...], dproj_ref[...], TN), (0, 4), n_dst, HALF)
    narrow[...] = dot(gated_ref[...], dsecond_ref[...], TN)
    for i in range(2):
        wscr[pl.ds(i * half + 12, n_dst, stride=HALF), :] = rows_of(narrow, i, n_dst, 2)
    core = core_index()
    keep_ref[...] = wscr[pl.ds(pl.multiple_of(core * half, 8), half), :]
    give_ref[...] = wscr[pl.ds(pl.multiple_of((1 - core) * half, 8), half), :].astype(BF16)


def project_cotangent(dq, dk, dv, gating, dgating):
    dq = dq.astype(BF16).astype(F32) * (C // HEADS) ** (-0.5)
    dg = dgating * gating * (1.0 - gating)
    return jnp.concatenate([dq.astype(BF16), dk.astype(BF16), dv.astype(BF16), dg.astype(BF16)], 1)


def plane_back(plane, n, p_ref, parts):
    p_ref[...] = jnp.zeros_like(p_ref)
    for i in range(3):
        p_ref[i * HEADS : (i + 1) * HEADS, :] = plane
    p = p_ref[...].astype(BF16)
    return dot(p, parts, TN).astype(BF16).astype(F32), dot(p, n)[0:HEADS]


def start_backward_kernel(
    recv_ref, keep_ref, got_ref, small_ref, n_ref, first_ref, qkv_ref, gating_ref, mix_ref, prob_ref, args_ref, parts_ref, wo_ref,
    send_ref, dfirst_ref, dproj_ref,
    fscr, gscr, plane, narrow, wide, sscr, wscr, p_ref,
):
    n_dst, in_rows, _ = recv_ref.shape
    N = 2 * n_dst
    rows = send_ref.shape[1]
    recv = recv_ref[...].astype(F32)
    total = jnp.sum(recv, 0)
    fscr[...] = recv.reshape(n_dst * in_rows, C)
    for r in range(2):
        for a in range(2):
            gscr[pl.ds(r * N + a, n_dst, stride=2), :] = rows_of(fscr, 8 + r * 2 + a, n_dst, in_rows)
    masks = head_masks(BF16)
    masks_f = head_masks(F32)
    gain_e = args_ref[G_E, :]
    parts = parts_ref[WT_E, :]
    wo = wo_ref[...].astype(BF16)
    results = {}

    def chain(r):
        part = slice(r * N, (r + 1) * N)
        xhat, rstd = ln_stats(first_ref[part, :].astype(F32))
        n_e = (xhat * gain_e).astype(BF16)
        yield
        dn_e, dbias_e = plane_back(total[r * HEADS : (r + 1) * HEADS], n_e, p_ref.at[r], parts)
        yield
        dxe, dgain_e = ln_back(dn_e, xhat, rstd, gain_e)
        dfirst = (gscr[part, :] + dxe).astype(BF16)
        dfirst_ref[part, :] = dfirst
        yield
        q = qkv_ref[part, :C]
        ks = stack_heads(qkv_ref[part, C : 2 * C], masks)
        vs = stack_heads(qkv_ref[part, 2 * C :], masks)
        gating = gating_ref[part, :]
        mix = mix_ref[part, :]
        prob = prob_ref[part, :]
        dgated = dot(dfirst, wo, NT).astype(BF16).astype(F32)
        yield
        dmix = (dgated * gating).astype(BF16)
        dprob = dot(dmix, vs, NT).astype(BF16).astype(F32)
        yield
        ds = []
        for h in range(HEADS):
            p = prob[:, h * N : (h + 1) * N]
            d = dprob[:, h * N : (h + 1) * N]
            ds.append(p * (d - jnp.sum(p * d, -1, keepdims=True)))
        dv = unstack_heads(dot(prob.astype(BF16), dmix, TN), masks_f)
        yield
        ds_b = jnp.concatenate(ds, 1).astype(BF16)
        dq = dot(ds_b, ks)
        dk = unstack_heads(dot(ds_b, q, TN), masks_f)
        yield
        dproj_ref[part, :] = project_cotangent(dq, dk, dv, gating, dgated * mix)
        results[r] = ds, dgain_e, dbias_e

    interleave([chain(r) for r in range(2)])
    (ds, dgain_e, dbias_e), (ds_b, dgain_b, dbias_b) = results[0], results[1]
    dgain_e, dbias_e = dgain_e + dgain_b, dbias_e + dbias_b
    for h in range(HEADS):
        plane[h * N : (h + 1) * N, :] = ds[h] + ds_b[h]
    for r in range(2):
        for h in range(HEADS):
            sscr[pl.ds(r * 4 + h, n_dst, stride=rows), :] = rows_of(plane, h * N + r, n_dst, 2)
    gated = (gating_ref[...] * mix_ref[...]).astype(BF16)
    narrow[0:C, :] = dot(gated, dfirst_ref[...], TN)
    put_narrow(sscr, narrow, 16, n_dst, rows, 2)
    put_wide(sscr, wide, dot(n_ref[...], dproj_ref[...], TN), (8, 12), n_dst, rows)
    smalls = [small_ref[0:1, :], small_ref[1:2, :], dgain_e] + [dbias_e[h : h + 1] for h in range(HEADS)]
    put_small(sscr, 18, smalls, n_dst, rows)
    wscr[...] = keep_ref[...] + got_ref[...].astype(F32)
    for i in range(HALF):
        sscr[pl.ds(19 + i, n_dst, stride=rows), :] = rows_of(wscr, i, n_dst, HALF)
    send_ref[...] = sscr[...].reshape(n_dst, rows, C).astype(BF16)


def start_plane_kernel(recv_ref, dproj_ref, x_ref, w_ref, args_ref, parts_ref, dn_ref, dn_plane_ref, part_ref, p_ref):
    total = jnp.sum(recv_ref[...].astype(F32), 0)
    xhat, _ = ln_stats(x_ref[...].astype(F32))
    n = (xhat * args_ref[G_S, :]).astype(BF16)
    dn = dot(dproj_ref[...], w_ref[...].astype(BF16), NT).astype(BF16)
    dn_ref[...] = dn
    N = n.shape[0] // 2
    backs = [
        plane_back(total[r * HEADS : (r + 1) * HEADS], n[r * N : (r + 1) * N], p_ref.at[r], parts_ref[WT_S, :])
        for r in range(2)
    ]
    dn_plane = jnp.concatenate([back[0] for back in backs], 0)
    dbias = backs[0][1] + backs[1][1]
    dn_plane_ref[...] = dn_plane.astype(BF16)
    part_ref[0:11, :] = total[8:19]
    part_ref[11:15, :] = dbias
    part_ref[15:16, :] = jnp.sum((dn_plane + dn.astype(F32)) * xhat, 0, keepdims=True)
    part_ref[16 : 16 + HALF, :] = total[19 : 19 + HALF]
    part_ref[16 + HALF : 32, :] = jnp.zeros((16 - HALF, C), F32)


def grad_kernel(dn_ref, dn_plane_ref, dfirst_ref, x_ref, args_ref, grad_ref):
    xhat, rstd = ln_stats(x_ref[...].astype(F32))
    dx, _ = ln_back(dn_ref[...].astype(F32), xhat, rstd, args_ref[G_S, :])
    dx_plane, _ = ln_back(dn_plane_ref[...].astype(F32), xhat, rstd, args_ref[G_S, :])
    grad_ref[...] = (dfirst_ref[...].astype(F32) + dx + dx_plane).astype(BF16)


def core_sum_kernel(own_ref, other_ref, out_ref):
    out_ref[0:16, :] = own_ref[0:16, :] + other_ref[0:16, :]
    out_ref[16:32, :] = own_ref[16:32, :]


def spread_kernel(own_ref, far_ref, out_ref, scr):
    total = own_ref[...] + far_ref[...]
    scr[0:8, :] = jnp.where(core_index() == 0, total[0:8], total[8:16])
    scr[8:24, :] = total[16:32]
    out_ref[...] = jnp.broadcast_to(scr[...].astype(BF16)[None], out_ref.shape)


def finish_kernel(
    factor, recv_ref, other_ref,
    gs_out, ps_out, bs_out, os_out, ge_out, pe_out, be_out, oe_out, gt_out, up_out, down_out,
    gs_ref, ps_ref, bs_ref, os_ref, ge_ref, pe_ref, be_ref, oe_ref, gt_ref, up_ref, down_ref,
    fscr, block, sems,
):
    copies = []

    def leave(ref, out):
        copies.append(pltpu.make_async_copy(ref, out, sems.at[len(copies)]))
        copies[-1].start()

    n_dst, half, _ = recv_ref.shape
    size = n_dst * half
    core = core_index()
    for index, ref in ((core, recv_ref), (1 - core, other_ref)):
        fscr[pl.ds(pl.multiple_of(index * size, 8), size), :] = ref[...].astype(F32).reshape(size, C) * factor

    def rows(row):
        return rows_of(fscr, row, n_dst, half)

    def wide(ref, starts):
        for t in range(4):
            for i in range(2):
                block[pl.ds(i, n_dst, stride=2), :] = rows(starts[i] + t)
            ref[:, t * C : (t + 1) * C] = block[...]

    def narrow(ref, starts):
        for i, start in enumerate(starts):
            ref[pl.ds(i, n_dst, stride=len(starts)), :] = rows(start)

    def one(e, row):
        start = e * half + row
        return fscr[start : start + 1, :]

    wide(ps_ref, (0, 4))
    leave(ps_ref, ps_out)
    wide(pe_ref, (8, 12))
    leave(pe_ref, pe_out)
    wide(up_ref, (16, size + 8))
    leave(up_ref, up_out)
    narrow(down_ref, range(size + 12, size + 20))
    leave(down_ref, down_out)
    narrow(os_ref, (size, size + 1))
    leave(os_ref, os_out)
    narrow(oe_ref, (20, size + 20))
    leave(oe_ref, oe_out)
    for h in range(HEADS):
        bs_ref[h : h + 1, :] = jnp.sum(rows(size + 3 + h), 0, keepdims=True)
        be_ref[h : h + 1, :] = one(3 + h, size + 2)
    gt_ref[...] = one(0, size + 2)
    ge_ref[...] = one(1, size + 2) + one(2, size + 2)
    gs_ref[...] = jnp.sum(rows(size + 7), 0, keepdims=True)
    for ref, out in ((bs_ref, bs_out), (be_ref, be_out), (gt_ref, gt_out), (ge_ref, ge_out), (gs_ref, gs_out)):
        leave(ref, out)
    for copy in copies:
        copy.wait()


def shape(dims, dtype=F32):
    return jax.ShapeDtypeStruct(dims, dtype)


def call(body, out_shape, scratch, *operands, in_hbm=(), out=pltpu.VMEM):
    many = isinstance(out_shape, (list, tuple))
    whole = pl.BlockSpec(memory_space=out)
    spaces = [pltpu.HBM if i in in_hbm else pltpu.VMEM for i in range(len(operands))]
    operands = [pltpu.with_memory_space_constraint(a, m) if m is pltpu.HBM else a for a, m in zip(operands, spaces)]
    return pl.pallas_call(
        body,
        out_shape=out_shape,
        in_specs=[pl.BlockSpec(memory_space=m) for m in spaces],
        out_specs=[whole] * len(out_shape) if many else whole,
        scratch_shapes=[pltpu.VMEM(s, F32) if isinstance(s, tuple) else s for s in scratch],
        compiler_params=pltpu.CompilerParams(vmem_limit_bytes=VMEM_LIMIT),
    )(*operands)


def swap(buffer):
    return lax.all_to_all(buffer, "dap", split_axis=0, concat_axis=0, tiled=True)


def local(
    pair_input, cotangent, residue_mask, gain_start, proj_start, bias_start, output_start,
    gain_end, proj_end, bias_end, output_end, gain_transition, transition_up, transition_down,
):
    _, _, N, _ = pair_input.shape
    n_dst = N // 2
    x = pair_input.reshape(2 * N, C)
    cot = cotangent.reshape(2 * N, C)
    g_s, g_e, g_t = (g.reshape(1, C) for g in (gain_start, gain_end, gain_transition))
    wt_s, wt_e = bias_start.T, bias_end.T
    tokens = (2 * N, C)
    wide = (C, 4 * C)

    send, args, parts = call(
        plane_local_kernel,
        [shape((n_dst, 8, C), BF16), shape((8, C)), shape((32, C), BF16)],
        [pltpu.VMEM(tokens, BF16), (1, C), (HEADS, C), (1, C), (HEADS, C), (1, C),
         pltpu.VMEM((1, C), jnp.int32), (8, C), (16, C), pltpu.SemaphoreType.DMA((7,))],
        x, g_s, wt_s, g_e, wt_e, g_t, residue_mask,
        in_hbm=range(7),
    )
    recv = swap(send)
    qkv, gating, score, n, cot, wo = call(
        start_scores_kernel,
        [shape((2 * N, 3 * C), BF16), shape(tokens), shape((2 * N, HEADS * N)), shape(tokens, BF16),
         shape(tokens, BF16), shape((C, C))],
        [pltpu.SemaphoreType.DMA((2,))],
        x, cot, args, proj_start, output_start,
        in_hbm=(1, 4),
    )
    send, mix, prob, first = call(
        start_forward_kernel,
        [shape((n_dst, 16, C), BF16), shape(tokens), shape((2 * N, HEADS * N)), shape(tokens, BF16)],
        [(n_dst * 8, C), (HEADS * N, N), (n_dst * 16, C), (8, C)],
        recv, x, cot, args, parts, qkv, gating, score, wo,
    )
    recv = swap(send)
    n_dp = lax.axis_size("dp")
    to_core = [(i, i ^ 1) for i in range(n_dp)]
    half = (n_dst * HALF, C)
    hidden = (2 * N, 4 * C)
    send, small, *saved = call(
        end_kernel,
        [shape((n_dst, 16, C), BF16), shape((8, C)), shape(hidden, BF16), shape(hidden, BF16), shape(tokens, BF16),
         shape(tokens, BF16), shape(tokens, BF16), shape(hidden, BF16), shape(tokens, BF16), shape(tokens, BF16)],
        [(n_dst * 16, C), tokens, tokens, (HEADS * N, N), (n_dst * 16, C)],
        recv, args, proj_end, output_end, transition_up, transition_down,
    )
    recv = swap(send)
    keep, give = call(
        end_weights_kernel,
        [shape(half), shape(half, BF16)],
        [(4 * C, C), (4 * C, C), (4 * C, C), (C, C), (n_dst * 2 * HALF, C)],
        *saved,
    )
    got = lax.ppermute(give, "dp", to_core)
    send, dfirst, dproj = call(
        start_backward_kernel,
        [shape((n_dst, 32, C), BF16), shape(tokens, BF16), shape(hidden, BF16)],
        [(n_dst * 16, C), tokens, (HEADS * N, N), (C, C), (4 * C, C), (n_dst * 32, C), half, (2, 16, C)],
        recv, keep, got, small, n, first, qkv, gating, mix, prob, args, parts, wo,
    )
    recv = swap(send)
    dn, dn_plane, part = call(
        start_plane_kernel,
        [shape(tokens, BF16), shape(tokens, BF16), shape((32, C))],
        [(2, 16, C)],
        recv, dproj, x, proj_start, args, parts,
    )
    part = call(core_sum_kernel, shape((32, C)), [], part, lax.ppermute(part, "dp", to_core))
    far = lax.ppermute(part, "dp", [(i, i ^ 2) for i in range(n_dp)])
    grad = call(grad_kernel, shape(tokens, BF16), [], dn, dn_plane, dfirst, x, args)
    grad, far = lax.optimization_barrier((grad, far))
    send = call(spread_kernel, shape((n_dst, 24, C), BF16), [(24, C)], part, far)
    recv = swap(send)
    other = lax.ppermute(recv, "dp", to_core)
    factor = 1.0 / (n_dp * N)
    vector, bias, square, tall = (1, C), (HEADS, C), (C, C), (4 * C, C)
    sizes = [vector, wide, bias, square, vector, wide, bias, square, vector, wide, tall]
    gs, ps, bs, os, ge, pe, be, oe, gt, up, down = call(
        functools.partial(finish_kernel, factor),
        [shape(size) for size in sizes],
        [*sizes, (n_dst * 48, C), square, pltpu.SemaphoreType.DMA((len(sizes),))],
        recv, other,
        out=pltpu.HBM,
    )
    return (
        grad.reshape(1, 2, N, C), gs.reshape(C), ps, bs.T, os, ge.reshape(C), pe, be.T, oe, gt.reshape(C), up, down,
    )


def solution(mesh):
    rows = P("dp", "dap", None, None)
    in_specs = (rows, rows, P("dp", None)) + (P(),) * 11
    out_specs = (rows,) + (P(),) * 11
    return jax.shard_map(local, mesh=mesh, in_specs=in_specs, out_specs=out_specs, check_vma=False)
```

```python
import functools

import jax
import jax.numpy as jnp
from jax import lax
from jax.experimental import pallas as pl
from jax.experimental.pallas import tpu as pltpu
from jax.sharding import PartitionSpec as P

HEADS = 4
EPS = 1e-05
F32 = jnp.float32
BF16 = jnp.bfloat16
C = 128
HALF = 13
VMEM_LIMIT = 48 * 1024 * 1024


def dot(a, b, contract=((1,), (0,))):
    return lax.dot_general(a, b, (contract, ((), ())), preferred_element_type=F32)


NN = ((1,), (0,))
NT = ((1,), (1,))
TN = ((0,), (0,))


def ln_stats(x):
    centre = x - jnp.mean(x, -1, keepdims=True)
    spread = jnp.mean(centre * centre, -1, keepdims=True)
    rstd = lax.rsqrt(spread + EPS)
    return centre * rstd, rstd


def ln_back(dn, xhat, rstd, gain):
    t = dn * gain
    m1 = jnp.mean(t, -1, keepdims=True)
    m2 = jnp.mean(t * xhat, -1, keepdims=True)
    dx = rstd * (t - m1 - xhat * m2)
    return dx.astype(BF16).astype(F32), jnp.sum(dn * xhat, 0, keepdims=True)


def head_masks(dtype):
    lane = lax.broadcasted_iota(jnp.int32, (1, C), 1)
    size = C // HEADS
    return [((lane >= h * size) & (lane < (h + 1) * size)).astype(dtype) for h in range(HEADS)]


def stack_heads(a, masks):
    return jnp.concatenate([a * m for m in masks], 0)


def unstack_heads(a, masks):
    n = a.shape[0] // HEADS
    total = a[:n] * masks[0]
    for h in range(1, HEADS):
        total = total + a[h * n : (h + 1) * n] * masks[h]
    return total


def interleave(chains):
    done = object()
    while chains:
        chains = [chain for chain in chains if next(chain, done) is not done]


def project(n, w):
    proj = dot(n, w)
    scale = (C // HEADS) ** (-0.5)
    q = (proj[:, :C] * scale).astype(BF16)
    k = proj[:, C : 2 * C].astype(BF16)
    v = proj[:, 2 * C : 3 * C].astype(BF16)
    return q, k, v, jax.nn.sigmoid(proj[:, 3 * C :])


def split(scr, wt):
    for i in range(3):
        part = wt.astype(BF16).astype(F32)
        scr[i * HEADS : (i + 1) * HEADS, :] = part
        wt = wt - part
    scr[3 * HEADS : 16, :] = jnp.zeros((16 - 3 * HEADS, C), F32)
    return scr[...].astype(BF16)


def plane_of(n, parts):
    out = dot(parts, n, NT)
    return out[0:4] + out[4:8] + out[8:12]


def core_index():
    return lax.rem(lax.axis_index("dp"), 2)


def rows_of(ref, start, count, stride):
    return ref[pl.ds(start, count, stride=stride), :]


WT_S, WT_E = slice(0, 16), slice(16, 32)
G_S, G_E, G_T, KEPT = slice(0, 1), slice(1, 2), slice(2, 3), slice(3, 4)


def plane_local_kernel(
    x_hbm, gs_hbm, wts_hbm, ge_hbm, wte_hbm, gt_hbm, mask_hbm, w_hbm, cot_hbm, wo_hbm,
    out_ref, args_ref, parts_ref, x_ref, qkv_ref, gating_ref, score_ref, n_ref, cot_ref, wo_ref,
    gs, wts, ge, wte, gt, mask, w_ref, small, scr, sems,
):
    n_dst, rows, _ = out_ref.shape
    moves = [
        (x_hbm, x_ref), (gs_hbm, gs), (wts_hbm, wts), (ge_hbm, ge), (wte_hbm, wte), (gt_hbm, gt), (mask_hbm, mask),
        (w_hbm, w_ref), (cot_hbm, cot_ref), (wo_hbm, wo_ref),
    ]
    copies = [pltpu.make_async_copy(src, dst, sems.at[i]) for i, (src, dst) in enumerate(moves)]
    for copy in copies:
        copy.start()
    for copy in copies[:-3]:
        copy.wait()
    parts_ref[WT_S, :] = split(scr, wts[...])
    parts_ref[WT_E, :] = split(scr, wte[...])
    args_ref[G_S, :] = gs[...]
    args_ref[G_E, :] = ge[...]
    args_ref[G_T, :] = gt[...]
    args_ref[KEPT, :] = mask[...].astype(F32)
    args_ref[4:8, :] = jnp.zeros((4, C), F32)
    xhat, _ = ln_stats(x_ref[...].astype(F32))
    n = (xhat * gs[...]).astype(BF16)
    plane = plane_of(n, parts_ref[WT_S, :])
    small[0:HEADS, :] = plane[:, :C]
    small[HEADS : 2 * HEADS, :] = plane[:, C:]
    out_ref[...] = jnp.broadcast_to(small[...].astype(BF16)[None], (n_dst, rows, C))
    n_ref[...] = n
    copies[-3].wait()
    w = w_ref[...].astype(BF16)
    masks = head_masks(BF16)
    N = 2 * n_dst

    def chain(r):
        part = slice(r * N, (r + 1) * N)
        q, k, v, gating = project(n[part], w)
        yield
        qkv_ref[part, :C] = q
        qkv_ref[part, C : 2 * C] = k
        qkv_ref[part, 2 * C :] = v
        gating_ref[part, :] = gating
        score_ref[part, :] = dot(q, stack_heads(k, masks), NT)

    interleave([chain(r) for r in range(2)])
    for copy in copies[-2:]:
        copy.wait()


def start_forward_kernel(
    recv_ref, x_ref, cot_ref, args_ref, parts_ref, qkv_ref, gating_ref, score_ref, wo_ref,
    send_ref, mix_ref, prob_ref, first_ref,
    fscr, plane, sscr, small,
):
    n_dst = recv_ref.shape[0]
    N = 2 * n_dst
    rows = send_ref.shape[1]
    fscr[...] = recv_ref[...].astype(F32).reshape(n_dst * 8, C)
    for r in range(2):
        for h in range(HEADS):
            plane[pl.ds(h * N + r, n_dst, stride=2), :] = rows_of(fscr, r * 4 + h, n_dst, 8)
    masks = head_masks(BF16)
    kept = args_ref[KEPT, :]
    x = x_ref[...].astype(F32)
    v = qkv_ref[:, 2 * C :]
    gating = gating_ref[...]
    wo = wo_ref[...].astype(BF16)
    parts = parts_ref[WT_E, :]

    def chain(r):
        part = slice(r * N, (r + 1) * N)
        probs = []
        for h in range(HEADS):
            w = jnp.exp(score_ref[part, h * N : (h + 1) * N] + plane[h * N : (h + 1) * N, :]) * kept
            probs.append(w * (1.0 / jnp.sum(w, -1, keepdims=True)))
        prob = jnp.concatenate(probs, 1)
        prob_ref[part, :] = prob
        yield
        mix = dot(prob.astype(BF16), stack_heads(v[part], masks))
        mix_ref[part, :] = mix
        yield
        first = (x[part] + dot((gating[part] * mix).astype(BF16), wo)).astype(BF16)
        first_ref[part, :] = first
        yield
        first = first.astype(F32)
        fscr[part, :] = first
        xhat, _ = ln_stats(first)
        yield
        small[r * HEADS : (r + 1) * HEADS, :] = plane_of((xhat * args_ref[G_E, :]).astype(BF16), parts)
        yield
        for a in range(2):
            sscr[pl.ds(r * 2 + a, n_dst, stride=rows), :] = rows_of(fscr, r * N + a, n_dst, 2)

    interleave([chain(r) for r in range(2)])
    fscr[0 : 2 * N, :] = cot_ref[...].astype(F32)
    for r in range(2):
        for a in range(2):
            sscr[pl.ds(4 + r * 2 + a, n_dst, stride=rows), :] = rows_of(fscr, r * N + a, n_dst, 2)
    for i in range(8):
        sscr[pl.ds(8 + i, n_dst, stride=rows), :] = jnp.broadcast_to(small[i : i + 1, :], (n_dst, C))
    send_ref[...] = sscr[...].reshape(n_dst, rows, C).astype(BF16)


def put_wide(scr, src, value, starts, n_dst, rows):
    for t in range(4):
        src[t * C : (t + 1) * C, :] = value[:, t * C : (t + 1) * C]
        for i in range(2):
            scr[pl.ds(starts[i] + t, n_dst, stride=rows), :] = rows_of(src, t * C + i, n_dst, 2)


def put_narrow(scr, src, row, n_dst, rows, each):
    for i in range(each):
        scr[pl.ds(row + i, n_dst, stride=rows), :] = rows_of(src, i, n_dst, each)


def put_small(scr, row, values, n_dst, rows):
    scr[pl.ds(row, n_dst, stride=rows), :] = jnp.zeros((n_dst, C), F32)
    for e, value in enumerate(values):
        scr[e * rows + row : e * rows + row + 1, :] = value


def end_kernel(
    recv_ref, args_ref, w_ref, wo_ref, wu_ref, wd_ref,
    send_ref, small_ref, hidden_ref, dup_ref, n_ref, n2_ref, cot_ref, dproj_ref, gated_ref, dsecond_ref,
    fscr, zscr, cscr, plane, sscr,
):
    n_dst, in_rows, _ = recv_ref.shape
    N = 2 * n_dst
    fscr[...] = recv_ref[...].astype(F32).reshape(n_dst * in_rows, C)
    for r in range(2):
        for a in range(2):
            zscr[pl.ds(a * N + r, n_dst, stride=2), :] = rows_of(fscr, r * 2 + a, n_dst, in_rows)
            cscr[pl.ds(a * N + r, n_dst, stride=2), :] = rows_of(fscr, 4 + r * 2 + a, n_dst, in_rows)
        for h in range(HEADS):
            plane[pl.ds(h * N + r, n_dst, stride=2), :] = rows_of(fscr, 8 + r * 4 + h, n_dst, in_rows)
    masks = head_masks(BF16)
    masks_f = head_masks(F32)
    gain, gain_t = args_ref[G_E, :], args_ref[G_T, :]
    length = jnp.sum(args_ref[KEPT, :], -1, keepdims=True)
    kept = (lax.broadcasted_iota(jnp.int32, (N, 1), 0).astype(F32) < length).astype(F32)
    w = w_ref[...].astype(BF16)
    wo = wo_ref[...].astype(BF16)
    wu = wu_ref[...].astype(BF16)
    wd = wd_ref[...].astype(BF16)
    results = {}

    def chain(a):
        part = slice(a * N, (a + 1) * N)
        x = zscr[part, :]
        cot = cscr[part, :]
        cot_b = cot.astype(BF16)
        cot_ref[part, :] = cot_b
        xhat, rstd = ln_stats(x)
        n = (xhat * gain).astype(BF16)
        n_ref[part, :] = n
        yield
        q, k, v, gating = project(n, w)
        yield
        ks = stack_heads(k, masks)
        vs = stack_heads(v, masks)
        s = dot(ks, q, NT) + plane[...]
        yield
        probs = []
        for h in range(HEADS):
            e = jnp.exp(s[h * N : (h + 1) * N]) * kept
            probs.append(e * (1.0 / jnp.sum(e, 0, keepdims=True)))
        prob = jnp.concatenate(probs, 0)
        prob_b = prob.astype(BF16)
        yield
        mix = dot(prob_b, vs, TN)
        yield
        gated = (gating * mix).astype(BF16)
        gated_ref[part, :] = gated
        second = (x + dot(gated, wo)).astype(BF16).astype(F32)
        yield
        xhat2, rstd2 = ln_stats(second)
        n2 = (xhat2 * gain_t).astype(BF16)
        n2_ref[part, :] = n2
        dhidden = dot(cot_b, wd, NT).astype(BF16).astype(F32)
        yield
        up = dot(n2, wu)
        yield
        cdf = 0.5 * (1.0 + lax.erf(up * (0.5**0.5)))
        slope = cdf + up * (jnp.exp(-0.5 * up * up) * 0.3989422804014327)
        dup = (dhidden * slope).astype(BF16)
        hidden_ref[part, :] = (up * cdf).astype(BF16)
        dup_ref[part, :] = dup
        yield
        dn2 = dot(dup, wu, NT).astype(BF16).astype(F32)
        yield
        dx2, dgain_t = ln_back(dn2, xhat2, rstd2, gain_t)
        dsecond = (cot + dx2).astype(BF16)
        dsecond_ref[part, :] = dsecond
        yield
        dgated = dot(dsecond, wo, NT).astype(BF16).astype(F32)
        yield
        dmix = (dgated * gating).astype(BF16)
        dprob = dot(vs, dmix, NT).astype(BF16).astype(F32)
        yield
        ds = []
        for h in range(HEADS):
            p = prob[h * N : (h + 1) * N]
            d = dprob[h * N : (h + 1) * N]
            ds.append(p * (d - jnp.sum(p * d, 0, keepdims=True)))
        ds = jnp.concatenate(ds, 0)
        dv = unstack_heads(dot(prob_b, dmix), masks_f)
        yield
        ds_b = ds.astype(BF16)
        dq = dot(ds_b, ks, TN)
        dk = unstack_heads(dot(ds_b, q), masks_f)
        yield
        dproj = project_cotangent(dq, dk, dv, gating, dgated * mix)
        dproj_ref[part, :] = dproj
        dn = dot(dproj, w, NT).astype(BF16).astype(F32)
        yield
        dx, dgain = ln_back(dn, xhat, rstd, gain)
        zscr[part, :] = dsecond.astype(F32) + dx
        results[a] = ds, dgain_t, dgain

    interleave([chain(a) for a in range(2)])
    (ds, dgain_t, dgain), (ds_b, dgain_t_b, dgain_b) = results[0], results[1]
    plane[...] = ds + ds_b
    for r in range(2):
        for h in range(HEADS):
            sscr[pl.ds(r * 8 + h, n_dst, stride=24), :] = rows_of(plane, h * N + r, n_dst, 2)
        for a in range(2):
            sscr[pl.ds(16 + r * 2 + a, n_dst, stride=24), :] = rows_of(zscr, a * N + r, n_dst, 2)
    send_ref[...] = sscr[...].reshape(n_dst, 3, 8, C)[:, :, 0:4, :].astype(BF16)
    small_ref[0:1, :] = dgain_t + dgain_t_b
    small_ref[1:2, :] = dgain + dgain_b
    small_ref[2:8, :] = jnp.zeros((6, C), F32)


def end_weights_kernel(
    hidden_ref, dup_ref, n_ref, n2_ref, cot_ref, dproj_ref, gated_ref, dsecond_ref,
    keep_ref, give_ref,
    down, up, proj, narrow, wscr,
):
    half = keep_ref.shape[0]
    n_dst = half // HALF
    down[...] = dot(hidden_ref[...], cot_ref[...], TN)
    put_narrow(wscr, down, half + 4, n_dst, HALF, 8)
    put_wide(wscr, up, dot(n2_ref[...], dup_ref[...], TN), (8, half), n_dst, HALF)
    put_wide(wscr, proj, dot(n_ref[...], dproj_ref[...], TN), (0, 4), n_dst, HALF)
    narrow[...] = dot(gated_ref[...], dsecond_ref[...], TN)
    for i in range(2):
        wscr[pl.ds(i * half + 12, n_dst, stride=HALF), :] = rows_of(narrow, i, n_dst, 2)
    core = core_index()
    keep_ref[...] = wscr[pl.ds(pl.multiple_of(core * half, 8), half), :]
    give_ref[...] = wscr[pl.ds(pl.multiple_of((1 - core) * half, 8), half), :].astype(BF16)


def project_cotangent(dq, dk, dv, gating, dgating):
    dq = dq.astype(BF16).astype(F32) * (C // HEADS) ** (-0.5)
    dg = dgating * gating * (1.0 - gating)
    return jnp.concatenate([dq.astype(BF16), dk.astype(BF16), dv.astype(BF16), dg.astype(BF16)], 1)


def plane_back(plane, n, p_ref, parts):
    p_ref[...] = jnp.zeros_like(p_ref)
    for i in range(3):
        p_ref[i * HEADS : (i + 1) * HEADS, :] = plane
    p = p_ref[...].astype(BF16)
    return dot(p, parts, TN).astype(BF16).astype(F32), dot(p, n)[0:HEADS]


def start_backward_kernel(
    recv_ref, keep_ref, got_ref, small_ref, n_ref, first_ref, qkv_ref, gating_ref, mix_ref, prob_ref, args_ref, parts_ref, wo_ref,
    send_ref, dfirst_ref, dproj_ref,
    fscr, gscr, plane, narrow, wide, sscr, wscr, p_ref,
):
    n_dst = recv_ref.shape[0]
    N = 2 * n_dst
    rows = send_ref.shape[1]
    total = jnp.sum(recv_ref[:, 0:2].astype(F32), 0)
    fscr[:, 0:4, :] = recv_ref[:, 2].astype(F32)
    grads = fscr.reshape(n_dst * 8, C)
    for r in range(2):
        for a in range(2):
            gscr[pl.ds(r * N + a, n_dst, stride=2), :] = rows_of(grads, r * 2 + a, n_dst, 8)
    masks = head_masks(BF16)
    masks_f = head_masks(F32)
    gain_e = args_ref[G_E, :]
    parts = parts_ref[WT_E, :]
    wo = wo_ref[...].astype(BF16)
    results = {}

    def chain(r):
        part = slice(r * N, (r + 1) * N)
        xhat, rstd = ln_stats(first_ref[part, :].astype(F32))
        n_e = (xhat * gain_e).astype(BF16)
        yield
        dn_e, dbias_e = plane_back(total[r], n_e, p_ref.at[r], parts)
        yield
        dxe, dgain_e = ln_back(dn_e, xhat, rstd, gain_e)
        dfirst = (gscr[part, :] + dxe).astype(BF16)
        dfirst_ref[part, :] = dfirst
        yield
        q = qkv_ref[part, :C]
        ks = stack_heads(qkv_ref[part, C : 2 * C], masks)
        vs = stack_heads(qkv_ref[part, 2 * C :], masks)
        gating = gating_ref[part, :]
        mix = mix_ref[part, :]
        prob = prob_ref[part, :]
        dgated = dot(dfirst, wo, NT).astype(BF16).astype(F32)
        yield
        dmix = (dgated * gating).astype(BF16)
        dprob = dot(dmix, vs, NT).astype(BF16).astype(F32)
        yield
        ds = []
        for h in range(HEADS):
            p = prob[:, h * N : (h + 1) * N]
            d = dprob[:, h * N : (h + 1) * N]
            ds.append(p * (d - jnp.sum(p * d, -1, keepdims=True)))
        dv = unstack_heads(dot(prob.astype(BF16), dmix, TN), masks_f)
        yield
        ds_b = jnp.concatenate(ds, 1).astype(BF16)
        dq = dot(ds_b, ks)
        dk = unstack_heads(dot(ds_b, q, TN), masks_f)
        yield
        dproj_ref[part, :] = project_cotangent(dq, dk, dv, gating, dgated * mix)
        results[r] = ds, dgain_e, dbias_e

    interleave([chain(r) for r in range(2)])
    (ds, dgain_e, dbias_e), (ds_b, dgain_b, dbias_b) = results[0], results[1]
    dgain_e, dbias_e = dgain_e + dgain_b, dbias_e + dbias_b
    for h in range(HEADS):
        plane[h * N : (h + 1) * N, :] = ds[h] + ds_b[h]
    for r in range(2):
        for h in range(HEADS):
            sscr[pl.ds(r * 4 + h, n_dst, stride=rows), :] = rows_of(plane, h * N + r, n_dst, 2)
    gated = (gating_ref[...] * mix_ref[...]).astype(BF16)
    narrow[0:C, :] = dot(gated, dfirst_ref[...], TN)
    put_narrow(sscr, narrow, 16, n_dst, rows, 2)
    put_wide(sscr, wide, dot(n_ref[...], dproj_ref[...], TN), (8, 12), n_dst, rows)
    smalls = [small_ref[0:1, :], small_ref[1:2, :], dgain_e] + [dbias_e[h : h + 1] for h in range(HEADS)]
    put_small(sscr, 18, smalls, n_dst, rows)
    wscr[...] = keep_ref[...] + got_ref[...].astype(F32)
    for i in range(HALF):
        sscr[pl.ds(19 + i, n_dst, stride=rows), :] = rows_of(wscr, i, n_dst, HALF)
    send_ref[...] = sscr[...].reshape(n_dst, rows, C).astype(BF16)


def start_plane_kernel(recv_ref, dproj_ref, x_ref, w_ref, args_ref, parts_ref, dn_ref, dn_plane_ref, part_ref, p_ref):
    total = jnp.sum(recv_ref[...].astype(F32), 0)
    xhat, _ = ln_stats(x_ref[...].astype(F32))
    n = (xhat * args_ref[G_S, :]).astype(BF16)
    dn = dot(dproj_ref[...], w_ref[...].astype(BF16), NT).astype(BF16)
    dn_ref[...] = dn
    N = n.shape[0] // 2
    backs = [
        plane_back(total[r * HEADS : (r + 1) * HEADS], n[r * N : (r + 1) * N], p_ref.at[r], parts_ref[WT_S, :])
        for r in range(2)
    ]
    dn_plane = jnp.concatenate([back[0] for back in backs], 0)
    dbias = backs[0][1] + backs[1][1]
    dn_plane_ref[...] = dn_plane.astype(BF16)
    part_ref[0:11, :] = total[8:19]
    part_ref[11:15, :] = dbias
    part_ref[15:16, :] = jnp.sum((dn_plane + dn.astype(F32)) * xhat, 0, keepdims=True)
    part_ref[16 : 16 + HALF, :] = total[19 : 19 + HALF]
    part_ref[16 + HALF : 32, :] = jnp.zeros((16 - HALF, C), F32)


def grad_kernel(dn_ref, dn_plane_ref, dfirst_ref, x_ref, args_ref, grad_ref):
    xhat, rstd = ln_stats(x_ref[...].astype(F32))
    dx, _ = ln_back(dn_ref[...].astype(F32), xhat, rstd, args_ref[G_S, :])
    dx_plane, _ = ln_back(dn_plane_ref[...].astype(F32), xhat, rstd, args_ref[G_S, :])
    grad_ref[...] = (dfirst_ref[...].astype(F32) + dx + dx_plane).astype(BF16)


def core_sum_kernel(own_ref, other_ref, out_ref):
    out_ref[0:16, :] = own_ref[0:16, :] + other_ref[0:16, :]
    out_ref[16:32, :] = own_ref[16:32, :]


def spread_kernel(own_ref, far_ref, out_ref, scr):
    total = own_ref[...] + far_ref[...]
    scr[0:8, :] = jnp.where(core_index() == 0, total[0:8], total[8:16])
    scr[8:24, :] = total[16:32]
    out_ref[...] = jnp.broadcast_to(scr[...].astype(BF16)[None], out_ref.shape)


def finish_kernel(
    factor, recv_ref, other_ref,
    gs_out, ps_out, bs_out, os_out, ge_out, pe_out, be_out, oe_out, gt_out, up_out, down_out,
    gs_ref, ps_ref, bs_ref, os_ref, ge_ref, pe_ref, be_ref, oe_ref, gt_ref, up_ref, down_ref,
    fscr, block, sems,
):
    copies = []

    def leave(ref, out):
        copies.append(pltpu.make_async_copy(ref, out, sems.at[len(copies)]))
        copies[-1].start()

    n_dst, half, _ = recv_ref.shape
    size = n_dst * half
    core = core_index()
    for index, ref in ((core, recv_ref), (1 - core, other_ref)):
        fscr[pl.ds(pl.multiple_of(index * size, 8), size), :] = ref[...].astype(F32).reshape(size, C) * factor

    def rows(row):
        return rows_of(fscr, row, n_dst, half)

    def wide(ref, starts):
        for t in range(4):
            for i in range(2):
                block[pl.ds(i, n_dst, stride=2), :] = rows(starts[i] + t)
            ref[:, t * C : (t + 1) * C] = block[...]

    def narrow(ref, starts):
        for i, start in enumerate(starts):
            ref[pl.ds(i, n_dst, stride=len(starts)), :] = rows(start)

    def one(e, row):
        start = e * half + row
        return fscr[start : start + 1, :]

    wide(ps_ref, (0, 4))
    leave(ps_ref, ps_out)
    wide(pe_ref, (8, 12))
    leave(pe_ref, pe_out)
    wide(up_ref, (16, size + 8))
    leave(up_ref, up_out)
    narrow(down_ref, range(size + 12, size + 20))
    leave(down_ref, down_out)
    narrow(os_ref, (size, size + 1))
    leave(os_ref, os_out)
    narrow(oe_ref, (20, size + 20))
    leave(oe_ref, oe_out)
    for h in range(HEADS):
        bs_ref[h : h + 1, :] = jnp.sum(rows(size + 3 + h), 0, keepdims=True)
        be_ref[h : h + 1, :] = one(3 + h, size + 2)
    gt_ref[...] = one(0, size + 2)
    ge_ref[...] = one(1, size + 2) + one(2, size + 2)
    gs_ref[...] = jnp.sum(rows(size + 7), 0, keepdims=True)
    for ref, out in ((bs_ref, bs_out), (be_ref, be_out), (gt_ref, gt_out), (ge_ref, ge_out), (gs_ref, gs_out)):
        leave(ref, out)
    for copy in copies:
        copy.wait()


def shape(dims, dtype=F32):
    return jax.ShapeDtypeStruct(dims, dtype)


def call(body, out_shape, scratch, *operands, in_hbm=(), out=pltpu.VMEM):
    many = isinstance(out_shape, (list, tuple))
    whole = pl.BlockSpec(memory_space=out)
    spaces = [pltpu.HBM if i in in_hbm else pltpu.VMEM for i in range(len(operands))]
    operands = [pltpu.with_memory_space_constraint(a, m) if m is pltpu.HBM else a for a, m in zip(operands, spaces)]
    return pl.pallas_call(
        body,
        out_shape=out_shape,
        in_specs=[pl.BlockSpec(memory_space=m) for m in spaces],
        out_specs=[whole] * len(out_shape) if many else whole,
        scratch_shapes=[pltpu.VMEM(s, F32) if isinstance(s, tuple) else s for s in scratch],
        compiler_params=pltpu.CompilerParams(vmem_limit_bytes=VMEM_LIMIT),
    )(*operands)


def swap(buffer):
    return lax.all_to_all(buffer, "dap", split_axis=0, concat_axis=0, tiled=True)


def local(
    pair_input, cotangent, residue_mask, gain_start, proj_start, bias_start, output_start,
    gain_end, proj_end, bias_end, output_end, gain_transition, transition_up, transition_down,
):
    _, _, N, _ = pair_input.shape
    n_dst = N // 2
    x = pair_input.reshape(2 * N, C)
    cot = cotangent.reshape(2 * N, C)
    g_s, g_e, g_t = (g.reshape(1, C) for g in (gain_start, gain_end, gain_transition))
    wt_s, wt_e = bias_start.T, bias_end.T
    tokens = (2 * N, C)
    wide = (C, 4 * C)

    send, args, parts, x_in, qkv, gating, score, n, cot, wo = call(
        plane_local_kernel,
        [shape((n_dst, 8, C), BF16), shape((8, C)), shape((32, C), BF16), shape(tokens, BF16), shape((2 * N, 3 * C), BF16),
         shape(tokens), shape((2 * N, HEADS * N)), shape(tokens, BF16), shape(tokens, BF16), shape((C, C))],
        [(1, C), (HEADS, C), (1, C), (HEADS, C), (1, C), pltpu.VMEM((1, C), jnp.int32), wide,
         (8, C), (16, C), pltpu.SemaphoreType.DMA((10,))],
        x, g_s, wt_s, g_e, wt_e, g_t, residue_mask, proj_start, cot, output_start,
        in_hbm=range(10),
    )
    recv = swap(send)
    send, mix, prob, first = call(
        start_forward_kernel,
        [shape((n_dst, 16, C), BF16), shape(tokens), shape((2 * N, HEADS * N)), shape(tokens, BF16)],
        [(n_dst * 8, C), (HEADS * N, N), (n_dst * 16, C), (8, C)],
        recv, x_in, cot, args, parts, qkv, gating, score, wo,
    )
    recv = swap(send)
    n_dp = lax.axis_size("dp")
    to_core = [(i, i ^ 1) for i in range(n_dp)]
    half = (n_dst * HALF, C)
    hidden = (2 * N, 4 * C)
    send, small, *saved = call(
        end_kernel,
        [shape((n_dst, 3, 4, C), BF16), shape((8, C)), shape(hidden, BF16), shape(hidden, BF16), shape(tokens, BF16),
         shape(tokens, BF16), shape(tokens, BF16), shape(hidden, BF16), shape(tokens, BF16), shape(tokens, BF16)],
        [(n_dst * 16, C), tokens, tokens, (HEADS * N, N), (n_dst * 24, C)],
        recv, args, proj_end, output_end, transition_up, transition_down,
    )
    recv = swap(send)
    keep, give = call(
        end_weights_kernel,
        [shape(half), shape(half, BF16)],
        [(4 * C, C), (4 * C, C), (4 * C, C), (C, C), (n_dst * 2 * HALF, C)],
        *saved,
    )
    got = lax.ppermute(give, "dp", to_core)
    send, dfirst, dproj = call(
        start_backward_kernel,
        [shape((n_dst, 32, C), BF16), shape(tokens, BF16), shape(hidden, BF16)],
        [(n_dst, 8, C), tokens, (HEADS * N, N), (C, C), (4 * C, C), (n_dst * 32, C), half, (2, 16, C)],
        recv, keep, got, small, n, first, qkv, gating, mix, prob, args, parts, wo,
    )
    recv = swap(send)
    dn, dn_plane, part = call(
        start_plane_kernel,
        [shape(tokens, BF16), shape(tokens, BF16), shape((32, C))],
        [(2, 16, C)],
        recv, dproj, x, proj_start, args, parts,
    )
    part = call(core_sum_kernel, shape((32, C)), [], part, lax.ppermute(part, "dp", to_core))
    far = lax.ppermute(part, "dp", [(i, i ^ 2) for i in range(n_dp)])
    grad = call(grad_kernel, shape(tokens, BF16), [], dn, dn_plane, dfirst, x, args)
    grad, far = lax.optimization_barrier((grad, far))
    send = call(spread_kernel, shape((n_dst, 24, C), BF16), [(24, C)], part, far)
    recv = swap(send)
    other = lax.ppermute(recv, "dp", to_core)
    factor = 1.0 / (n_dp * N)
    vector, bias, square, tall = (1, C), (HEADS, C), (C, C), (4 * C, C)
    sizes = [vector, wide, bias, square, vector, wide, bias, square, vector, wide, tall]
    gs, ps, bs, os, ge, pe, be, oe, gt, up, down = call(
        functools.partial(finish_kernel, factor),
        [shape(size) for size in sizes],
        [*sizes, (n_dst * 48, C), square, pltpu.SemaphoreType.DMA((len(sizes),))],
        recv, other,
        out=pltpu.HBM,
    )
    return (
        grad.reshape(1, 2, N, C), gs.reshape(C), ps, bs.T, os, ge.reshape(C), pe, be.T, oe, gt.reshape(C), up, down,
    )


def solution(mesh):
    rows = P("dp", "dap", None, None)
    in_specs = (rows, rows, P("dp", None)) + (P(),) * 11
    out_specs = (rows,) + (P(),) * 11
    return jax.shard_map(local, mesh=mesh, in_specs=in_specs, out_specs=out_specs, check_vma=False)
```

```python
import functools

import jax
import jax.numpy as jnp
from jax import lax
from jax.experimental import pallas as pl
from jax.experimental.pallas import tpu as pltpu
from jax.sharding import PartitionSpec as P

HEADS = 4
EPS = 1e-05
F32 = jnp.float32
BF16 = jnp.bfloat16
C = 128
HALF = 13
VMEM_LIMIT = 48 * 1024 * 1024


def dot(a, b, contract=((1,), (0,))):
    return lax.dot_general(a, b, (contract, ((), ())), preferred_element_type=F32)


NN = ((1,), (0,))
NT = ((1,), (1,))
TN = ((0,), (0,))


def ln_stats(x):
    centre = x - jnp.mean(x, -1, keepdims=True)
    spread = jnp.mean(centre * centre, -1, keepdims=True)
    rstd = lax.rsqrt(spread + EPS)
    return centre * rstd, rstd


def ln_back(dn, xhat, rstd, gain):
    t = dn * gain
    m1 = jnp.mean(t, -1, keepdims=True)
    m2 = jnp.mean(t * xhat, -1, keepdims=True)
    dx = rstd * (t - m1 - xhat * m2)
    return dx.astype(BF16).astype(F32), jnp.sum(dn * xhat, 0, keepdims=True)


def head_masks(dtype):
    lane = lax.broadcasted_iota(jnp.int32, (1, C), 1)
    size = C // HEADS
    return [((lane >= h * size) & (lane < (h + 1) * size)).astype(dtype) for h in range(HEADS)]


def stack_heads(a, masks):
    return jnp.concatenate([a * m for m in masks], 0)


def unstack_heads(a, masks):
    n = a.shape[0] // HEADS
    total = a[:n] * masks[0]
    for h in range(1, HEADS):
        total = total + a[h * n : (h + 1) * n] * masks[h]
    return total


def interleave(chains):
    done = object()
    while chains:
        chains = [chain for chain in chains if next(chain, done) is not done]


def project(n, w):
    proj = dot(n, w)
    scale = (C // HEADS) ** (-0.5)
    q = (proj[:, :C] * scale).astype(BF16)
    k = proj[:, C : 2 * C].astype(BF16)
    v = proj[:, 2 * C : 3 * C].astype(BF16)
    return q, k, v, jax.nn.sigmoid(proj[:, 3 * C :])


def split(scr, wt):
    for i in range(3):
        part = wt.astype(BF16).astype(F32)
        scr[i * HEADS : (i + 1) * HEADS, :] = part
        wt = wt - part
    scr[3 * HEADS : 16, :] = jnp.zeros((16 - 3 * HEADS, C), F32)
    return scr[...].astype(BF16)


def plane_of(n, parts):
    out = dot(parts, n, NT)
    return out[0:4] + out[4:8] + out[8:12]


def core_index():
    return lax.rem(lax.axis_index("dp"), 2)


def rows_of(ref, start, count, stride):
    return ref[pl.ds(start, count, stride=stride), :]


WT_S, WT_E = slice(0, 16), slice(16, 32)
G_S, G_E, G_T, KEPT = slice(0, 1), slice(1, 2), slice(2, 3), slice(3, 4)


def plane_local_kernel(
    x_hbm, gs_hbm, wts_hbm, ge_hbm, wte_hbm, gt_hbm, mask_hbm, w_hbm, cot_hbm, wo_hbm,
    out_ref, args_ref, parts_ref, x_ref, qkv_ref, gating_ref, score_ref, n_ref, cot_ref, wo_ref,
    gs, wts, ge, wte, gt, mask, w_ref, small, scr, sems,
):
    n_dst, rows, _ = out_ref.shape
    moves = [
        (x_hbm, x_ref), (gs_hbm, gs), (wts_hbm, wts), (ge_hbm, ge), (wte_hbm, wte), (gt_hbm, gt), (mask_hbm, mask),
        (w_hbm, w_ref), (cot_hbm, cot_ref), (wo_hbm, wo_ref),
    ]
    copies = [pltpu.make_async_copy(src, dst, sems.at[i]) for i, (src, dst) in enumerate(moves)]
    for copy in copies:
        copy.start()
    for copy in copies[:-3]:
        copy.wait()
    parts_ref[WT_S, :] = split(scr, wts[...])
    parts_ref[WT_E, :] = split(scr, wte[...])
    args_ref[G_S, :] = gs[...]
    args_ref[G_E, :] = ge[...]
    args_ref[G_T, :] = gt[...]
    args_ref[KEPT, :] = mask[...].astype(F32)
    args_ref[4:8, :] = jnp.zeros((4, C), F32)
    xhat, _ = ln_stats(x_ref[...].astype(F32))
    n = (xhat * gs[...]).astype(BF16)
    plane = plane_of(n, parts_ref[WT_S, :])
    small[0:HEADS, :] = plane[:, :C]
    small[HEADS : 2 * HEADS, :] = plane[:, C:]
    out_ref[...] = jnp.broadcast_to(small[...].astype(BF16)[None], (n_dst, rows, C))
    n_ref[...] = n
    copies[-3].wait()
    w = w_ref[...].astype(BF16)
    masks = head_masks(BF16)
    N = 2 * n_dst

    def chain(r):
        part = slice(r * N, (r + 1) * N)
        q, k, v, gating = project(n[part], w)
        yield
        qkv_ref[part, :C] = q
        qkv_ref[part, C : 2 * C] = k
        qkv_ref[part, 2 * C :] = v
        gating_ref[part, :] = gating
        score_ref[part, :] = dot(q, stack_heads(k, masks), NT)

    interleave([chain(r) for r in range(2)])
    for copy in copies[-2:]:
        copy.wait()


def start_forward_kernel(
    recv_ref, x_ref, cot_ref, args_ref, parts_ref, qkv_ref, gating_ref, score_ref, wo_ref,
    send_ref, mix_ref, prob_ref, first_ref,
    fscr, plane, sscr, small,
):
    n_dst = recv_ref.shape[0]
    N = 2 * n_dst
    rows = send_ref.shape[1]
    fscr[...] = recv_ref[...].astype(F32).reshape(n_dst * 8, C)
    for r in range(2):
        for h in range(HEADS):
            plane[pl.ds(h * N + r, n_dst, stride=2), :] = rows_of(fscr, r * 4 + h, n_dst, 8)
    masks = head_masks(BF16)
    kept = args_ref[KEPT, :]
    x = x_ref[...].astype(F32)
    v = qkv_ref[:, 2 * C :]
    gating = gating_ref[...]
    wo = wo_ref[...].astype(BF16)
    parts = parts_ref[WT_E, :]

    def chain(r):
        part = slice(r * N, (r + 1) * N)
        probs = []
        for h in range(HEADS):
            w = jnp.exp(score_ref[part, h * N : (h + 1) * N] + plane[h * N : (h + 1) * N, :]) * kept
            probs.append(w * (1.0 / jnp.sum(w, -1, keepdims=True)))
        prob = jnp.concatenate(probs, 1)
        prob_ref[part, :] = prob
        yield
        mix = dot(prob.astype(BF16), stack_heads(v[part], masks))
        mix_ref[part, :] = mix
        yield
        first = (x[part] + dot((gating[part] * mix).astype(BF16), wo)).astype(BF16)
        first_ref[part, :] = first
        yield
        first = first.astype(F32)
        fscr[part, :] = first
        xhat, _ = ln_stats(first)
        yield
        small[r * HEADS : (r + 1) * HEADS, :] = plane_of((xhat * args_ref[G_E, :]).astype(BF16), parts)
        yield
        for a in range(2):
            sscr[pl.ds(r * 2 + a, n_dst, stride=rows), :] = rows_of(fscr, r * N + a, n_dst, 2)

    interleave([chain(r) for r in range(2)])
    fscr[0 : 2 * N, :] = cot_ref[...].astype(F32)
    for r in range(2):
        for a in range(2):
            sscr[pl.ds(4 + r * 2 + a, n_dst, stride=rows), :] = rows_of(fscr, r * N + a, n_dst, 2)
    for i in range(8):
        sscr[pl.ds(8 + i, n_dst, stride=rows), :] = jnp.broadcast_to(small[i : i + 1, :], (n_dst, C))
    send_ref[...] = sscr[...].reshape(n_dst, rows, C).astype(BF16)


def put_wide(scr, src, value, starts, n_dst, rows):
    for t in range(4):
        src[t * C : (t + 1) * C, :] = value[:, t * C : (t + 1) * C]
        for i in range(2):
            scr[pl.ds(starts[i] + t, n_dst, stride=rows), :] = rows_of(src, t * C + i, n_dst, 2)


def put_narrow(scr, src, row, n_dst, rows, each):
    for i in range(each):
        scr[pl.ds(row + i, n_dst, stride=rows), :] = rows_of(src, i, n_dst, each)


def put_small(scr, row, values, n_dst, rows):
    scr[pl.ds(row, n_dst, stride=rows), :] = jnp.zeros((n_dst, C), F32)
    for e, value in enumerate(values):
        scr[e * rows + row : e * rows + row + 1, :] = value


def end_kernel(
    recv_ref, args_ref, w_ref, wo_ref, wu_ref, wd_ref,
    send_ref, small_ref, hidden_ref, dup_ref, n_ref, n2_ref, cot_ref, dproj_ref, gated_ref, dsecond_ref,
    fscr, zscr, cscr, plane, sscr,
):
    n_dst, in_rows, _ = recv_ref.shape
    N = 2 * n_dst
    fscr[...] = recv_ref[...].astype(F32).reshape(n_dst * in_rows, C)
    for r in range(2):
        for a in range(2):
            zscr[pl.ds(a * N + r, n_dst, stride=2), :] = rows_of(fscr, r * 2 + a, n_dst, in_rows)
            cscr[pl.ds(a * N + r, n_dst, stride=2), :] = rows_of(fscr, 4 + r * 2 + a, n_dst, in_rows)
        for h in range(HEADS):
            plane[pl.ds(h * N + r, n_dst, stride=2), :] = rows_of(fscr, 8 + r * 4 + h, n_dst, in_rows)
    masks = head_masks(BF16)
    masks_f = head_masks(F32)
    gain, gain_t = args_ref[G_E, :], args_ref[G_T, :]
    length = jnp.sum(args_ref[KEPT, :], -1, keepdims=True)
    kept = (lax.broadcasted_iota(jnp.int32, (N, 1), 0).astype(F32) < length).astype(F32)
    w = w_ref[...].astype(BF16)
    wo = wo_ref[...].astype(BF16)
    wu = wu_ref[...].astype(BF16)
    wd = wd_ref[...].astype(BF16)
    results = {}

    def chain(a):
        part = slice(a * N, (a + 1) * N)
        x = zscr[part, :]
        cot = cscr[part, :]
        cot_b = cot.astype(BF16)
        cot_ref[part, :] = cot_b
        xhat, rstd = ln_stats(x)
        n = (xhat * gain).astype(BF16)
        n_ref[part, :] = n
        yield
        q, k, v, gating = project(n, w)
        yield
        ks = stack_heads(k, masks)
        vs = stack_heads(v, masks)
        s = dot(ks, q, NT) + plane[...]
        yield
        probs = []
        for h in range(HEADS):
            e = jnp.exp(s[h * N : (h + 1) * N]) * kept
            probs.append(e * (1.0 / jnp.sum(e, 0, keepdims=True)))
        prob = jnp.concatenate(probs, 0)
        prob_b = prob.astype(BF16)
        yield
        mix = dot(prob_b, vs, TN)
        yield
        gated = (gating * mix).astype(BF16)
        gated_ref[part, :] = gated
        second = (x + dot(gated, wo)).astype(BF16).astype(F32)
        yield
        xhat2, rstd2 = ln_stats(second)
        n2 = (xhat2 * gain_t).astype(BF16)
        n2_ref[part, :] = n2
        dhidden = dot(cot_b, wd, NT).astype(BF16).astype(F32)
        yield
        up = dot(n2, wu)
        yield
        cdf = 0.5 * (1.0 + lax.erf(up * (0.5**0.5)))
        slope = cdf + up * (jnp.exp(-0.5 * up * up) * 0.3989422804014327)
        dup = (dhidden * slope).astype(BF16)
        hidden_ref[part, :] = (up * cdf).astype(BF16)
        dup_ref[part, :] = dup
        yield
        dn2 = dot(dup, wu, NT).astype(BF16).astype(F32)
        yield
        dx2, dgain_t = ln_back(dn2, xhat2, rstd2, gain_t)
        dsecond = (cot + dx2).astype(BF16)
        dsecond_ref[part, :] = dsecond
        yield
        dgated = dot(dsecond, wo, NT).astype(BF16).astype(F32)
        yield
        dmix = (dgated * gating).astype(BF16)
        dprob = dot(vs, dmix, NT).astype(BF16).astype(F32)
        yield
        ds = []
        for h in range(HEADS):
            p = prob[h * N : (h + 1) * N]
            d = dprob[h * N : (h + 1) * N]
            ds.append(p * (d - jnp.sum(p * d, 0, keepdims=True)))
        ds = jnp.concatenate(ds, 0)
        dv = unstack_heads(dot(prob_b, dmix), masks_f)
        yield
        ds_b = ds.astype(BF16)
        dq = dot(ds_b, ks, TN)
        dk = unstack_heads(dot(ds_b, q), masks_f)
        yield
        dproj = project_cotangent(dq, dk, dv, gating, dgated * mix)
        dproj_ref[part, :] = dproj
        dn = dot(dproj, w, NT).astype(BF16).astype(F32)
        yield
        dx, dgain = ln_back(dn, xhat, rstd, gain)
        zscr[part, :] = dsecond.astype(F32) + dx
        results[a] = ds, dgain_t, dgain

    interleave([chain(a) for a in range(2)])
    (ds, dgain_t, dgain), (ds_b, dgain_t_b, dgain_b) = results[0], results[1]
    plane[...] = ds + ds_b
    for r in range(2):
        for h in range(HEADS):
            sscr[pl.ds(r * 8 + h, n_dst, stride=24), :] = rows_of(plane, h * N + r, n_dst, 2)
        for a in range(2):
            sscr[pl.ds(16 + r * 2 + a, n_dst, stride=24), :] = rows_of(zscr, a * N + r, n_dst, 2)
    send_ref[...] = sscr[...].reshape(n_dst, 3, 8, C)[:, :, 0:4, :].astype(BF16)
    small_ref[0:1, :] = dgain_t + dgain_t_b
    small_ref[1:2, :] = dgain + dgain_b
    small_ref[2:8, :] = jnp.zeros((6, C), F32)


def end_weights_kernel(
    hidden_ref, dup_ref, n_ref, n2_ref, cot_ref, dproj_ref, gated_ref, dsecond_ref,
    keep_ref, give_ref,
    down, up, proj, narrow, wscr,
):
    half = keep_ref.shape[0]
    n_dst = half // HALF
    down[...] = dot(hidden_ref[...], cot_ref[...], TN)
    put_narrow(wscr, down, half + 4, n_dst, HALF, 8)
    put_wide(wscr, up, dot(n2_ref[...], dup_ref[...], TN), (8, half), n_dst, HALF)
    put_wide(wscr, proj, dot(n_ref[...], dproj_ref[...], TN), (0, 4), n_dst, HALF)
    narrow[...] = dot(gated_ref[...], dsecond_ref[...], TN)
    for i in range(2):
        wscr[pl.ds(i * half + 12, n_dst, stride=HALF), :] = rows_of(narrow, i, n_dst, 2)
    core = core_index()
    keep_ref[...] = wscr[pl.ds(pl.multiple_of(core * half, 8), half), :]
    give_ref[...] = wscr[pl.ds(pl.multiple_of((1 - core) * half, 8), half), :].astype(BF16)


def project_cotangent(dq, dk, dv, gating, dgating):
    dq = dq.astype(BF16).astype(F32) * (C // HEADS) ** (-0.5)
    dg = dgating * gating * (1.0 - gating)
    return jnp.concatenate([dq.astype(BF16), dk.astype(BF16), dv.astype(BF16), dg.astype(BF16)], 1)


def plane_back(plane, n, p_ref, parts):
    p_ref[...] = jnp.zeros_like(p_ref)
    for i in range(3):
        p_ref[i * HEADS : (i + 1) * HEADS, :] = plane
    p = p_ref[...].astype(BF16)
    return dot(p, parts, TN).astype(BF16).astype(F32), dot(p, n)[0:HEADS]


def first_norm_kernel(first_ref, gating_ref, mix_ref, args_ref, after_ref, xhat_ref, rstd_ref, n_ref, gated_ref):
    xhat, rstd = ln_stats(first_ref[...].astype(F32))
    xhat_ref[...] = xhat
    rstd_ref[...] = jnp.broadcast_to(rstd, rstd_ref.shape)
    n_ref[...] = (xhat * args_ref[G_E, :]).astype(BF16)
    gated_ref[...] = (gating_ref[...] * mix_ref[...]).astype(BF16)


def start_backward_kernel(
    recv_ref, keep_ref, got_ref, small_ref, n_ref, xhat_ref, rstd_ref, ne_ref, gated_ref, qkv_ref, gating_ref, mix_ref, prob_ref, args_ref, parts_ref, wo_ref,
    send_ref, dfirst_ref, dproj_ref,
    fscr, gscr, plane, narrow, wide, sscr, wscr, p_ref,
):
    n_dst = recv_ref.shape[0]
    N = 2 * n_dst
    rows = send_ref.shape[1]
    total = jnp.sum(recv_ref[:, 0:2].astype(F32), 0)
    fscr[:, 0:4, :] = recv_ref[:, 2].astype(F32)
    grads = fscr.reshape(n_dst * 8, C)
    for r in range(2):
        for a in range(2):
            gscr[pl.ds(r * N + a, n_dst, stride=2), :] = rows_of(grads, r * 2 + a, n_dst, 8)
    masks = head_masks(BF16)
    masks_f = head_masks(F32)
    gain_e = args_ref[G_E, :]
    parts = parts_ref[WT_E, :]
    wo = wo_ref[...].astype(BF16)
    results = {}

    def chain(r):
        part = slice(r * N, (r + 1) * N)
        xhat, rstd = xhat_ref[part, :], rstd_ref[part, :]
        n_e = ne_ref[part, :]
        dn_e, dbias_e = plane_back(total[r], n_e, p_ref.at[r], parts)
        yield
        dxe, dgain_e = ln_back(dn_e, xhat, rstd, gain_e)
        dfirst = (gscr[part, :] + dxe).astype(BF16)
        dfirst_ref[part, :] = dfirst
        yield
        q = qkv_ref[part, :C]
        ks = stack_heads(qkv_ref[part, C : 2 * C], masks)
        vs = stack_heads(qkv_ref[part, 2 * C :], masks)
        gating = gating_ref[part, :]
        mix = mix_ref[part, :]
        prob = prob_ref[part, :]
        dgated = dot(dfirst, wo, NT).astype(BF16).astype(F32)
        yield
        dmix = (dgated * gating).astype(BF16)
        dprob = dot(dmix, vs, NT).astype(BF16).astype(F32)
        yield
        ds = []
        for h in range(HEADS):
            p = prob[:, h * N : (h + 1) * N]
            d = dprob[:, h * N : (h + 1) * N]
            ds.append(p * (d - jnp.sum(p * d, -1, keepdims=True)))
        dv = unstack_heads(dot(prob.astype(BF16), dmix, TN), masks_f)
        yield
        ds_b = jnp.concatenate(ds, 1).astype(BF16)
        dq = dot(ds_b, ks)
        dk = unstack_heads(dot(ds_b, q, TN), masks_f)
        yield
        dproj_ref[part, :] = project_cotangent(dq, dk, dv, gating, dgated * mix)
        results[r] = ds, dgain_e, dbias_e

    interleave([chain(r) for r in range(2)])
    (ds, dgain_e, dbias_e), (ds_b, dgain_b, dbias_b) = results[0], results[1]
    dgain_e, dbias_e = dgain_e + dgain_b, dbias_e + dbias_b
    for h in range(HEADS):
        plane[h * N : (h + 1) * N, :] = ds[h] + ds_b[h]
    for r in range(2):
        for h in range(HEADS):
            sscr[pl.ds(r * 4 + h, n_dst, stride=rows), :] = rows_of(plane, h * N + r, n_dst, 2)
    narrow[0:C, :] = dot(gated_ref[...], dfirst_ref[...], TN)
    put_narrow(sscr, narrow, 16, n_dst, rows, 2)
    put_wide(sscr, wide, dot(n_ref[...], dproj_ref[...], TN), (8, 12), n_dst, rows)
    smalls = [small_ref[0:1, :], small_ref[1:2, :], dgain_e] + [dbias_e[h : h + 1] for h in range(HEADS)]
    put_small(sscr, 18, smalls, n_dst, rows)
    wscr[...] = keep_ref[...] + got_ref[...].astype(F32)
    for i in range(HALF):
        sscr[pl.ds(19 + i, n_dst, stride=rows), :] = rows_of(wscr, i, n_dst, HALF)
    send_ref[...] = sscr[...].reshape(n_dst, rows, C).astype(BF16)


def start_plane_kernel(recv_ref, dproj_ref, x_ref, w_ref, args_ref, parts_ref, dn_ref, dn_plane_ref, part_ref, p_ref):
    total = jnp.sum(recv_ref[...].astype(F32), 0)
    xhat, _ = ln_stats(x_ref[...].astype(F32))
    n = (xhat * args_ref[G_S, :]).astype(BF16)
    dn = dot(dproj_ref[...], w_ref[...].astype(BF16), NT).astype(BF16)
    dn_ref[...] = dn
    N = n.shape[0] // 2
    backs = [
        plane_back(total[r * HEADS : (r + 1) * HEADS], n[r * N : (r + 1) * N], p_ref.at[r], parts_ref[WT_S, :])
        for r in range(2)
    ]
    dn_plane = jnp.concatenate([back[0] for back in backs], 0)
    dbias = backs[0][1] + backs[1][1]
    dn_plane_ref[...] = dn_plane.astype(BF16)
    part_ref[0:11, :] = total[8:19]
    part_ref[11:15, :] = dbias
    part_ref[15:16, :] = jnp.sum((dn_plane + dn.astype(F32)) * xhat, 0, keepdims=True)
    part_ref[16 : 16 + HALF, :] = total[19 : 19 + HALF]
    part_ref[16 + HALF : 32, :] = jnp.zeros((16 - HALF, C), F32)


def grad_kernel(dn_ref, dn_plane_ref, dfirst_ref, x_ref, args_ref, grad_ref):
    xhat, rstd = ln_stats(x_ref[...].astype(F32))
    dx, _ = ln_back(dn_ref[...].astype(F32), xhat, rstd, args_ref[G_S, :])
    dx_plane, _ = ln_back(dn_plane_ref[...].astype(F32), xhat, rstd, args_ref[G_S, :])
    grad_ref[...] = (dfirst_ref[...].astype(F32) + dx + dx_plane).astype(BF16)


def core_sum_kernel(own_ref, other_ref, out_ref):
    out_ref[0:16, :] = own_ref[0:16, :] + other_ref[0:16, :]
    out_ref[16:32, :] = own_ref[16:32, :]


def spread_kernel(own_ref, far_ref, out_ref, scr):
    total = own_ref[...] + far_ref[...]
    scr[0:8, :] = jnp.where(core_index() == 0, total[0:8], total[8:16])
    scr[8:24, :] = total[16:32]
    out_ref[...] = jnp.broadcast_to(scr[...].astype(BF16)[None], out_ref.shape)


def finish_kernel(
    factor, recv_ref, other_ref,
    gs_out, ps_out, bs_out, os_out, ge_out, pe_out, be_out, oe_out, gt_out, up_out, down_out,
    gs_ref, ps_ref, bs_ref, os_ref, ge_ref, pe_ref, be_ref, oe_ref, gt_ref, up_ref, down_ref,
    fscr, block, sems,
):
    copies = []

    def leave(ref, out):
        copies.append(pltpu.make_async_copy(ref, out, sems.at[len(copies)]))
        copies[-1].start()

    n_dst, half, _ = recv_ref.shape
    size = n_dst * half
    core = core_index()
    for index, ref in ((core, recv_ref), (1 - core, other_ref)):
        fscr[pl.ds(pl.multiple_of(index * size, 8), size), :] = ref[...].astype(F32).reshape(size, C) * factor

    def rows(row):
        return rows_of(fscr, row, n_dst, half)

    def wide(ref, starts):
        for t in range(4):
            for i in range(2):
                block[pl.ds(i, n_dst, stride=2), :] = rows(starts[i] + t)
            ref[:, t * C : (t + 1) * C] = block[...]

    def narrow(ref, starts):
        for i, start in enumerate(starts):
            ref[pl.ds(i, n_dst, stride=len(starts)), :] = rows(start)

    def one(e, row):
        start = e * half + row
        return fscr[start : start + 1, :]

    wide(ps_ref, (0, 4))
    leave(ps_ref, ps_out)
    wide(pe_ref, (8, 12))
    leave(pe_ref, pe_out)
    wide(up_ref, (16, size + 8))
    leave(up_ref, up_out)
    narrow(down_ref, range(size + 12, size + 20))
    leave(down_ref, down_out)
    narrow(os_ref, (size, size + 1))
    leave(os_ref, os_out)
    narrow(oe_ref, (20, size + 20))
    leave(oe_ref, oe_out)
    for h in range(HEADS):
        bs_ref[h : h + 1, :] = jnp.sum(rows(size + 3 + h), 0, keepdims=True)
        be_ref[h : h + 1, :] = one(3 + h, size + 2)
    gt_ref[...] = one(0, size + 2)
    ge_ref[...] = one(1, size + 2) + one(2, size + 2)
    gs_ref[...] = jnp.sum(rows(size + 7), 0, keepdims=True)
    for ref, out in ((bs_ref, bs_out), (be_ref, be_out), (gt_ref, gt_out), (ge_ref, ge_out), (gs_ref, gs_out)):
        leave(ref, out)
    for copy in copies:
        copy.wait()


def shape(dims, dtype=F32):
    return jax.ShapeDtypeStruct(dims, dtype)


def call(body, out_shape, scratch, *operands, in_hbm=(), out=pltpu.VMEM):
    many = isinstance(out_shape, (list, tuple))
    whole = pl.BlockSpec(memory_space=out)
    spaces = [pltpu.HBM if i in in_hbm else pltpu.VMEM for i in range(len(operands))]
    operands = [pltpu.with_memory_space_constraint(a, m) if m is pltpu.HBM else a for a, m in zip(operands, spaces)]
    return pl.pallas_call(
        body,
        out_shape=out_shape,
        in_specs=[pl.BlockSpec(memory_space=m) for m in spaces],
        out_specs=[whole] * len(out_shape) if many else whole,
        scratch_shapes=[pltpu.VMEM(s, F32) if isinstance(s, tuple) else s for s in scratch],
        compiler_params=pltpu.CompilerParams(vmem_limit_bytes=VMEM_LIMIT),
    )(*operands)


def swap(buffer):
    return lax.all_to_all(buffer, "dap", split_axis=0, concat_axis=0, tiled=True)


def local(
    pair_input, cotangent, residue_mask, gain_start, proj_start, bias_start, output_start,
    gain_end, proj_end, bias_end, output_end, gain_transition, transition_up, transition_down,
):
    _, _, N, _ = pair_input.shape
    n_dst = N // 2
    x = pair_input.reshape(2 * N, C)
    cot = cotangent.reshape(2 * N, C)
    g_s, g_e, g_t = (g.reshape(1, C) for g in (gain_start, gain_end, gain_transition))
    wt_s, wt_e = bias_start.T, bias_end.T
    tokens = (2 * N, C)
    wide = (C, 4 * C)

    send, args, parts, x_in, qkv, gating, score, n, cot, wo = call(
        plane_local_kernel,
        [shape((n_dst, 8, C), BF16), shape((8, C)), shape((32, C), BF16), shape(tokens, BF16), shape((2 * N, 3 * C), BF16),
         shape(tokens), shape((2 * N, HEADS * N)), shape(tokens, BF16), shape(tokens, BF16), shape((C, C))],
        [(1, C), (HEADS, C), (1, C), (HEADS, C), (1, C), pltpu.VMEM((1, C), jnp.int32), wide,
         (8, C), (16, C), pltpu.SemaphoreType.DMA((10,))],
        x, g_s, wt_s, g_e, wt_e, g_t, residue_mask, proj_start, cot, output_start,
        in_hbm=range(10),
    )
    recv = swap(send)
    send, mix, prob, first = call(
        start_forward_kernel,
        [shape((n_dst, 16, C), BF16), shape(tokens), shape((2 * N, HEADS * N)), shape(tokens, BF16)],
        [(n_dst * 8, C), (HEADS * N, N), (n_dst * 16, C), (8, C)],
        recv, x_in, cot, args, parts, qkv, gating, score, wo,
    )
    recv = swap(send)
    n_dp = lax.axis_size("dp")
    to_core = [(i, i ^ 1) for i in range(n_dp)]
    half = (n_dst * HALF, C)
    hidden = (2 * N, 4 * C)
    send, small, *saved = call(
        end_kernel,
        [shape((n_dst, 3, 4, C), BF16), shape((8, C)), shape(hidden, BF16), shape(hidden, BF16), shape(tokens, BF16),
         shape(tokens, BF16), shape(tokens, BF16), shape(hidden, BF16), shape(tokens, BF16), shape(tokens, BF16)],
        [(n_dst * 16, C), tokens, tokens, (HEADS * N, N), (n_dst * 24, C)],
        recv, args, proj_end, output_end, transition_up, transition_down,
    )
    recv = swap(send)
    keep, give = call(
        end_weights_kernel,
        [shape(half), shape(half, BF16)],
        [(4 * C, C), (4 * C, C), (4 * C, C), (C, C), (n_dst * 2 * HALF, C)],
        *saved,
    )
    got = lax.ppermute(give, "dp", to_core)
    normed = call(
        first_norm_kernel,
        [shape(tokens), shape(tokens), shape(tokens, BF16), shape(tokens, BF16)],
        [],
        first, gating, mix, args, small,
    )
    send, dfirst, dproj = call(
        start_backward_kernel,
        [shape((n_dst, 32, C), BF16), shape(tokens, BF16), shape(hidden, BF16)],
        [(n_dst, 8, C), tokens, (HEADS * N, N), (C, C), (4 * C, C), (n_dst * 32, C), half, (2, 16, C)],
        recv, keep, got, small, n, *normed, qkv, gating, mix, prob, args, parts, wo,
    )
    recv = swap(send)
    dn, dn_plane, part = call(
        start_plane_kernel,
        [shape(tokens, BF16), shape(tokens, BF16), shape((32, C))],
        [(2, 16, C)],
        recv, dproj, x, proj_start, args, parts,
    )
    part = call(core_sum_kernel, shape((32, C)), [], part, lax.ppermute(part, "dp", to_core))
    far = lax.ppermute(part, "dp", [(i, i ^ 2) for i in range(n_dp)])
    grad = call(grad_kernel, shape(tokens, BF16), [], dn, dn_plane, dfirst, x, args)
    grad, far = lax.optimization_barrier((grad, far))
    send = call(spread_kernel, shape((n_dst, 24, C), BF16), [(24, C)], part, far)
    recv = swap(send)
    other = lax.ppermute(recv, "dp", to_core)
    factor = 1.0 / (n_dp * N)
    vector, bias, square, tall = (1, C), (HEADS, C), (C, C), (4 * C, C)
    sizes = [vector, wide, bias, square, vector, wide, bias, square, vector, wide, tall]
    gs, ps, bs, os, ge, pe, be, oe, gt, up, down = call(
        functools.partial(finish_kernel, factor),
        [shape(size) for size in sizes],
        [*sizes, (n_dst * 48, C), square, pltpu.SemaphoreType.DMA((len(sizes),))],
        recv, other,
        out=pltpu.HBM,
    )
    return (
        grad.reshape(1, 2, N, C), gs.reshape(C), ps, bs.T, os, ge.reshape(C), pe, be.T, oe, gt.reshape(C), up, down,
    )


def solution(mesh):
    rows = P("dp", "dap", None, None)
    in_specs = (rows, rows, P("dp", None)) + (P(),) * 11
    out_specs = (rows,) + (P(),) * 11
    return jax.shard_map(local, mesh=mesh, in_specs=in_specs, out_specs=out_specs, check_vma=False)
```

```python
import functools

import jax
import jax.numpy as jnp
from jax import lax
from jax.experimental import pallas as pl
from jax.experimental.pallas import tpu as pltpu
from jax.sharding import PartitionSpec as P

HEADS = 4
EPS = 1e-05
F32 = jnp.float32
BF16 = jnp.bfloat16
C = 128
HALF = 13
VMEM_LIMIT = 48 * 1024 * 1024


def dot(a, b, contract=((1,), (0,))):
    return lax.dot_general(a, b, (contract, ((), ())), preferred_element_type=F32)


NN = ((1,), (0,))
NT = ((1,), (1,))
TN = ((0,), (0,))


def ln_stats(x):
    centre = x - jnp.mean(x, -1, keepdims=True)
    spread = jnp.mean(centre * centre, -1, keepdims=True)
    rstd = lax.rsqrt(spread + EPS)
    return centre * rstd, rstd


def ln_back(dn, xhat, rstd, gain):
    t = dn * gain
    m1 = jnp.mean(t, -1, keepdims=True)
    m2 = jnp.mean(t * xhat, -1, keepdims=True)
    dx = rstd * (t - m1 - xhat * m2)
    return dx.astype(BF16).astype(F32), jnp.sum(dn * xhat, 0, keepdims=True)


def head_masks(dtype):
    lane = lax.broadcasted_iota(jnp.int32, (1, C), 1)
    size = C // HEADS
    return [((lane >= h * size) & (lane < (h + 1) * size)).astype(dtype) for h in range(HEADS)]


def stack_heads(a, masks):
    return jnp.concatenate([a * m for m in masks], 0)


def unstack_heads(a, masks):
    n = a.shape[0] // HEADS
    total = a[:n] * masks[0]
    for h in range(1, HEADS):
        total = total + a[h * n : (h + 1) * n] * masks[h]
    return total


def interleave(chains):
    done = object()
    while chains:
        chains = [chain for chain in chains if next(chain, done) is not done]


def project(n, w):
    proj = dot(n, w)
    scale = (C // HEADS) ** (-0.5)
    q = (proj[:, :C] * scale).astype(BF16)
    k = proj[:, C : 2 * C].astype(BF16)
    v = proj[:, 2 * C : 3 * C].astype(BF16)
    return q, k, v, jax.nn.sigmoid(proj[:, 3 * C :])


def split(scr, wt):
    for i in range(3):
        part = wt.astype(BF16).astype(F32)
        scr[i * HEADS : (i + 1) * HEADS, :] = part
        wt = wt - part
    scr[3 * HEADS : 16, :] = jnp.zeros((16 - 3 * HEADS, C), F32)
    return scr[...].astype(BF16)


def plane_of(n, parts):
    out = dot(parts, n, NT)
    return out[0:4] + out[4:8] + out[8:12]


def core_index():
    return lax.rem(lax.axis_index("dp"), 2)


def rows_of(ref, start, count, stride):
    return ref[pl.ds(start, count, stride=stride), :]


WT_S, WT_E = slice(0, 16), slice(16, 32)
G_S, G_E, G_T, KEPT = slice(0, 1), slice(1, 2), slice(2, 3), slice(3, 4)


def plane_local_kernel(
    x_hbm, gs_hbm, wts_hbm, ge_hbm, wte_hbm, gt_hbm, mask_hbm, w_hbm, cot_hbm, wo_hbm,
    out_ref, args_ref, parts_ref, x_ref, qkv_ref, gating_ref, score_ref, n_ref, cot_ref, wo_ref,
    gs, wts, ge, wte, gt, mask, w_ref, small, scr, sems,
):
    n_dst, rows, _ = out_ref.shape
    moves = [
        (x_hbm, x_ref), (gs_hbm, gs), (wts_hbm, wts), (ge_hbm, ge), (wte_hbm, wte), (gt_hbm, gt), (mask_hbm, mask),
        (w_hbm, w_ref), (cot_hbm, cot_ref), (wo_hbm, wo_ref),
    ]
    copies = [pltpu.make_async_copy(src, dst, sems.at[i]) for i, (src, dst) in enumerate(moves)]
    for copy in copies:
        copy.start()
    for copy in copies[:-3]:
        copy.wait()
    parts_ref[WT_S, :] = split(scr, wts[...])
    parts_ref[WT_E, :] = split(scr, wte[...])
    args_ref[G_S, :] = gs[...]
    args_ref[G_E, :] = ge[...]
    args_ref[G_T, :] = gt[...]
    args_ref[KEPT, :] = mask[...].astype(F32)
    args_ref[4:8, :] = jnp.zeros((4, C), F32)
    xhat, _ = ln_stats(x_ref[...].astype(F32))
    n = (xhat * gs[...]).astype(BF16)
    plane = plane_of(n, parts_ref[WT_S, :])
    small[0:HEADS, :] = plane[:, :C]
    small[HEADS : 2 * HEADS, :] = plane[:, C:]
    out_ref[...] = jnp.broadcast_to(small[...].astype(BF16)[None], (n_dst, rows, C))
    n_ref[...] = n
    copies[-3].wait()
    w = w_ref[...].astype(BF16)
    masks = head_masks(BF16)
    N = 2 * n_dst

    def chain(r):
        part = slice(r * N, (r + 1) * N)
        q, k, v, gating = project(n[part], w)
        yield
        qkv_ref[part, :C] = q
        qkv_ref[part, C : 2 * C] = k
        qkv_ref[part, 2 * C :] = v
        gating_ref[part, :] = gating
        score_ref[part, :] = dot(q, stack_heads(k, masks), NT)

    interleave([chain(r) for r in range(2)])
    for copy in copies[-2:]:
        copy.wait()


def start_forward_kernel(
    recv_ref, x_ref, cot_ref, args_ref, parts_ref, qkv_ref, gating_ref, score_ref, wo_ref,
    send_ref, mix_ref, prob_ref, first_ref,
    fscr, plane, sscr, small,
):
    n_dst = recv_ref.shape[0]
    N = 2 * n_dst
    rows = send_ref.shape[1]
    fscr[...] = recv_ref[...].astype(F32).reshape(n_dst * 8, C)
    for r in range(2):
        for h in range(HEADS):
            plane[pl.ds(h * N + r, n_dst, stride=2), :] = rows_of(fscr, r * 4 + h, n_dst, 8)
    masks = head_masks(BF16)
    kept = args_ref[KEPT, :]
    x = x_ref[...].astype(F32)
    v = qkv_ref[:, 2 * C :]
    gating = gating_ref[...]
    wo = wo_ref[...].astype(BF16)
    parts = parts_ref[WT_E, :]

    def chain(r):
        part = slice(r * N, (r + 1) * N)
        probs = []
        for h in range(HEADS):
            w = jnp.exp(score_ref[part, h * N : (h + 1) * N] + plane[h * N : (h + 1) * N, :]) * kept
            probs.append(w * (1.0 / jnp.sum(w, -1, keepdims=True)))
        prob = jnp.concatenate(probs, 1)
        prob_ref[part, :] = prob
        yield
        mix = dot(prob.astype(BF16), stack_heads(v[part], masks))
        mix_ref[part, :] = mix
        yield
        first = (x[part] + dot((gating[part] * mix).astype(BF16), wo)).astype(BF16)
        first_ref[part, :] = first
        yield
        first = first.astype(F32)
        fscr[part, :] = first
        xhat, _ = ln_stats(first)
        yield
        small[r * HEADS : (r + 1) * HEADS, :] = plane_of((xhat * args_ref[G_E, :]).astype(BF16), parts)
        yield
        for a in range(2):
            sscr[pl.ds(r * 2 + a, n_dst, stride=rows), :] = rows_of(fscr, r * N + a, n_dst, 2)

    interleave([chain(r) for r in range(2)])
    fscr[0 : 2 * N, :] = cot_ref[...].astype(F32)
    for r in range(2):
        for a in range(2):
            sscr[pl.ds(4 + r * 2 + a, n_dst, stride=rows), :] = rows_of(fscr, r * N + a, n_dst, 2)
    for i in range(8):
        sscr[pl.ds(8 + i, n_dst, stride=rows), :] = jnp.broadcast_to(small[i : i + 1, :], (n_dst, C))
    send_ref[...] = sscr[...].reshape(n_dst, rows, C).astype(BF16)


def put_wide(scr, src, value, starts, n_dst, rows):
    for t in range(4):
        src[t * C : (t + 1) * C, :] = value[:, t * C : (t + 1) * C]
        for i in range(2):
            scr[pl.ds(starts[i] + t, n_dst, stride=rows), :] = rows_of(src, t * C + i, n_dst, 2)


def put_narrow(scr, src, row, n_dst, rows, each):
    for i in range(each):
        scr[pl.ds(row + i, n_dst, stride=rows), :] = rows_of(src, i, n_dst, each)


def put_small(scr, row, values, n_dst, rows):
    scr[pl.ds(row, n_dst, stride=rows), :] = jnp.zeros((n_dst, C), F32)
    for e, value in enumerate(values):
        scr[e * rows + row : e * rows + row + 1, :] = value


def end_kernel(
    recv_ref, args_ref, w_ref, wo_ref, wu_ref, wd_ref,
    send_ref, small_ref, hidden_ref, dup_ref, n_ref, n2_ref, cot_ref, dproj_ref, gated_ref, dsecond_ref,
    fscr, zscr, cscr, plane, sscr,
):
    n_dst, in_rows, _ = recv_ref.shape
    N = 2 * n_dst
    fscr[...] = recv_ref[...].astype(F32).reshape(n_dst * in_rows, C)
    for r in range(2):
        for a in range(2):
            zscr[pl.ds(a * N + r, n_dst, stride=2), :] = rows_of(fscr, r * 2 + a, n_dst, in_rows)
            cscr[pl.ds(a * N + r, n_dst, stride=2), :] = rows_of(fscr, 4 + r * 2 + a, n_dst, in_rows)
        for h in range(HEADS):
            plane[pl.ds(h * N + r, n_dst, stride=2), :] = rows_of(fscr, 8 + r * 4 + h, n_dst, in_rows)
    masks = head_masks(BF16)
    masks_f = head_masks(F32)
    gain, gain_t = args_ref[G_E, :], args_ref[G_T, :]
    length = jnp.sum(args_ref[KEPT, :], -1, keepdims=True)
    kept = (lax.broadcasted_iota(jnp.int32, (N, 1), 0).astype(F32) < length).astype(F32)
    w = w_ref[...].astype(BF16)
    wo = wo_ref[...].astype(BF16)
    wu = wu_ref[...].astype(BF16)
    wd = wd_ref[...].astype(BF16)
    results = {}

    def chain(a):
        part = slice(a * N, (a + 1) * N)
        x = zscr[part, :]
        cot = cscr[part, :]
        cot_b = cot.astype(BF16)
        cot_ref[part, :] = cot_b
        xhat, rstd = ln_stats(x)
        n = (xhat * gain).astype(BF16)
        n_ref[part, :] = n
        yield
        q, k, v, gating = project(n, w)
        yield
        ks = stack_heads(k, masks)
        vs = stack_heads(v, masks)
        s = dot(ks, q, NT) + plane[...]
        yield
        probs = []
        for h in range(HEADS):
            e = jnp.exp(s[h * N : (h + 1) * N]) * kept
            probs.append(e * (1.0 / jnp.sum(e, 0, keepdims=True)))
        prob = jnp.concatenate(probs, 0)
        prob_b = prob.astype(BF16)
        yield
        mix = dot(prob_b, vs, TN)
        yield
        gated = (gating * mix).astype(BF16)
        gated_ref[part, :] = gated
        second = (x + dot(gated, wo)).astype(BF16).astype(F32)
        yield
        xhat2, rstd2 = ln_stats(second)
        n2 = (xhat2 * gain_t).astype(BF16)
        n2_ref[part, :] = n2
        dhidden = dot(cot_b, wd, NT).astype(BF16).astype(F32)
        yield
        up = dot(n2, wu)
        yield
        cdf = 0.5 * (1.0 + lax.erf(up * (0.5**0.5)))
        slope = cdf + up * (jnp.exp(-0.5 * up * up) * 0.3989422804014327)
        dup = (dhidden * slope).astype(BF16)
        hidden_ref[part, :] = (up * cdf).astype(BF16)
        dup_ref[part, :] = dup
        yield
        dn2 = dot(dup, wu, NT).astype(BF16).astype(F32)
        yield
        dx2, dgain_t = ln_back(dn2, xhat2, rstd2, gain_t)
        dsecond = (cot + dx2).astype(BF16)
        dsecond_ref[part, :] = dsecond
        yield
        dgated = dot(dsecond, wo, NT).astype(BF16).astype(F32)
        yield
        dmix = (dgated * gating).astype(BF16)
        dprob = dot(vs, dmix, NT).astype(BF16).astype(F32)
        yield
        ds = []
        for h in range(HEADS):
            p = prob[h * N : (h + 1) * N]
            d = dprob[h * N : (h + 1) * N]
            ds.append(p * (d - jnp.sum(p * d, 0, keepdims=True)))
        ds = jnp.concatenate(ds, 0)
        dv = unstack_heads(dot(prob_b, dmix), masks_f)
        yield
        ds_b = ds.astype(BF16)
        dq = dot(ds_b, ks, TN)
        dk = unstack_heads(dot(ds_b, q), masks_f)
        yield
        dproj = project_cotangent(dq, dk, dv, gating, dgated * mix)
        dproj_ref[part, :] = dproj
        dn = dot(dproj, w, NT).astype(BF16).astype(F32)
        yield
        dx, dgain = ln_back(dn, xhat, rstd, gain)
        zscr[part, :] = dsecond.astype(F32) + dx
        results[a] = ds, dgain_t, dgain

    interleave([chain(a) for a in range(2)])
    (ds, dgain_t, dgain), (ds_b, dgain_t_b, dgain_b) = results[0], results[1]
    plane[...] = ds + ds_b
    for r in range(2):
        for h in range(HEADS):
            sscr[pl.ds(r * 8 + h, n_dst, stride=24), :] = rows_of(plane, h * N + r, n_dst, 2)
        for a in range(2):
            sscr[pl.ds(16 + r * 2 + a, n_dst, stride=24), :] = rows_of(zscr, a * N + r, n_dst, 2)
    send_ref[...] = sscr[...].reshape(n_dst, 3, 8, C)[:, :, 0:4, :].astype(BF16)
    small_ref[0:1, :] = dgain_t + dgain_t_b
    small_ref[1:2, :] = dgain + dgain_b
    small_ref[2:8, :] = jnp.zeros((6, C), F32)


def end_weights_kernel(
    hidden_ref, dup_ref, n_ref, n2_ref, cot_ref, dproj_ref, gated_ref, dsecond_ref,
    keep_ref, give_ref,
    down, up, proj, narrow, wscr,
):
    half = keep_ref.shape[0]
    n_dst = half // HALF
    down[...] = dot(hidden_ref[...], cot_ref[...], TN)
    put_narrow(wscr, down, half + 4, n_dst, HALF, 8)
    put_wide(wscr, up, dot(n2_ref[...], dup_ref[...], TN), (8, half), n_dst, HALF)
    put_wide(wscr, proj, dot(n_ref[...], dproj_ref[...], TN), (0, 4), n_dst, HALF)
    narrow[...] = dot(gated_ref[...], dsecond_ref[...], TN)
    for i in range(2):
        wscr[pl.ds(i * half + 12, n_dst, stride=HALF), :] = rows_of(narrow, i, n_dst, 2)
    core = core_index()
    keep_ref[...] = wscr[pl.ds(pl.multiple_of(core * half, 8), half), :]
    give_ref[...] = wscr[pl.ds(pl.multiple_of((1 - core) * half, 8), half), :].astype(BF16)


def project_cotangent(dq, dk, dv, gating, dgating):
    dq = dq.astype(BF16).astype(F32) * (C // HEADS) ** (-0.5)
    dg = dgating * gating * (1.0 - gating)
    return jnp.concatenate([dq.astype(BF16), dk.astype(BF16), dv.astype(BF16), dg.astype(BF16)], 1)


def plane_back(plane, n, p_ref, parts):
    p_ref[...] = jnp.zeros_like(p_ref)
    for i in range(3):
        p_ref[i * HEADS : (i + 1) * HEADS, :] = plane
    p = p_ref[...].astype(BF16)
    return dot(p, parts, TN).astype(BF16).astype(F32), dot(p, n)[0:HEADS]


def start_backward_kernel(
    recv_ref, keep_ref, got_ref, small_ref, n_ref, first_ref, qkv_ref, gating_ref, mix_ref, prob_ref, args_ref, parts_ref, wo_ref,
    send_ref, dfirst_ref, dproj_ref,
    fscr, gscr, plane, narrow, wide, sscr, wscr, p_ref,
):
    n_dst = recv_ref.shape[0]
    N = 2 * n_dst
    rows = send_ref.shape[1]
    total = jnp.sum(recv_ref[:, 0:2].astype(F32), 0)
    fscr[:, 0:4, :] = recv_ref[:, 2].astype(F32)
    grads = fscr.reshape(n_dst * 8, C)
    for r in range(2):
        for a in range(2):
            gscr[pl.ds(r * N + a, n_dst, stride=2), :] = rows_of(grads, r * 2 + a, n_dst, 8)
    masks = head_masks(BF16)
    masks_f = head_masks(F32)
    gain_e = args_ref[G_E, :]
    parts = parts_ref[WT_E, :]
    wo = wo_ref[...].astype(BF16)
    results = {}

    def chain(r):
        part = slice(r * N, (r + 1) * N)
        xhat, rstd = ln_stats(first_ref[part, :].astype(F32))
        n_e = (xhat * gain_e).astype(BF16)
        yield
        dn_e, dbias_e = plane_back(total[r], n_e, p_ref.at[r], parts)
        yield
        dxe, dgain_e = ln_back(dn_e, xhat, rstd, gain_e)
        dfirst = (gscr[part, :] + dxe).astype(BF16)
        dfirst_ref[part, :] = dfirst
        yield
        q = qkv_ref[part, :C]
        ks = stack_heads(qkv_ref[part, C : 2 * C], masks)
        vs = stack_heads(qkv_ref[part, 2 * C :], masks)
        gating = gating_ref[part, :]
        mix = mix_ref[part, :]
        prob = prob_ref[part, :]
        dgated = dot(dfirst, wo, NT).astype(BF16).astype(F32)
        yield
        dmix = (dgated * gating).astype(BF16)
        dprob = dot(dmix, vs, NT).astype(BF16).astype(F32)
        yield
        ds = []
        for h in range(HEADS):
            p = prob[:, h * N : (h + 1) * N]
            d = dprob[:, h * N : (h + 1) * N]
            ds.append(p * (d - jnp.sum(p * d, -1, keepdims=True)))
        dv = unstack_heads(dot(prob.astype(BF16), dmix, TN), masks_f)
        yield
        ds_b = jnp.concatenate(ds, 1).astype(BF16)
        dq = dot(ds_b, ks)
        dk = unstack_heads(dot(ds_b, q, TN), masks_f)
        yield
        dproj_ref[part, :] = project_cotangent(dq, dk, dv, gating, dgated * mix)
        results[r] = ds, dgain_e, dbias_e

    interleave([chain(r) for r in range(2)])
    (ds, dgain_e, dbias_e), (ds_b, dgain_b, dbias_b) = results[0], results[1]
    dgain_e, dbias_e = dgain_e + dgain_b, dbias_e + dbias_b
    for h in range(HEADS):
        plane[h * N : (h + 1) * N, :] = ds[h] + ds_b[h]
    for r in range(2):
        for h in range(HEADS):
            sscr[pl.ds(r * 4 + h, n_dst, stride=rows), :] = rows_of(plane, h * N + r, n_dst, 2)
    gated = (gating_ref[...] * mix_ref[...]).astype(BF16)
    narrow[0:C, :] = dot(gated, dfirst_ref[...], TN)
    put_narrow(sscr, narrow, 16, n_dst, rows, 2)
    put_wide(sscr, wide, dot(n_ref[...], dproj_ref[...], TN), (8, 12), n_dst, rows)
    smalls = [small_ref[0:1, :], small_ref[1:2, :], dgain_e] + [dbias_e[h : h + 1] for h in range(HEADS)]
    put_small(sscr, 18, smalls, n_dst, rows)
    wscr[...] = keep_ref[...] + got_ref[...].astype(F32)
    for i in range(HALF):
        sscr[pl.ds(19 + i, n_dst, stride=rows), :] = rows_of(wscr, i, n_dst, HALF)
    send_ref[...] = sscr[...].reshape(n_dst, rows, C).astype(BF16)


def start_plane_kernel(recv_ref, dproj_ref, x_ref, w_ref, args_ref, parts_ref, dn_ref, dn_plane_ref, part_ref, half_ref, p_ref):
    total = jnp.sum(recv_ref[...].astype(F32), 0)
    xhat, _ = ln_stats(x_ref[...].astype(F32))
    n = (xhat * args_ref[G_S, :]).astype(BF16)
    dn = dot(dproj_ref[...], w_ref[...].astype(BF16), NT).astype(BF16)
    dn_ref[...] = dn
    N = n.shape[0] // 2
    backs = [
        plane_back(total[r * HEADS : (r + 1) * HEADS], n[r * N : (r + 1) * N], p_ref.at[r], parts_ref[WT_S, :])
        for r in range(2)
    ]
    dn_plane = jnp.concatenate([back[0] for back in backs], 0)
    dbias = backs[0][1] + backs[1][1]
    dn_plane_ref[...] = dn_plane.astype(BF16)
    part_ref[0:11, :] = total[8:19]
    part_ref[11:15, :] = dbias
    part_ref[15:16, :] = jnp.sum((dn_plane + dn.astype(F32)) * xhat, 0, keepdims=True)
    half_ref[0:HALF, :] = total[19 : 19 + HALF]
    half_ref[HALF:16, :] = jnp.zeros((16 - HALF, C), F32)


def grad_kernel(dn_ref, dn_plane_ref, dfirst_ref, x_ref, args_ref, grad_ref):
    xhat, rstd = ln_stats(x_ref[...].astype(F32))
    dx, _ = ln_back(dn_ref[...].astype(F32), xhat, rstd, args_ref[G_S, :])
    dx_plane, _ = ln_back(dn_plane_ref[...].astype(F32), xhat, rstd, args_ref[G_S, :])
    grad_ref[...] = (dfirst_ref[...].astype(F32) + dx + dx_plane).astype(BF16)


def core_sum_kernel(own_ref, other_ref, half_ref, out_ref):
    out_ref[0:16, :] = own_ref[...] + other_ref[...]
    out_ref[16:32, :] = half_ref[...]


def spread_kernel(own_ref, far_ref, out_ref, scr):
    total = own_ref[...] + far_ref[...]
    scr[0:8, :] = jnp.where(core_index() == 0, total[0:8], total[8:16])
    scr[8:24, :] = total[16:32]
    out_ref[...] = jnp.broadcast_to(scr[...].astype(BF16)[None], out_ref.shape)


def finish_kernel(
    factor, recv_ref, other_ref,
    gs_out, ps_out, bs_out, os_out, ge_out, pe_out, be_out, oe_out, gt_out, up_out, down_out,
    gs_ref, ps_ref, bs_ref, os_ref, ge_ref, pe_ref, be_ref, oe_ref, gt_ref, up_ref, down_ref,
    fscr, block, sems,
):
    copies = []

    def leave(ref, out):
        copies.append(pltpu.make_async_copy(ref, out, sems.at[len(copies)]))
        copies[-1].start()

    n_dst, half, _ = recv_ref.shape
    size = n_dst * half
    core = core_index()
    for index, ref in ((core, recv_ref), (1 - core, other_ref)):
        fscr[pl.ds(pl.multiple_of(index * size, 8), size), :] = ref[...].astype(F32).reshape(size, C) * factor

    def rows(row):
        return rows_of(fscr, row, n_dst, half)

    def wide(ref, starts):
        for t in range(4):
            for i in range(2):
                block[pl.ds(i, n_dst, stride=2), :] = rows(starts[i] + t)
            ref[:, t * C : (t + 1) * C] = block[...]

    def narrow(ref, starts):
        for i, start in enumerate(starts):
            ref[pl.ds(i, n_dst, stride=len(starts)), :] = rows(start)

    def one(e, row):
        start = e * half + row
        return fscr[start : start + 1, :]

    wide(ps_ref, (0, 4))
    leave(ps_ref, ps_out)
    wide(pe_ref, (8, 12))
    leave(pe_ref, pe_out)
    wide(up_ref, (16, size + 8))
    leave(up_ref, up_out)
    narrow(down_ref, range(size + 12, size + 20))
    leave(down_ref, down_out)
    narrow(os_ref, (size, size + 1))
    leave(os_ref, os_out)
    narrow(oe_ref, (20, size + 20))
    leave(oe_ref, oe_out)
    for h in range(HEADS):
        bs_ref[h : h + 1, :] = jnp.sum(rows(size + 3 + h), 0, keepdims=True)
        be_ref[h : h + 1, :] = one(3 + h, size + 2)
    gt_ref[...] = one(0, size + 2)
    ge_ref[...] = one(1, size + 2) + one(2, size + 2)
    gs_ref[...] = jnp.sum(rows(size + 7), 0, keepdims=True)
    for ref, out in ((bs_ref, bs_out), (be_ref, be_out), (gt_ref, gt_out), (ge_ref, ge_out), (gs_ref, gs_out)):
        leave(ref, out)
    for copy in copies:
        copy.wait()


def shape(dims, dtype=F32):
    return jax.ShapeDtypeStruct(dims, dtype)


def call(body, out_shape, scratch, *operands, in_hbm=(), out=pltpu.VMEM):
    many = isinstance(out_shape, (list, tuple))
    whole = pl.BlockSpec(memory_space=out)
    spaces = [pltpu.HBM if i in in_hbm else pltpu.VMEM for i in range(len(operands))]
    operands = [pltpu.with_memory_space_constraint(a, m) if m is pltpu.HBM else a for a, m in zip(operands, spaces)]
    return pl.pallas_call(
        body,
        out_shape=out_shape,
        in_specs=[pl.BlockSpec(memory_space=m) for m in spaces],
        out_specs=[whole] * len(out_shape) if many else whole,
        scratch_shapes=[pltpu.VMEM(s, F32) if isinstance(s, tuple) else s for s in scratch],
        compiler_params=pltpu.CompilerParams(vmem_limit_bytes=VMEM_LIMIT),
    )(*operands)


def swap(buffer):
    return lax.all_to_all(buffer, "dap", split_axis=0, concat_axis=0, tiled=True)


def local(
    pair_input, cotangent, residue_mask, gain_start, proj_start, bias_start, output_start,
    gain_end, proj_end, bias_end, output_end, gain_transition, transition_up, transition_down,
):
    _, _, N, _ = pair_input.shape
    n_dst = N // 2
    x = pair_input.reshape(2 * N, C)
    cot = cotangent.reshape(2 * N, C)
    g_s, g_e, g_t = (g.reshape(1, C) for g in (gain_start, gain_end, gain_transition))
    wt_s, wt_e = bias_start.T, bias_end.T
    tokens = (2 * N, C)
    wide = (C, 4 * C)

    send, args, parts, x_in, qkv, gating, score, n, cot, wo = call(
        plane_local_kernel,
        [shape((n_dst, 8, C), BF16), shape((8, C)), shape((32, C), BF16), shape(tokens, BF16), shape((2 * N, 3 * C), BF16),
         shape(tokens), shape((2 * N, HEADS * N)), shape(tokens, BF16), shape(tokens, BF16), shape((C, C))],
        [(1, C), (HEADS, C), (1, C), (HEADS, C), (1, C), pltpu.VMEM((1, C), jnp.int32), wide,
         (8, C), (16, C), pltpu.SemaphoreType.DMA((10,))],
        x, g_s, wt_s, g_e, wt_e, g_t, residue_mask, proj_start, cot, output_start,
        in_hbm=range(10),
    )
    recv = swap(send)
    send, mix, prob, first = call(
        start_forward_kernel,
        [shape((n_dst, 16, C), BF16), shape(tokens), shape((2 * N, HEADS * N)), shape(tokens, BF16)],
        [(n_dst * 8, C), (HEADS * N, N), (n_dst * 16, C), (8, C)],
        recv, x_in, cot, args, parts, qkv, gating, score, wo,
    )
    recv = swap(send)
    n_dp = lax.axis_size("dp")
    to_core = [(i, i ^ 1) for i in range(n_dp)]
    half = (n_dst * HALF, C)
    hidden = (2 * N, 4 * C)
    send, small, *saved = call(
        end_kernel,
        [shape((n_dst, 3, 4, C), BF16), shape((8, C)), shape(hidden, BF16), shape(hidden, BF16), shape(tokens, BF16),
         shape(tokens, BF16), shape(tokens, BF16), shape(hidden, BF16), shape(tokens, BF16), shape(tokens, BF16)],
        [(n_dst * 16, C), tokens, tokens, (HEADS * N, N), (n_dst * 24, C)],
        recv, args, proj_end, output_end, transition_up, transition_down,
    )
    recv = swap(send)
    keep, give = call(
        end_weights_kernel,
        [shape(half), shape(half, BF16)],
        [(4 * C, C), (4 * C, C), (4 * C, C), (C, C), (n_dst * 2 * HALF, C)],
        *saved,
    )
    got = lax.ppermute(give, "dp", to_core)
    send, dfirst, dproj = call(
        start_backward_kernel,
        [shape((n_dst, 32, C), BF16), shape(tokens, BF16), shape(hidden, BF16)],
        [(n_dst, 8, C), tokens, (HEADS * N, N), (C, C), (4 * C, C), (n_dst * 32, C), half, (2, 16, C)],
        recv, keep, got, small, n, first, qkv, gating, mix, prob, args, parts, wo,
    )
    recv = swap(send)
    dn, dn_plane, part, half_part = call(
        start_plane_kernel,
        [shape(tokens, BF16), shape(tokens, BF16), shape((16, C)), shape((16, C))],
        [(2, 16, C)],
        recv, dproj, x, proj_start, args, parts,
    )
    part = call(core_sum_kernel, shape((32, C)), [], part, lax.ppermute(part, "dp", to_core), half_part)
    far = lax.ppermute(part, "dp", [(i, i ^ 2) for i in range(n_dp)])
    grad = call(grad_kernel, shape(tokens, BF16), [], dn, dn_plane, dfirst, x, args)
    grad, far = lax.optimization_barrier((grad, far))
    send = call(spread_kernel, shape((n_dst, 24, C), BF16), [(24, C)], part, far)
    recv = swap(send)
    other = lax.ppermute(recv, "dp", to_core)
    factor = 1.0 / (n_dp * N)
    vector, bias, square, tall = (1, C), (HEADS, C), (C, C), (4 * C, C)
    sizes = [vector, wide, bias, square, vector, wide, bias, square, vector, wide, tall]
    gs, ps, bs, os, ge, pe, be, oe, gt, up, down = call(
        functools.partial(finish_kernel, factor),
        [shape(size) for size in sizes],
        [*sizes, (n_dst * 48, C), square, pltpu.SemaphoreType.DMA((len(sizes),))],
        recv, other,
        out=pltpu.HBM,
    )
    return (
        grad.reshape(1, 2, N, C), gs.reshape(C), ps, bs.T, os, ge.reshape(C), pe, be.T, oe, gt.reshape(C), up, down,
    )


def solution(mesh):
    rows = P("dp", "dap", None, None)
    in_specs = (rows, rows, P("dp", None)) + (P(),) * 11
    out_specs = (rows,) + (P(),) * 11
    return jax.shard_map(local, mesh=mesh, in_specs=in_specs, out_specs=out_specs, check_vma=False)
```
